32 devices in a mesh: dp: 32 (over z, y, x, core).
Axes of the slice: x: 2, y: 2, z: 4, core: 2. Of those that a mesh axis runs over, the one named last changes fastest.
Arguments:
- question_tokens: bfloat16 [256, 64, 512], P('dp'), may hold values from -6 to 6
- passage_tokens: bfloat16 [160, 256, 512], P('dp'), may hold values from -6 to 6
- question_lengths: int32 [256], P('dp'), may hold values from 8 to 64, as said below
- passage_lengths: int32 [160], P('dp'), may hold values from 40 to 256, as said below
- positives: int32 [256], P('dp'), may hold values from 0 to 159
- question_in_proj: bfloat16 [512, 1536], replicated, may hold values from -0.25 to 0.25
- question_in_bias: float32 [2, 512], replicated, may hold values from -1.8 to 1.8
- question_out_proj: bfloat16 [512, 512], replicated, may hold values from -0.5 to 0.5
- question_out_bias: float32 [2, 512], replicated, may hold values from -1.8 to 1.8
- question_gains: float32 [2, 512], replicated, may hold values from 0.5 to 1.5
- question_shifts: float32 [2, 512], replicated, may hold values from -1.8 to 1.8
- question_up_proj: bfloat16 [512, 2048], replicated, may hold values from -0.25 to 0.25
- question_up_bias: float32 [2048], replicated, may hold values from -1.8 to 1.8
- question_down_proj: bfloat16 [2048, 512], replicated, may hold values from -0.125 to 0.125
- passage_in_proj: bfloat16 [512, 1536], replicated, may hold values from -0.25 to 0.25
- passage_in_bias: float32 [2, 512], replicated, may hold values from -1.8 to 1.8
- passage_out_proj: bfloat16 [512, 512], replicated, may hold values from -0.5 to 0.5
- passage_out_bias: float32 [2, 512], replicated, may hold values from -1.8 to 1.8
- passage_gains: float32 [2, 512], replicated, may hold values from 0.5 to 1.5
- passage_shifts: float32 [2, 512], replicated, may hold values from -1.8 to 1.8
- passage_up_proj: bfloat16 [512, 2048], replicated, may hold values from -0.25 to 0.25
- passage_up_bias: float32 [2048], replicated, may hold values from -1.8 to 1.8
- passage_down_proj: bfloat16 [2048, 512], replicated, may hold values from -0.125 to 0.125
Outputs:
- loss: float32 [], replicated
- question_out: bfloat16 [256, 64, 512], P('dp')
- passage_out: bfloat16 [160, 256, 512], P('dp')
- question_grad: bfloat16 [256, 64, 512], P('dp')
- passage_grad: bfloat16 [160, 256, 512], P('dp')
- grad_question_in_proj: float32 [512, 1536], replicated
- grad_question_in_bias: float32 [2, 512], replicated
- grad_question_out_proj: float32 [512, 512], replicated
- grad_question_out_bias: float32 [2, 512], replicated
- grad_question_gains: float32 [2, 512], replicated
- grad_question_shifts: float32 [2, 512], replicated
- grad_question_up_proj: float32 [512, 2048], replicated
- grad_question_up_bias: float32 [2048], replicated
- grad_question_down_proj: float32 [2048, 512], replicated
- grad_passage_in_proj: float32 [512, 1536], replicated
- grad_passage_in_bias: float32 [2, 512], replicated
- grad_passage_out_proj: float32 [512, 512], replicated
- grad_passage_out_bias: float32 [2, 512], replicated
- grad_passage_gains: float32 [2, 512], replicated
- grad_passage_shifts: float32 [2, 512], replicated
- grad_passage_up_proj: float32 [512, 2048], replicated
- grad_passage_up_bias: float32 [2048], replicated
- grad_passage_down_proj: float32 [2048, 512], replicated
The draws below stay inside these ranges and needn't reach their ends.
Inputs may be any that keep to these rules, and one draw needn't show every extreme that they name: `question_lengths`: real tokens of each question; the positions from it on are padding. `passage_lengths`: real tokens of each passage; the positions from it on are padding.
All inputs are finite; a program needn't handle non-finite values.
Results may differ from the reference program's by a relative error of at most 0.019.
The reference program's roundings to bfloat16 on the way count: a program that leaves them out, or rounds other values in their place, can miss the bound.
Values may be sent and summed in bfloat16 or wider, within the bound.
No kernel may reach another device: no remote copies, remote signals or barrier semaphores. Data moves between devices by JAX's collectives and lax.ppermute only.
A program may use at most 192 MiB of HBM per device.

```python
import jax
import jax.numpy as jnp
from jax import lax

EMBED_BREADTH = 512
HD = 64
FF = 2048
QB = 8
PB = 5
LQ = 64
LP = 256
QMIN = 8
PMIN = 40
QTOT = 256
PTOT = 160


def ragged_lengths(key, total_rows, least, most):
    key_values, key_long, key_short = jax.random.split(key, 3)
    drawn = jax.random.randint(key_values, (total_rows,), least, most + 1)
    longest = jax.random.randint(key_long, (), 0, total_rows)
    shortest = (longest + 1 + jax.random.randint(key_short, (), 0, total_rows - 1)) % total_rows
    return drawn.at[longest].set(most).at[shortest].set(least).astype(jnp.int32)


def draw_question_lengths(key, part):
    key = jax.random.fold_in(key, 11)
    return ragged_lengths(key, QTOT, QMIN, LQ)


def draw_passage_lengths(key, part):
    key = jax.random.fold_in(key, 23)
    return ragged_lengths(key, PTOT, PMIN, LP)


def place_ends(array, stream_key, low, high):
    index_at = [jax.random.randint(jax.random.fold_in(stream_key, axis), (), 0, length) for axis, length in enumerate(array.shape)]
    widest = array.shape.index(max(array.shape))
    beside = index_at[:widest] + [(index_at[widest] + 1) % array.shape[widest]] + index_at[widest + 1:]
    return array.at[tuple(index_at)].set(low).at[tuple(beside)].set(high)


def shard_levels(rng, dims, shards, low, top_value):
    loudness = 1.0
    for dim, blocks in shards:
        steps = jax.random.uniform(jax.random.fold_in(jax.random.fold_in(rng, 6), dim), (blocks,), jnp.float32, low / len(shards), top_value / len(shards))
        loudness = loudness * jnp.repeat(jnp.exp(steps), dims[dim] // blocks).reshape((-1,) + (1,) * (len(dims) - 1 - dim))
    return loudness


def gaussian(rng, extent, width, limit, shards=(), kind=jnp.bfloat16):
    factor_of = shard_levels(rng, extent, shards, -0.22, 0.18) if shards else 1.0
    array = jax.random.normal(rng, extent, jnp.float32) * width * factor_of
    return jnp.minimum(jnp.maximum(array, -limit), limit).astype(kind)


def setup_inputs(seed: int = 0) -> dict:
    arg_keys = jax.random.split(jax.random.key(seed), 24)
    return {
        "question_tokens": gaussian(arg_keys[0], (QTOT, LQ, EMBED_BREADTH), 1.0, 6.0, ((0, 32),)),
        "passage_tokens": gaussian(arg_keys[1], (PTOT, LP, EMBED_BREADTH), 1.0, 6.0, ((0, 32),)),
        "question_lengths": draw_question_lengths(jax.random.fold_in(arg_keys[23], 71), 0),
        "passage_lengths": draw_passage_lengths(jax.random.fold_in(arg_keys[23], 71), 0),
        "positives": place_ends(jax.random.randint(arg_keys[4], (QTOT,), 0, PTOT), jax.random.fold_in(arg_keys[4], 1), 0, PTOT - 1).astype(jnp.int32),
        "question_in_proj": gaussian(arg_keys[5], (EMBED_BREADTH, 3 * EMBED_BREADTH), EMBED_BREADTH ** -0.5, 0.25),
        "question_in_bias": gaussian(arg_keys[6], (2, EMBED_BREADTH), 0.3, 1.8, (), jnp.float32),
        "question_out_proj": gaussian(arg_keys[7], (EMBED_BREADTH, EMBED_BREADTH), (EMBED_BREADTH // 4) ** -0.5, 0.5),
        "question_out_bias": gaussian(arg_keys[8], (2, EMBED_BREADTH), 0.3, 1.8, (), jnp.float32),
        "question_gains": jnp.clip(1.0 + 0.1 * jax.random.normal(arg_keys[9], (2, EMBED_BREADTH), jnp.float32), 0.5, 1.5),
        "question_shifts": gaussian(arg_keys[10], (2, EMBED_BREADTH), 0.3, 1.8, (), jnp.float32),
        "question_up_proj": gaussian(arg_keys[11], (EMBED_BREADTH, FF), EMBED_BREADTH ** -0.5, 0.25),
        "question_up_bias": gaussian(arg_keys[12], (FF,), 0.3, 1.8, (), jnp.float32),
        "question_down_proj": gaussian(arg_keys[13], (FF, EMBED_BREADTH), FF ** -0.5, 0.125),
        "passage_in_proj": gaussian(arg_keys[14], (EMBED_BREADTH, 3 * EMBED_BREADTH), EMBED_BREADTH ** -0.5, 0.25),
        "passage_in_bias": gaussian(arg_keys[15], (2, EMBED_BREADTH), 0.3, 1.8, (), jnp.float32),
        "passage_out_proj": gaussian(arg_keys[16], (EMBED_BREADTH, EMBED_BREADTH), (EMBED_BREADTH // 4) ** -0.5, 0.5),
        "passage_out_bias": gaussian(arg_keys[17], (2, EMBED_BREADTH), 0.3, 1.8, (), jnp.float32),
        "passage_gains": jnp.clip(1.0 + 0.1 * jax.random.normal(arg_keys[18], (2, EMBED_BREADTH), jnp.float32), 0.5, 1.5),
        "passage_shifts": gaussian(arg_keys[19], (2, EMBED_BREADTH), 0.3, 1.8, (), jnp.float32),
        "passage_up_proj": gaussian(arg_keys[20], (EMBED_BREADTH, FF), EMBED_BREADTH ** -0.5, 0.25),
        "passage_up_bias": gaussian(arg_keys[21], (FF,), 0.3, 1.8, (), jnp.float32),
        "passage_down_proj": gaussian(arg_keys[22], (FF, EMBED_BREADTH), FF ** -0.5, 0.125),
    }


logit_sharpness_divisor = 20.0
big_neg = -1e+30
norm_eps = 1e-06
finest_accuracy = lax.Precision.HIGHEST

@jax.custom_vjp
def low(v):
    return lax.optimization_barrier(v.astype(jnp.bfloat16)).astype(jnp.float32)

@jax.custom_vjp
def low_back(v):
    return v

def low_keep(v):
    return (low(v), None)

def low_pass(kept, grad):
    return (grad,)

def back_keep(v):
    return (v, None)

def back_low(kept, grad):
    return (low(grad),)
low.defvjp(low_keep, low_pass)
low_back.defvjp(back_keep, back_low)

def norm_rows(tensor, gain_row, shift_row):
    center = tensor - lax.optimization_barrier(jnp.mean(tensor, -1, keepdims=True))
    spread = lax.optimization_barrier(jnp.mean(center * center, -1, keepdims=True))
    return center * lax.rsqrt(spread + norm_eps) * gain_row + shift_row

def layer_pool(tokens, lengths, params):
    in_proj, in_bias, out_proj, out_bias, gains, shifts, up_proj, up_bias, down_proj = params
    examples, seq_width, model_width = tokens.shape
    head_count = model_width // HD
    token_rows = tokens.reshape(examples * seq_width, model_width)
    mixed_rows = jnp.dot(token_rows, in_proj, precision=finest_accuracy)
    query_rows = low(low_back(mixed_rows[:, :model_width] + in_bias[0]))
    key_rows = low(low_back(mixed_rows[:, model_width:2 * model_width]))
    value_rows = low(low_back(mixed_rows[:, 2 * model_width:] + in_bias[1]))
    head_shape = (examples, seq_width, head_count, HD)
    raw_scores = jnp.einsum('bqhe,bkhe->bhqk', query_rows.reshape(head_shape), key_rows.reshape(head_shape), precision=finest_accuracy) * HD ** (-0.5)
    key_valid = jnp.arange(seq_width)[None, :] < lengths[:, None]
    scores = low_back(jnp.where(key_valid[:, None, None, :], raw_scores, big_neg))
    attn_probs = low(jax.nn.softmax(scores, axis=-1))
    context = jnp.einsum('bhqk,bkhe->bqhe', attn_probs, value_rows.reshape(head_shape), precision=finest_accuracy)
    context = low(low_back(context.reshape(examples * seq_width, model_width)))
    attn_out = low_back(jnp.dot(context, out_proj, precision=finest_accuracy) + out_bias[0])
    middle_full = norm_rows(token_rows + attn_out, gains[0], shifts[0])
    middle = low(middle_full)
    hidden_pre = low_back(jnp.dot(middle, up_proj, precision=finest_accuracy) + up_bias)
    hidden_act = low(jax.nn.gelu(hidden_pre, approximate=False))
    ffn_out = low_back(jnp.dot(hidden_act, down_proj, precision=finest_accuracy) + out_bias[1])
    layer_out = norm_rows(middle_full + ffn_out, gains[1], shifts[1]).reshape(examples, seq_width, model_width)
    valid_float = key_valid.astype(layer_out.dtype)
    summed = lax.optimization_barrier(jnp.sum(layer_out * valid_float[:, :, None], 1)) / lengths[:, None].astype(layer_out.dtype)
    unit_rows = summed * lax.rsqrt(lax.optimization_barrier(jnp.mean(summed * summed, -1, keepdims=True)) + norm_eps)
    return (layer_out, low(unit_rows))

def encode(tokens, lengths, params, per_group):
    groups = tokens.shape[0] // per_group
    layer_step = jax.checkpoint(layer_pool)
    grouped = tokens.reshape((groups, per_group) + tokens.shape[1:])
    grouped_lengths = lengths.reshape(groups, per_group)
    group_outs, group_units = lax.map(lambda group_pair: layer_step(group_pair[0], group_pair[1], params), (grouped, grouped_lengths))
    return (group_outs.reshape(tokens.shape), group_units.reshape(tokens.shape[0], tokens.shape[2]))

def reference(question_tokens, passage_tokens, question_lengths, passage_lengths, positives, question_in_proj, question_in_bias, question_out_proj, question_out_bias, question_gains, question_shifts, question_up_proj, question_up_bias, question_down_proj, passage_in_proj, passage_in_bias, passage_out_proj, passage_out_bias, passage_gains, passage_shifts, passage_up_proj, passage_up_bias, passage_down_proj):
    question_params = jax.tree.map(lambda tensor: tensor.astype(jnp.float32), (question_in_proj, question_in_bias, question_out_proj, question_out_bias, question_gains, question_shifts, question_up_proj, question_up_bias, question_down_proj))
    passage_params = jax.tree.map(lambda tensor: tensor.astype(jnp.float32), (passage_in_proj, passage_in_bias, passage_out_proj, passage_out_bias, passage_gains, passage_shifts, passage_up_proj, passage_up_bias, passage_down_proj))

    def forward_all(question_float, passage_float, question_weights, passage_weights):
        question_out, inquiry_unitlength = encode(question_float, question_lengths, question_weights, QB)
        passage_out, document_unitlength = encode(passage_float, passage_lengths, passage_weights, PB)
        similarity_logits = low_back(jnp.dot(inquiry_unitlength, document_unitlength.T, precision=finest_accuracy) * (logit_sharpness_divisor / EMBED_BREADTH))
        logsum = jax.nn.logsumexp(similarity_logits, axis=1)
        chosen = jnp.take_along_axis(similarity_logits, positives[:, None], 1)[:, 0]
        loss = jnp.sum(logsum - chosen)
        return (loss, (question_out, passage_out))
    loss, back_fn, outputs = jax.vjp(forward_all, question_tokens.astype(jnp.float32), passage_tokens.astype(jnp.float32), question_params, passage_params, has_aux=True)
    question_grad, passage_grad, question_wgrad, passage_wgrad = back_fn(jnp.ones_like(loss))
    return (loss, outputs[0].astype(jnp.bfloat16), outputs[1].astype(jnp.bfloat16), question_grad.astype(jnp.bfloat16), passage_grad.astype(jnp.bfloat16), question_wgrad[0], question_wgrad[1], question_wgrad[2], question_wgrad[3], question_wgrad[4], question_wgrad[5], question_wgrad[6], question_wgrad[7], question_wgrad[8], passage_wgrad[0], passage_wgrad[1], passage_wgrad[2], passage_wgrad[3], passage_wgrad[4], passage_wgrad[5], passage_wgrad[6], passage_wgrad[7], passage_wgrad[8])
```

```python
import math
from functools import partial

import jax
import jax.numpy as jnp
from jax import lax
from jax.experimental import pallas as pl
from jax.experimental.pallas import tpu as pltpu
from jax.sharding import PartitionSpec as P

HEAD = 64
ROWS = 256
SHARPNESS = 20.0
NEG = -1e30
EPS = 1e-06
F32 = jnp.float32
BF16 = jnp.bfloat16
VMEM_BYTES = 48 * 1024 * 1024
FORWARD_VMEM_BYTES = 60 * 1024 * 1024

DENSITY = 1.0 / math.sqrt(2.0 * math.pi)


def nn(a, b):
    return lax.dot_general(a, b, (((1,), (0,)), ((), ())), preferred_element_type=F32)


def nt(a, b):
    return lax.dot_general(a, b, (((1,), (1,)), ((), ())), preferred_element_type=F32)


def tn(a, b):
    return lax.dot_general(a, b, (((0,), (0,)), ((), ())), preferred_element_type=F32)


def gelu_pair(v):
    cdf = 0.5 + 0.5 * lax.erf(v * math.sqrt(0.5))
    bell = jnp.exp(v * v * -0.5)
    return v * cdf, cdf + v * (bell * DENSITY)


def layer_norm(v):
    center = v - jnp.mean(v, -1, keepdims=True)
    scale = lax.rsqrt(jnp.mean(center * center, -1, keepdims=True) + EPS)
    return center * scale, scale


def norm_back(grad, unit, scale, gain):
    t = grad * gain
    return scale * (
        t - jnp.mean(t, -1, keepdims=True) - unit * jnp.mean(t * unit, -1, keepdims=True)
    )


def fold_rows(v):
    return jnp.sum(v, 0, keepdims=True)


def cost(micros):
    return pl.CostEstimate(flops=int(micros * 1.15e9), bytes_accessed=0, transcendentals=0)


def full(array):
    zeros = (0,) * array.ndim
    return pl.BlockSpec(array.shape, lambda *_: zeros, pipeline_mode=pl.Buffered(1))


FAR = pl.BlockSpec(memory_space=pltpu.HBM)


def room(*arrays):
    return [*[pltpu.VMEM(a.shape, a.dtype) for a in arrays], pltpu.SemaphoreType.DMA((len(arrays),))]


def fetch(*pairs, arrived):
    copies = [pltpu.make_async_copy(far, near, arrived.at[i]) for i, (far, near) in enumerate(pairs)]

    @pl.when(pl.program_id(0) == 0)
    def _():
        for copy in copies:
            copy.start()

    return copies


def ready(copy):
    @pl.when(pl.program_id(0) == 0)
    def _():
        copy.wait()


def rows(width, length=ROWS):
    return pl.BlockSpec((length, width), lambda i, *_: (i, 0))


def forward_kernel(
    seq,
    lens,
    x_ref,
    in_bias,
    out_bias,
    gains,
    shifts,
    up_bias,
    in_proj_far,
    out_proj_far,
    up_far,
    down_far,
    out_ref,
    summed_ref,
    qkv_ref,
    probs_ref,
    context_ref,
    unit1_ref,
    unit2_ref,
    scale_ref,
    middle_ref,
    act_ref,
    slope_ref,
    in_proj,
    out_proj,
    up,
    down,
    arrived,
):
    block = pl.program_id(0)
    groups = ROWS // seq
    width = x_ref.shape[1]
    weights = fetch(
        (in_proj_far, in_proj), (out_proj_far, out_proj), (up_far, up), (down_far, down), arrived=arrived
    )
    row = lax.broadcasted_iota(jnp.int32, (ROWS, 128), 0)
    lane = lax.broadcasted_iota(jnp.int32, (ROWS, 128), 1)
    slot = lane % HEAD
    low_half = lane < HEAD
    group = row // seq
    limit = jnp.zeros((ROWS, 128), jnp.int32)
    for g in range(groups):
        limit = jnp.where(group == g, lens[block * groups + g], limit)
    live = (row - group * seq) < limit
    query_mark = jnp.where(slot == group, 1.0, 0.0).astype(BF16)
    key_mark = jnp.where(
        slot < groups, jnp.where(jnp.logical_and(slot == group, live), 0.0, NEG), 0.0
    ).astype(BF16)
    x = x_ref[...]
    ready(weights[0])
    mixed = nn(x, in_proj[...])
    query = ((mixed[:, :width] + in_bias[0:1]).astype(BF16) * (HEAD**-0.5)).astype(BF16)
    key = mixed[:, width : 2 * width].astype(BF16)
    value = (mixed[:, 2 * width :] + in_bias[1:2]).astype(BF16)
    qkv_ref[:, :width] = query
    qkv_ref[:, width : 2 * width] = key
    qkv_ref[:, 2 * width :] = value
    pairs = []
    for p in range(width // 128):
        cols = slice(128 * p, 128 * p + 128)
        total = None
        for h in range(2):
            mine = low_half if h == 0 else jnp.logical_not(low_half)
            query_h = jnp.where(mine, query[:, cols], query_mark)
            key_h = jnp.where(mine, key[:, cols], key_mark)
            value_h = jnp.where(mine, value[:, cols], jnp.zeros_like(key_mark))
            scores = nt(key_h, query_h)
            top = jnp.max(scores, 0, keepdims=True)
            weight = jnp.exp(scores - top)
            probs = (weight * (1.0 / jnp.sum(weight, 0, keepdims=True))).astype(BF16)
            probs_ref[0, 2 * p + h] = probs
            part = tn(probs, value_h)
            total = part if total is None else total + part
        pairs.append(total.astype(BF16))
    context = jnp.concatenate(pairs, 1)
    context_ref[...] = context
    ready(weights[1])
    first = x.astype(F32) + nn(context, out_proj[...]) + out_bias[0:1]
    unit1, scale1 = layer_norm(first)
    unit1_ref[...] = unit1
    middle_full = unit1 * gains[0:1] + shifts[0:1]
    middle = middle_full.astype(BF16)
    middle_ref[...] = middle
    second = middle_full + out_bias[1:2]
    ready(weights[2])
    ready(weights[3])
    chunk = 256
    for c in range(up.shape[1] // chunk):
        cols = slice(chunk * c, chunk * c + chunk)
        pre = nn(middle, up[:, cols]) + up_bias[:, cols]
        act, slope = gelu_pair(pre)
        act = act.astype(BF16)
        act_ref[:, cols] = act
        slope_ref[:, cols] = slope.astype(BF16)
        second += nn(act, down[cols, :])
    unit2, scale2 = layer_norm(second)
    unit2_ref[...] = unit2
    scale_ref[...] = jnp.where(lane == 0, scale1, scale2)
    out = unit2 * gains[1:2] + shifts[1:2]
    out_ref[...] = out.astype(BF16)
    kept = jnp.where(live[:, :1], out, 0.0)
    for g in range(groups):
        length = lens[block * groups + g].astype(F32)
        summed_ref[0, g : g + 1] = fold_rows(kept[g * seq : (g + 1) * seq]) / length


def forward(x, lens, params):
    in_proj, in_bias, out_proj, out_bias, gains, shifts, up, up_bias, down = params
    examples, seq, width = x.shape
    tokens = examples * seq
    blocks, groups, heads = tokens // ROWS, ROWS // seq, width // HEAD
    inner = up.shape[1]
    near = (in_bias, out_bias, gains, shifts, up_bias[None])
    far = (in_proj, out_proj, up, down)
    sds = jax.ShapeDtypeStruct
    outs = pl.pallas_call(
        partial(forward_kernel, seq),
        grid_spec=pltpu.PrefetchScalarGridSpec(
            num_scalar_prefetch=1,
            grid=(blocks,),
            in_specs=[rows(width), *[full(w) for w in near], *[FAR] * len(far)],
            out_specs=[
                rows(width),
                pl.BlockSpec((1, groups, width), lambda i, *_: (i, 0, 0)),
                rows(3 * width),
                pl.BlockSpec((1, heads, ROWS, ROWS), lambda i, *_: (i, 0, 0, 0)),
                rows(width),
                rows(width),
                rows(width),
                rows(128),
                rows(width),
                rows(inner),
                rows(inner),
            ],
            scratch_shapes=room(*far),
        ),
        out_shape=[
            sds((tokens, width), BF16),
            sds((blocks, groups, width), F32),
            sds((tokens, 3 * width), BF16),
            sds((blocks, heads, ROWS, ROWS), BF16),
            sds((tokens, width), BF16),
            sds((tokens, width), F32),
            sds((tokens, width), F32),
            sds((tokens, 128), F32),
            sds((tokens, width), BF16),
            sds((tokens, inner), BF16),
            sds((tokens, inner), BF16),
        ],
        compiler_params=pltpu.CompilerParams(vmem_limit_bytes=FORWARD_VMEM_BYTES),
        cost_estimate=cost(tokens / 36),
        name="layer_forward",
    )(lens, x.reshape(tokens, width), *near, *far)
    return outs


def ffn_back_kernel(
    seq,
    lens,
    grow_ref,
    unit1_ref,
    unit2_ref,
    scale_ref,
    slope_ref,
    gains,
    down_far,
    up_far,
    gffn_ref,
    gpre_ref,
    gfirst_ref,
    small_ref,
    down,
    up,
    arrived,
):
    block = pl.program_id(0)
    groups = ROWS // seq
    weights = fetch((down_far, down), (up_far, up), arrived=arrived)

    @pl.when(block == 0)
    def _():
        small_ref[...] = jnp.zeros_like(small_ref)

    width = unit1_ref.shape[1]
    row = lax.broadcasted_iota(jnp.int32, (seq, width), 0)
    grad_out = jnp.concatenate(
        [
            jnp.where(row < lens[block * groups + g], grow_ref[0, g : g + 1], 0.0)
            for g in range(groups)
        ],
        0,
    )
    unit2 = unit2_ref[...]
    small_ref[7:8] += fold_rows(grad_out)
    small_ref[5:6] += fold_rows(grad_out * unit2)
    gsecond = norm_back(grad_out, unit2, scale_ref[:, 1:2], gains[1:2])
    gffn = gsecond.astype(BF16)
    gffn_ref[...] = gffn
    small_ref[3:4] += fold_rows(gffn.astype(F32))
    gmiddle = gsecond
    ready(weights[0])
    ready(weights[1])
    chunk = 256
    for c in range(up.shape[1] // chunk):
        cols = slice(chunk * c, chunk * c + chunk)
        gpre = (nt(gffn, down[cols, :]) * slope_ref[:, cols].astype(F32)).astype(BF16)
        gpre_ref[:, cols] = gpre
        line, left = 8 + chunk * c // width, chunk * c % width
        small_ref[line : line + 1, left : left + chunk] += fold_rows(gpre.astype(F32))
        gmiddle += nt(gpre, up[:, cols])
    unit1 = unit1_ref[...]
    small_ref[6:7] += fold_rows(gmiddle)
    small_ref[4:5] += fold_rows(gmiddle * unit1)
    gfirst = norm_back(gmiddle, unit1, scale_ref[:, 0:1], gains[0:1])
    gfirst_ref[...] = gfirst
    small_ref[2:3] += fold_rows(gfirst.astype(BF16).astype(F32))


def ffn_back(lens, grow, kept, params, seq):
    unit1, unit2, scale, slope = kept
    _, _, _, _, gains, _, up, _, down = params
    tokens, width = unit1.shape
    blocks, groups, inner = tokens // ROWS, ROWS // seq, up.shape[1]
    sds = jax.ShapeDtypeStruct
    return pl.pallas_call(
        partial(ffn_back_kernel, seq),
        grid_spec=pltpu.PrefetchScalarGridSpec(
            num_scalar_prefetch=1,
            grid=(blocks,),
            in_specs=[
                pl.BlockSpec((1, groups, width), lambda i, *_: (i, 0, 0)),
                rows(width),
                rows(width),
                rows(128),
                rows(inner),
                full(gains),
                FAR,
                FAR,
            ],
            out_specs=[
                rows(width),
                rows(inner),
                rows(width),
                pl.BlockSpec((16, width), lambda i, *_: (0, 0)),
            ],
            scratch_shapes=room(down, up),
        ),
        out_shape=[
            sds((tokens, width), BF16),
            sds((tokens, inner), BF16),
            sds((tokens, width), F32),
            sds((16, width), F32),
        ],
        compiler_params=pltpu.CompilerParams(vmem_limit_bytes=VMEM_BYTES),
        cost_estimate=cost(tokens / 80),
        name="ffn_backward",
    )(lens, grow.reshape(blocks, groups, width), unit1, unit2, scale, slope, gains, down, up)


def attention_back_kernel(
    gfirst_ref,
    context_ref,
    qkv_ref,
    probs_ref,
    before_ref,
    out_proj_far,
    in_proj_far,
    gmixed_ref,
    gtokens_ref,
    gattn_ref,
    small_ref,
    out_proj,
    in_proj,
    arrived,
):
    weights = fetch((out_proj_far, out_proj), (in_proj_far, in_proj), arrived=arrived)

    @pl.when(pl.program_id(0) == 0)
    def _():
        small_ref[...] = before_ref[...]

    width = gfirst_ref.shape[1]
    lane = lax.broadcasted_iota(jnp.int32, (ROWS, 128), 1)
    low_half = lane < HEAD
    blank = jnp.zeros((ROWS, 128), BF16)
    gfirst = gfirst_ref[...]
    gattn = gfirst.astype(BF16)
    gattn_ref[...] = gattn
    ready(weights[0])
    gcontext = nt(gattn, out_proj[...]).astype(BF16)
    heads = width // HEAD
    member = (
        lax.broadcasted_iota(jnp.int32, (16, width), 1) // HEAD
        == lax.broadcasted_iota(jnp.int32, (16, width), 0)
    )
    member = jnp.where(member, 1.0, 0.0).astype(BF16)
    product = gcontext.astype(F32) * context_ref[...].astype(F32)
    coarse = product.astype(BF16)
    fine = (product - coarse.astype(F32)).astype(BF16)
    offsets = nt(member, coarse) + nt(member, fine)
    for p in range(width // 128):
        cols = slice(128 * p, 128 * p + 128)
        kcols = slice(width + 128 * p, width + 128 * p + 128)
        vcols = slice(2 * width + 128 * p, 2 * width + 128 * p + 128)
        query, key, value = qkv_ref[:, cols], qkv_ref[:, kcols], qkv_ref[:, vcols]
        gquery = gkey = gvalue = None
        for h in range(2):
            mine = low_half if h == 0 else jnp.logical_not(low_half)
            gcontext_h = jnp.where(mine, gcontext[:, cols], blank)
            probs = probs_ref[0, 2 * p + h]
            gprobs = nt(value, gcontext_h)
            head = 2 * p + h
            gscores = (probs.astype(F32) * (gprobs - offsets[head : head + 1])).astype(BF16)
            parts = (
                tn(gscores, jnp.where(mine, key, blank)),
                nn(gscores, jnp.where(mine, query, blank)),
                nn(probs, gcontext_h),
            )
            if h == 0:
                gquery, gkey, gvalue = parts
            else:
                gquery, gkey, gvalue = gquery + parts[0], gkey + parts[1], gvalue + parts[2]
        gquery = (gquery * (HEAD**-0.5)).astype(BF16)
        gmixed_ref[:, cols] = gquery
        gmixed_ref[:, kcols] = gkey.astype(BF16)
        gvalue = gvalue.astype(BF16)
        gmixed_ref[:, vcols] = gvalue
        small_ref[0:1, cols] += fold_rows(gquery.astype(F32))
        small_ref[1:2, cols] += fold_rows(gvalue.astype(F32))
    ready(weights[1])
    gtokens_ref[...] = (gfirst + nt(gmixed_ref[...], in_proj[...])).astype(BF16)


def attention_back(gfirst, context, qkv, probs, small, params):
    in_proj, out_proj = params[0], params[2]
    tokens, width = context.shape
    sds = jax.ShapeDtypeStruct
    return pl.pallas_call(
        attention_back_kernel,
        grid=(tokens // ROWS,),
        in_specs=[
            rows(width),
            rows(width),
            rows(3 * width),
            pl.BlockSpec((1, *probs.shape[1:]), lambda i: (i, 0, 0, 0)),
            full(small),
            FAR,
            FAR,
        ],
        out_specs=[
            rows(3 * width),
            rows(width),
            rows(width),
            pl.BlockSpec(small.shape, lambda i: (0, 0)),
        ],
        out_shape=[
            sds((tokens, 3 * width), BF16),
            sds((tokens, width), BF16),
            sds((tokens, width), BF16),
            sds(small.shape, F32),
        ],
        scratch_shapes=room(out_proj, in_proj),
        compiler_params=pltpu.CompilerParams(vmem_limit_bytes=VMEM_BYTES),
        cost_estimate=cost(tokens / 70),
        name="attention_backward",
    )(gfirst, context, qkv, probs, small, out_proj, in_proj)


def match_kernel(masks, questions, passages, blocks_ref, spot, summed_ref, lens_ref, loss_ref, grow_ref, units_ref):
    per_device, width = summed_ref.shape
    for k, mask in enumerate(masks):
        lead = pl.multiple_of((spot[0] ^ mask) * per_device, per_device)
        units_ref[pl.ds(lead, per_device), :] = blocks_ref[k]
    every = units_ref[...]
    count = every.shape[0]
    units = every[:, :width]
    scale = SHARPNESS / width
    ri = lax.broadcasted_iota(jnp.int32, (count, count), 0)
    ci = lax.broadcasted_iota(jnp.int32, (count, count), 1)
    pick = jnp.where(
        lax.broadcasted_iota(jnp.int32, (8, 128), 0) == lax.broadcasted_iota(jnp.int32, (8, 128), 1), 1.0, 0.0
    ).astype(BF16)
    digits = nt(pick, every[:, width:])
    positive = (digits[0:1] * 256.0 + digits[1:2]).astype(jnp.int32)
    place = (positive // passages) * per_device + questions + positive % passages
    rlocal = ri % per_device
    is_passage = jnp.logical_and(rlocal >= questions, rlocal < questions + passages)
    is_question = (ci[0:1] % per_device) < questions
    match = nt(units, units) * scale
    shown = jnp.where(is_passage, match, NEG)
    top = jnp.max(shown, 0, keepdims=True)
    total = jnp.sum(jnp.exp(shown - top), 0, keepdims=True)
    logsum = top + jnp.log(total)
    hit = ri == place
    chosen = jnp.sum(jnp.where(hit, match, 0.0), 0, keepdims=True)
    loss_ref[...] = jnp.sum(jnp.where(is_question, logsum - chosen, 0.0), 1, keepdims=True)

    first = spot[0] * per_device
    own = blocks_ref[0]
    own_units = own[:, :width]
    rown = lax.broadcasted_iota(jnp.int32, (per_device, count), 0)
    cown = lax.broadcasted_iota(jnp.int32, (per_device, count), 1)
    match_own = nt(own_units, units) * scale
    hit_p = jnp.logical_and(place == first + rown, is_question)
    share_p = jnp.exp(match_own - logsum) - jnp.where(hit_p, 1.0, 0.0)
    share_p = jnp.where(is_question, share_p, 0.0)
    clocal = cown % per_device
    col_passage = jnp.logical_and(clocal >= questions, clocal < questions + passages)
    shown_q = jnp.where(col_passage, match_own, NEG)
    weight_q = jnp.exp(shown_q - jnp.max(shown_q, 1, keepdims=True))
    code = own[:, width:].astype(F32)
    positive_q = (code[:, 0:1] * 256.0 + code[:, 1:2]).astype(jnp.int32)
    place_q = (positive_q // passages) * per_device + questions + positive_q % passages
    share_q = weight_q / jnp.sum(weight_q, 1, keepdims=True) - jnp.where(cown == place_q, 1.0, 0.0)
    share = jnp.where(rown < questions, share_q, share_p).astype(BF16)
    gunit = nn(share, units) * scale
    summed = summed_ref[...]
    r = lax.rsqrt(jnp.mean(summed * summed, -1, keepdims=True) + EPS)
    gsummed = r * gunit - (r * r * r) * summed * jnp.mean(gunit * summed, -1, keepdims=True)
    grow_ref[...] = gsummed / lens_ref[:, 0:1]


def match_loss(blocks, masks, spot, summed, lens, questions, passages):
    count, per_device, wide = blocks.shape
    vmem = pl.BlockSpec(memory_space=pltpu.VMEM)
    return pl.pallas_call(
        partial(match_kernel, masks, questions, passages),
        in_specs=[vmem, pl.BlockSpec(memory_space=pltpu.SMEM), vmem, vmem],
        out_specs=[vmem, vmem],
        out_shape=[
            jax.ShapeDtypeStruct((1, 1), F32),
            jax.ShapeDtypeStruct(summed.shape, F32),
        ],
        scratch_shapes=[pltpu.VMEM((count * per_device, wide), BF16)],
        compiler_params=pltpu.CompilerParams(vmem_limit_bytes=VMEM_BYTES),
        cost_estimate=cost(3),
        name="match_loss",
    )(blocks, spot, summed, lens)


ORDERS = ("xyz", "yxz")
PIECE = 512


def axis_layout(devices):
    bits = devices.bit_length() - 2
    x = bits // 3
    y = (bits - x) // 2
    return {"x": (1, x), "y": (1 + x, y), "z": (1 + x + y, bits - x - y)}


def chip_number(me, devices, order):
    layout = axis_layout(devices)
    number = jnp.zeros((), jnp.int32)
    for axis in order:
        start, count = layout[axis]
        number = (number << count) | ((me >> start) & ((1 << count) - 1))
    return number


def weight_grad_kernel(streams, spots, *refs):
    *operands, send_ref, keep_ref = refs
    _, pieces, tall, wide = send_ref.shape
    for side, out in enumerate((send_ref, keep_ref)):
        for stream, terms in enumerate(streams):
            column = 0
            columns = sum(n // wide for *_, n in terms)
            for x, g, first, n in terms:
                x_ref, g_ref = operands[x], operands[g]
                half = x_ref.shape[1] // 2
                step = min(half, 256)
                for s in range(half // step):
                    lead = pl.multiple_of((spots[0] ^ (1 - side)) * half + s * step, step)
                    tile = tn(x_ref[:, pl.ds(lead, step)], g_ref[:, first : first + n]).astype(BF16)
                    for b in range(step // tall):
                        for c in range(n // wide):
                            number = (s * (step // tall) + b) * columns + column + c
                            out[stream, number ^ spots[1 + stream]] = tile[
                                b * tall : (b + 1) * tall, c * wide : (c + 1) * wide
                            ]
                column += n // wide


def weight_grad(operands, streams, spots, devices, micros):
    pieces = devices // 2
    size = sum(operands[x].shape[1] * n for x, _, _, n in streams[0]) // devices
    tall = max(16, size // PIECE)
    vmem = pl.BlockSpec(memory_space=pltpu.VMEM)
    out = jax.ShapeDtypeStruct((len(streams), pieces, tall, size // tall), BF16)
    return pl.pallas_call(
        partial(weight_grad_kernel, streams),
        in_specs=[pl.BlockSpec(memory_space=pltpu.SMEM), *[vmem] * len(operands)],
        out_specs=[vmem, vmem],
        out_shape=[out, out],
        compiler_params=pltpu.CompilerParams(vmem_limit_bytes=VMEM_BYTES),
        cost_estimate=cost(micros),
        name="weight_gradient",
    )(spots, *operands)


PARTS = 4


def place_kernel(outputs, spots, *refs):
    inputs, outs = refs[:4], refs[4:]
    _, group, tall, wide = inputs[0].shape
    for side in range(2):

        @pl.when(pl.program_id(0) == side)
        def _(side=side):
            for out, (blocks, columns) in zip(outs, outputs):
                for k, (st, column) in enumerate(blocks):
                    inner = spots[1 + st] & (group - 1)
                    for b in range(out.shape[0] // tall):
                        piece = inputs[2 * side + st][0, (b * columns + column) ^ inner]
                        out[b * tall : (b + 1) * tall, k * wide : (k + 1) * wide] = piece.astype(F32)


def place(mine, other, spots, layout):
    _, pieces, tall, wide = mine.shape
    group = pieces // PARTS

    def piece_spec(side, stream):
        def index(s, g, spots):
            g = jnp.where(s == side, g, (1 - side) * (PARTS - 1))
            return (stream, g ^ spots[3 + stream], 0, 0)

        return pl.BlockSpec((1, group, tall, wide), index)

    outputs, out_specs, out_shape = [], [], []
    for height, places in layout:
        width = PIECE * len(places)
        fine = PIECE // wide
        blocks = tuple((st, col * fine + k) for st, col, _ in places for k in range(fine))
        outputs.append((blocks, places[0][2] * fine))
        out_specs.append(
            pl.BlockSpec((height // (2 * PARTS), width), lambda s, g, spots: ((spots[0] ^ s) * PARTS + g, 0))
        )
        out_shape.append(jax.ShapeDtypeStruct((height, width), F32))
    return pl.pallas_call(
        partial(place_kernel, outputs),
        grid_spec=pltpu.PrefetchScalarGridSpec(
            num_scalar_prefetch=1,
            grid=(2, PARTS),
            in_specs=[piece_spec(side, stream) for side in range(2) for stream in range(2)],
            out_specs=out_specs,
        ),
        out_shape=out_shape,
        compiler_params=pltpu.CompilerParams(vmem_limit_bytes=VMEM_BYTES),
        cost_estimate=cost(5),
        name="place_gradient",
    )(spots, mine, mine, other, other)


def swap(array, mask, devices):
    return lax.ppermute(array, "dp", [(i, i ^ mask) for i in range(devices)])


def add(*terms):
    total = terms[0].astype(F32)
    for t in terms[1:]:
        total = total + t.astype(F32)
    return total.astype(BF16)


def sum_pieces(send, keep, devices):
    layout = axis_layout(devices)
    (got,) = yield [(send, 1)]
    held = [[keep[i], got[i]] for i in range(len(ORDERS))]
    for level in range(2):
        parts = []
        for terms, order in zip(held, ORDERS):
            ways = 1 << layout[order[level]][1]
            size = terms[0].shape[0] // ways
            parts.append([add(*[t[m * size : (m + 1) * size] for t in terms]) for m in range(ways)])
        got = yield [
            (p, m << layout[order[level]][0])
            for stream, order in zip(parts, ORDERS)
            for m, p in enumerate(stream)
            if m
        ]
        held = []
        for stream in parts:
            held.append([stream[0], *got[: len(stream) - 1]])
            got = got[len(stream) - 1 :]
    start, count = layout["z"]
    ways = 1 << count
    size = held[0][0].shape[0] // ways
    both = [
        jnp.stack([add(*[t[m * size : (m + 1) * size] for t in terms]) for terms in held])
        for m in range(ways)
    ]
    got = yield [(b, m << start) for m, b in enumerate(both) if m]
    total = add(both[0], *got)
    got = yield [(total, m << start) for m in range(1, ways)]
    every = jnp.concatenate([total, *got], 1)
    done = [every[i] for i in range(len(ORDERS))]
    for level in (1, 0):
        sends = []
        for mine, order in zip(done, ORDERS):
            start, count = layout[order[level]]
            sends.append([(mine, m << start) for m in range(1, 1 << count)])
        got = yield [s for stream in sends for s in stream]
        grown = []
        for mine, stream in zip(done, sends):
            grown.append(jnp.concatenate([mine, *got[: len(stream)]], 0))
            got = got[len(stream) :]
        done = grown
    mine = jnp.stack(done)
    (other,) = yield [(mine, 1)]
    return mine, other


def sum_small(array, devices):
    for bit in range(devices.bit_length() - 1):
        (got,) = yield [(array, 1 << bit)]
        array = array + got
    return array


class Line:
    def __init__(self, devices):
        self.devices = devices
        self.running = {}
        self.done = {}

    def add(self, name, steps):
        self.running[name] = (steps, next(steps))

    def step(self, names, kernel=None, operand=None):
        names = [n for n in names if n in self.running]
        sends = [self.running[n][1] for n in names]
        arrays = [[a for a, _ in s] for s in sends]
        arrays, operand = lax.optimization_barrier((arrays, operand))
        got = [[swap(a, m, self.devices) for a, (_, m) in zip(x, s)] for x, s in zip(arrays, sends)]
        result = kernel(operand) if kernel else None
        got, result = lax.optimization_barrier((got, result))
        for n, g in zip(names, got):
            steps, _ = self.running.pop(n)
            try:
                self.running[n] = (steps, steps.send(g))
            except StopIteration as end:
                self.done[n] = end.value
        return result


def gather_stages(devices):
    (x, nx), (y, ny), (z, nz) = (axis_layout(devices)[a] for a in "xyz")
    plane = [(x, nx + ny)] if nx + ny < 3 else [(y, ny), (x, nx)]
    return [(z, nz), *plane, (0, 1)]


def gather_units(own, devices):
    every, masks = own[None], [0]
    for start, count in gather_stages(devices):
        steps = [m << start for m in range(1 << count)]
        every = jnp.concatenate([every] + [swap(every, m, devices) for m in steps[1:]], 0)
        masks = [k ^ m for m in steps for k in masks]
    return every, masks


def on_device(devices, *args):
    (question_tokens, passage_tokens, question_lengths, passage_lengths, positives), weights = args[:5], args[5:]
    question_params, passage_params = weights[:9], weights[9:]
    me = lax.axis_index("dp").astype(jnp.int32)
    chips = [chip_number(me, devices, order) for order in ORDERS]
    group = devices // 8
    spots = jnp.stack([me & 1, *chips, *[c // group for c in chips]])
    questions, question_seq, width = question_tokens.shape
    passages, passage_seq, _ = passage_tokens.shape

    p_fwd = forward(passage_tokens, passage_lengths, passage_params)
    q_fwd = forward(question_tokens, question_lengths, question_params)
    q_summed = q_fwd[1].reshape(questions, width)
    p_summed = p_fwd[1].reshape(passages, width)
    per_device = -(-(questions + passages) // 16) * 16
    spare = per_device - questions - passages
    summed = jnp.concatenate([q_summed, p_summed, jnp.zeros((spare, width), F32)], 0)
    units = (summed * lax.rsqrt(jnp.mean(summed * summed, -1, keepdims=True) + EPS)).astype(BF16)
    code = jnp.pad(
        jnp.stack([positives // 256, positives % 256], 1).astype(BF16),
        ((0, per_device - questions), (0, 126)),
    )
    every, masks = gather_units(jnp.concatenate([units, code], 1), devices)
    lens = jnp.concatenate([question_lengths, passage_lengths, jnp.ones((spare,), jnp.int32)])
    lens = jnp.broadcast_to(lens.astype(F32)[:, None], (per_device, 128))
    loss, grow = match_loss(every, masks, me[None], summed, lens, questions, passages)

    _, _, p_qkv, p_probs, p_context, *p_norm, p_middle, p_act, p_slope = p_fwd
    _, _, q_qkv, q_probs, q_context, *q_norm, q_middle, q_act, q_slope = q_fwd
    inner = p_act.shape[1]
    x_p, x_q = passage_tokens.reshape(-1, width), question_tokens.reshape(-1, width)

    def ffn_p(part):
        return ffn_back(passage_lengths, part, (*p_norm, p_slope), passage_params, passage_seq)

    def ffn_q(part):
        return ffn_back(question_lengths, part, (*q_norm, q_slope), question_params, question_seq)

    def ffn_grads(middle, act, gpre, gffn, micros):
        streams = [[(0, 1, 0, inner)], [(2, 3, 0, width)]]
        return weight_grad([middle, gpre, act, gffn], streams, spots, devices, micros)

    def attention_grads(x, gmixed, context, gattn, micros):
        streams = [[(0, 1, 0, 2 * width)], [(0, 1, 2 * width, width), (2, 3, 0, width)]]
        return weight_grad([x, gmixed, context, gattn], streams, spots, devices, micros)

    ffn_layout = (
        (width, [(0, c, inner // PIECE) for c in range(inner // PIECE)]),
        (inner, [(1, 0, 1)]),
    )
    attention_layout = ((width, [(0, 0, 2), (0, 1, 2), (1, 0, 2)]), (width, [(1, 1, 2)]))

    line = Line(devices)
    p_gffn, p_gpre, p_first, p_small = ffn_p(grow[questions : questions + passages])
    line.add("1", sum_pieces(*ffn_grads(p_middle, p_act, p_gpre, p_gffn, 11), devices))
    q_gffn, q_gpre, q_first, q_small = line.step("1", ffn_q, grow[:questions])
    halves = line.step("1", lambda g: ffn_grads(q_middle, q_act, g, q_gffn, 8), q_gpre)
    line.add("2", sum_pieces(*halves, devices))
    q_mixed, q_grad, q_attn, q_small = line.step(
        "12", lambda g: attention_back(g, q_context, q_qkv, q_probs, q_small, question_params), q_first
    )
    halves = line.step("12", lambda g: attention_grads(x_q, g, q_context, q_attn, 5), q_mixed)
    line.add("4", sum_pieces(*halves, devices))
    p_mixed, p_grad, p_attn, p_small = line.step(
        "124", lambda g: attention_back(g, p_context, p_qkv, p_probs, p_small, passage_params), p_first
    )
    halves = line.step("124", lambda g: attention_grads(x_p, g, p_context, p_attn, 8), p_mixed)
    line.add("3", sum_pieces(*halves, devices))
    small = jnp.stack([q_small, p_small])
    line.add("s", sum_small(small, devices))
    line.step("1234")
    line.step("1234s")
    p_up, p_down = line.step(
        "234s", lambda mine: place(mine, line.done["1"][1], spots, ffn_layout), line.done["1"][0]
    )
    line.step("234s")
    q_up, q_down = line.step(
        "34s", lambda mine: place(mine, line.done["2"][1], spots, ffn_layout), line.done["2"][0]
    )
    line.step("34s")
    q_in, q_out = line.step(
        "3", lambda mine: place(mine, line.done["4"][1], spots, attention_layout), line.done["4"][0]
    )
    while line.running:
        line.step("3s")
    p_in, p_out = place(*line.done["3"], spots, attention_layout)
    small = line.done["s"]

    def outputs(small, gin, gout, gup, gdown):
        return (
            gin,
            small[0:2],
            gout,
            small[2:4],
            small[4:6],
            small[6:8],
            gup,
            small[8 : 8 + inner // width].reshape(inner),
            gdown,
        )

    return (
        loss[0, 0],
        q_fwd[0].reshape(question_tokens.shape),
        p_fwd[0].reshape(passage_tokens.shape),
        q_grad.reshape(question_tokens.shape),
        p_grad.reshape(passage_tokens.shape),
        *outputs(small[0], q_in, q_out, q_up, q_down),
        *outputs(small[1], p_in, p_out, p_up, p_down),
    )


def solution(mesh):
    batch = P("dp", None, None)
    return jax.shard_map(
        partial(on_device, mesh.shape["dp"]),
        mesh=mesh,
        in_specs=(batch, batch, P("dp"), P("dp"), P("dp"), *[P()] * 18),
        out_specs=(P(), batch, batch, batch, batch, *[P()] * 18),
        check_vma=False,
    )
```

```python
import math
from functools import partial

import jax
import jax.numpy as jnp
from jax import lax
from jax.experimental import pallas as pl
from jax.experimental.pallas import tpu as pltpu
from jax.sharding import PartitionSpec as P

HEAD = 64
ROWS = 256
SHARPNESS = 20.0
NEG = -1e30
EPS = 1e-06
F32 = jnp.float32
BF16 = jnp.bfloat16
VMEM_BYTES = 48 * 1024 * 1024
FORWARD_VMEM_BYTES = 60 * 1024 * 1024

DENSITY = 1.0 / math.sqrt(2.0 * math.pi)


def nn(a, b):
    return lax.dot_general(a, b, (((1,), (0,)), ((), ())), preferred_element_type=F32)


def nt(a, b):
    return lax.dot_general(a, b, (((1,), (1,)), ((), ())), preferred_element_type=F32)


def tn(a, b):
    return lax.dot_general(a, b, (((0,), (0,)), ((), ())), preferred_element_type=F32)


def gelu_pair(v):
    cdf = 0.5 + 0.5 * lax.erf(v * math.sqrt(0.5))
    bell = jnp.exp(v * v * -0.5)
    return v * cdf, cdf + v * (bell * DENSITY)


def layer_norm(v):
    center = v - jnp.mean(v, -1, keepdims=True)
    scale = lax.rsqrt(jnp.mean(center * center, -1, keepdims=True) + EPS)
    return center * scale, scale


def norm_back(grad, unit, scale, gain):
    t = grad * gain
    return scale * (
        t - jnp.mean(t, -1, keepdims=True) - unit * jnp.mean(t * unit, -1, keepdims=True)
    )


def fold_rows(v):
    return jnp.sum(v, 0, keepdims=True)


def cost(micros):
    return pl.CostEstimate(flops=int(micros * 1.15e9), bytes_accessed=0, transcendentals=0)


def full(array):
    zeros = (0,) * array.ndim
    return pl.BlockSpec(array.shape, lambda *_: zeros, pipeline_mode=pl.Buffered(1))


FAR = pl.BlockSpec(memory_space=pltpu.HBM)


def room(*arrays):
    return [*[pltpu.VMEM(a.shape, a.dtype) for a in arrays], pltpu.SemaphoreType.DMA((len(arrays),))]


def fetch(*pairs, arrived):
    copies = [pltpu.make_async_copy(far, near, arrived.at[i]) for i, (far, near) in enumerate(pairs)]

    @pl.when(pl.program_id(0) == 0)
    def _():
        for copy in copies:
            copy.start()

    return copies


def ready(copy, step=0):
    @pl.when(pl.program_id(0) == step)
    def _():
        copy.wait()


def rows(width, length=ROWS):
    return pl.BlockSpec((length, width), lambda i, *_: (i, 0))


def forward_kernel(seqs, counts, *refs):
    lens, refs = refs[:2], refs[2:]
    near, far, outs, held = refs[:12], refs[12:20], refs[20:42], refs[42:50]
    copies = fetch(*zip(far, held), arrived=refs[50])
    step = pl.program_id(0)
    first = 0
    for e, (seq, count) in enumerate(zip(seqs, counts)):

        @pl.when(jnp.logical_and(step >= first, step < first + count))
        def _(e=e, seq=seq, first=first):
            forward_block(
                seq,
                step - first,
                [partial(ready, copy, first) for copy in copies[4 * e : 4 * e + 4]],
                lens[e],
                *near[6 * e : 6 * e + 6],
                *outs[11 * e : 11 * e + 11],
                *held[4 * e : 4 * e + 4],
            )

        first += count


def forward_block(
    seq,
    block,
    wait,
    lens,
    x_ref,
    in_bias,
    out_bias,
    gains,
    shifts,
    up_bias,
    out_ref,
    summed_ref,
    qkv_ref,
    probs_ref,
    context_ref,
    unit1_ref,
    unit2_ref,
    scale_ref,
    middle_ref,
    act_ref,
    slope_ref,
    in_proj,
    out_proj,
    up,
    down,
):
    groups = ROWS // seq
    width = x_ref.shape[1]
    row = lax.broadcasted_iota(jnp.int32, (ROWS, 128), 0)
    lane = lax.broadcasted_iota(jnp.int32, (ROWS, 128), 1)
    slot = lane % HEAD
    low_half = lane < HEAD
    group = row // seq
    limit = jnp.zeros((ROWS, 128), jnp.int32)
    for g in range(groups):
        limit = jnp.where(group == g, lens[block * groups + g], limit)
    live = (row - group * seq) < limit
    query_mark = jnp.where(slot == group, 1.0, 0.0).astype(BF16)
    key_mark = jnp.where(
        slot < groups, jnp.where(jnp.logical_and(slot == group, live), 0.0, NEG), 0.0
    ).astype(BF16)
    x = x_ref[...]
    wait[0]()
    mixed = nn(x, in_proj[...])
    query = ((mixed[:, :width] + in_bias[0:1]).astype(BF16) * (HEAD**-0.5)).astype(BF16)
    key = mixed[:, width : 2 * width].astype(BF16)
    value = (mixed[:, 2 * width :] + in_bias[1:2]).astype(BF16)
    qkv_ref[:, :width] = query
    qkv_ref[:, width : 2 * width] = key
    qkv_ref[:, 2 * width :] = value
    pairs = []
    for p in range(width // 128):
        cols = slice(128 * p, 128 * p + 128)
        total = None
        for h in range(2):
            mine = low_half if h == 0 else jnp.logical_not(low_half)
            query_h = jnp.where(mine, query[:, cols], query_mark)
            key_h = jnp.where(mine, key[:, cols], key_mark)
            value_h = jnp.where(mine, value[:, cols], jnp.zeros_like(key_mark))
            scores = nt(key_h, query_h)
            top = jnp.max(scores, 0, keepdims=True)
            weight = jnp.exp(scores - top)
            probs = (weight * (1.0 / jnp.sum(weight, 0, keepdims=True))).astype(BF16)
            probs_ref[0, 2 * p + h] = probs
            part = tn(probs, value_h)
            total = part if total is None else total + part
        pairs.append(total.astype(BF16))
    context = jnp.concatenate(pairs, 1)
    context_ref[...] = context
    wait[1]()
    first = x.astype(F32) + nn(context, out_proj[...]) + out_bias[0:1]
    unit1, scale1 = layer_norm(first)
    unit1_ref[...] = unit1.astype(BF16)
    middle_full = unit1 * gains[0:1] + shifts[0:1]
    middle = middle_full.astype(BF16)
    middle_ref[...] = middle
    second = middle_full + out_bias[1:2]
    wait[2]()
    wait[3]()
    chunk = 256
    for c in range(up.shape[1] // chunk):
        cols = slice(chunk * c, chunk * c + chunk)
        pre = nn(middle, up[:, cols]) + up_bias[:, cols]
        act, slope = gelu_pair(pre)
        act = act.astype(BF16)
        act_ref[:, cols] = act
        slope_ref[:, cols] = slope.astype(BF16)
        second += nn(act, down[cols, :])
    unit2, scale2 = layer_norm(second)
    unit2_ref[...] = unit2.astype(BF16)
    scale_ref[...] = jnp.where(lane == 0, scale1, scale2)
    out = unit2 * gains[1:2] + shifts[1:2]
    out_ref[...] = out.astype(BF16)
    kept = jnp.where(live[:, :1], out, 0.0)
    for g in range(groups):
        length = lens[block * groups + g].astype(F32)
        summed_ref[0, g : g + 1] = fold_rows(kept[g * seq : (g + 1) * seq]) / length


def forward(encoders):
    sds = jax.ShapeDtypeStruct
    lens, near, near_specs, far, out_specs, out_shape, seqs, counts = [], [], [], [], [], [], [], []
    first = 0
    for x, length, params in encoders:
        in_proj, in_bias, out_proj, out_bias, gains, shifts, up, up_bias, down = params
        examples, seq, width = x.shape
        tokens = examples * seq
        blocks, groups, heads = tokens // ROWS, ROWS // seq, width // HEAD
        inner = up.shape[1]

        def block(*shape, first=first, blocks=blocks):
            rest = (0,) * (len(shape) - 1)
            return pl.BlockSpec(shape, lambda i, *_: (jnp.clip(i - first, 0, blocks - 1), *rest))

        small = (in_bias, out_bias, gains, shifts, up_bias[None])
        lens.append(length)
        near += [x.reshape(tokens, width), *small]
        near_specs += [block(ROWS, width), *[full(w) for w in small]]
        far += [in_proj, out_proj, up, down]
        shapes = [
            ((tokens, width), BF16),
            ((blocks, groups, width), F32),
            ((tokens, 3 * width), BF16),
            ((blocks, heads, ROWS, ROWS), BF16),
            ((tokens, width), BF16),
            ((tokens, width), BF16),
            ((tokens, width), BF16),
            ((tokens, 128), F32),
            ((tokens, width), BF16),
            ((tokens, inner), BF16),
            ((tokens, inner), BF16),
        ]
        for shape, kind in shapes:
            out_specs.append(block(1 if shape[0] == blocks else ROWS, *shape[1:]))
            out_shape.append(sds(shape, kind))
        seqs.append(seq)
        counts.append(blocks)
        first += blocks
    outs = pl.pallas_call(
        partial(forward_kernel, seqs, counts),
        grid_spec=pltpu.PrefetchScalarGridSpec(
            num_scalar_prefetch=2,
            grid=(first,),
            in_specs=[*near_specs, *[FAR] * len(far)],
            out_specs=out_specs,
            scratch_shapes=room(*far),
        ),
        out_shape=out_shape,
        compiler_params=pltpu.CompilerParams(vmem_limit_bytes=FORWARD_VMEM_BYTES),
        cost_estimate=cost(40),
        name="layer_forward",
    )(*lens, *near, *far)
    return outs[:11], outs[11:]


def ffn_back_kernel(
    seq,
    lens,
    grow_ref,
    unit1_ref,
    unit2_ref,
    scale_ref,
    slope_ref,
    gains,
    down_far,
    up_far,
    gffn_ref,
    gpre_ref,
    gattn_ref,
    small_ref,
    down,
    up,
    arrived,
):
    block = pl.program_id(0)
    groups = ROWS // seq
    weights = fetch((down_far, down), (up_far, up), arrived=arrived)

    @pl.when(block == 0)
    def _():
        small_ref[...] = jnp.zeros_like(small_ref)

    width = unit1_ref.shape[1]
    row = lax.broadcasted_iota(jnp.int32, (seq, width), 0)
    grad_out = jnp.concatenate(
        [
            jnp.where(row < lens[block * groups + g], grow_ref[0, g : g + 1], 0.0)
            for g in range(groups)
        ],
        0,
    )
    unit2 = unit2_ref[...].astype(F32)
    small_ref[7:8] += fold_rows(grad_out)
    small_ref[5:6] += fold_rows(grad_out * unit2)
    gsecond = norm_back(grad_out, unit2, scale_ref[:, 1:2], gains[1:2])
    gffn = gsecond.astype(BF16)
    gffn_ref[...] = gffn
    small_ref[3:4] += fold_rows(gffn.astype(F32))
    gmiddle = gsecond
    ready(weights[0])
    ready(weights[1])
    chunk = 256
    for c in range(up.shape[1] // chunk):
        cols = slice(chunk * c, chunk * c + chunk)
        gpre = (nt(gffn, down[cols, :]) * slope_ref[:, cols].astype(F32)).astype(BF16)
        gpre_ref[:, cols] = gpre
        line, left = 8 + chunk * c // width, chunk * c % width
        small_ref[line : line + 1, left : left + chunk] += fold_rows(gpre.astype(F32))
        gmiddle += nt(gpre, up[:, cols])
    unit1 = unit1_ref[...].astype(F32)
    small_ref[6:7] += fold_rows(gmiddle)
    small_ref[4:5] += fold_rows(gmiddle * unit1)
    gfirst = norm_back(gmiddle, unit1, scale_ref[:, 0:1], gains[0:1])
    gattn = gfirst.astype(BF16)
    gattn_ref[...] = gattn
    small_ref[2:3] += fold_rows(gattn.astype(F32))


def ffn_back(lens, grow, kept, params, seq):
    unit1, unit2, scale, slope = kept
    _, _, _, _, gains, _, up, _, down = params
    tokens, width = unit1.shape
    blocks, groups, inner = tokens // ROWS, ROWS // seq, up.shape[1]
    sds = jax.ShapeDtypeStruct
    return pl.pallas_call(
        partial(ffn_back_kernel, seq),
        grid_spec=pltpu.PrefetchScalarGridSpec(
            num_scalar_prefetch=1,
            grid=(blocks,),
            in_specs=[
                pl.BlockSpec((1, groups, width), lambda i, *_: (i, 0, 0)),
                rows(width),
                rows(width),
                rows(128),
                rows(inner),
                full(gains),
                FAR,
                FAR,
            ],
            out_specs=[
                rows(width),
                rows(inner),
                rows(width),
                pl.BlockSpec((16, width), lambda i, *_: (0, 0)),
            ],
            scratch_shapes=room(down, up),
        ),
        out_shape=[
            sds((tokens, width), BF16),
            sds((tokens, inner), BF16),
            sds((tokens, width), BF16),
            sds((16, width), F32),
        ],
        compiler_params=pltpu.CompilerParams(vmem_limit_bytes=VMEM_BYTES),
        cost_estimate=cost(tokens / 80),
        name="ffn_backward",
    )(lens, grow.reshape(blocks, groups, width), unit1, unit2, scale, slope, gains, down, up)


def attention_back_kernel(
    gattn_ref,
    context_ref,
    qkv_ref,
    probs_ref,
    before_ref,
    out_proj_far,
    in_proj_far,
    gmixed_ref,
    gtokens_ref,
    small_ref,
    out_proj,
    in_proj,
    arrived,
):
    weights = fetch((out_proj_far, out_proj), (in_proj_far, in_proj), arrived=arrived)

    @pl.when(pl.program_id(0) == 0)
    def _():
        small_ref[...] = before_ref[...]

    width = gattn_ref.shape[1]
    lane = lax.broadcasted_iota(jnp.int32, (ROWS, 128), 1)
    low_half = lane < HEAD
    blank = jnp.zeros((ROWS, 128), BF16)
    gattn = gattn_ref[...]
    ready(weights[0])
    gcontext = nt(gattn, out_proj[...]).astype(BF16)
    heads = width // HEAD
    member = (
        lax.broadcasted_iota(jnp.int32, (16, width), 1) // HEAD
        == lax.broadcasted_iota(jnp.int32, (16, width), 0)
    )
    member = jnp.where(member, 1.0, 0.0).astype(BF16)
    product = gcontext.astype(F32) * context_ref[...].astype(F32)
    coarse = product.astype(BF16)
    fine = (product - coarse.astype(F32)).astype(BF16)
    offsets = nt(member, coarse) + nt(member, fine)
    for p in range(width // 128):
        cols = slice(128 * p, 128 * p + 128)
        kcols = slice(width + 128 * p, width + 128 * p + 128)
        vcols = slice(2 * width + 128 * p, 2 * width + 128 * p + 128)
        query, key, value = qkv_ref[:, cols], qkv_ref[:, kcols], qkv_ref[:, vcols]
        gquery = gkey = gvalue = None
        for h in range(2):
            mine = low_half if h == 0 else jnp.logical_not(low_half)
            gcontext_h = jnp.where(mine, gcontext[:, cols], blank)
            probs = probs_ref[0, 2 * p + h]
            gprobs = nt(value, gcontext_h)
            head = 2 * p + h
            gscores = (probs.astype(F32) * (gprobs - offsets[head : head + 1])).astype(BF16)
            parts = (
                tn(gscores, jnp.where(mine, key, blank)),
                nn(gscores, jnp.where(mine, query, blank)),
                nn(probs, gcontext_h),
            )
            if h == 0:
                gquery, gkey, gvalue = parts
            else:
                gquery, gkey, gvalue = gquery + parts[0], gkey + parts[1], gvalue + parts[2]
        gquery = (gquery * (HEAD**-0.5)).astype(BF16)
        gmixed_ref[:, cols] = gquery
        gmixed_ref[:, kcols] = gkey.astype(BF16)
        gvalue = gvalue.astype(BF16)
        gmixed_ref[:, vcols] = gvalue
        small_ref[0:1, cols] += fold_rows(gquery.astype(F32))
        small_ref[1:2, cols] += fold_rows(gvalue.astype(F32))
    ready(weights[1])
    gtokens_ref[...] = (gattn.astype(F32) + nt(gmixed_ref[...], in_proj[...])).astype(BF16)


def attention_back(gattn, context, qkv, probs, small, params):
    in_proj, out_proj = params[0], params[2]
    tokens, width = context.shape
    sds = jax.ShapeDtypeStruct
    return pl.pallas_call(
        attention_back_kernel,
        grid=(tokens // ROWS,),
        in_specs=[
            rows(width),
            rows(width),
            rows(3 * width),
            pl.BlockSpec((1, *probs.shape[1:]), lambda i: (i, 0, 0, 0)),
            full(small),
            FAR,
            FAR,
        ],
        out_specs=[
            rows(3 * width),
            rows(width),
            pl.BlockSpec(small.shape, lambda i: (0, 0)),
        ],
        out_shape=[
            sds((tokens, 3 * width), BF16),
            sds((tokens, width), BF16),
            sds(small.shape, F32),
        ],
        scratch_shapes=room(out_proj, in_proj),
        compiler_params=pltpu.CompilerParams(vmem_limit_bytes=VMEM_BYTES),
        cost_estimate=cost(tokens / 70),
        name="attention_backward",
    )(gattn, context, qkv, probs, small, out_proj, in_proj)


def match_kernel(masks, questions, passages, blocks_ref, spot, summed_ref, lens_ref, loss_ref, grow_ref, units_ref):
    per_device, width = summed_ref.shape
    for k, mask in enumerate(masks):
        lead = pl.multiple_of((spot[0] ^ mask) * per_device, per_device)
        units_ref[pl.ds(lead, per_device), :] = blocks_ref[k]
    every = units_ref[...]
    count = every.shape[0]
    units = every[:, :width]
    scale = SHARPNESS / width
    ri = lax.broadcasted_iota(jnp.int32, (count, count), 0)
    ci = lax.broadcasted_iota(jnp.int32, (count, count), 1)
    pick = jnp.where(
        lax.broadcasted_iota(jnp.int32, (8, 128), 0) == lax.broadcasted_iota(jnp.int32, (8, 128), 1), 1.0, 0.0
    ).astype(BF16)
    digits = nt(pick, every[:, width:])
    positive = (digits[0:1] * 256.0 + digits[1:2]).astype(jnp.int32)
    place = (positive // passages) * per_device + questions + positive % passages
    rlocal = ri % per_device
    is_passage = jnp.logical_and(rlocal >= questions, rlocal < questions + passages)
    is_question = (ci[0:1] % per_device) < questions
    match = nt(units, units) * scale
    shown = jnp.where(is_passage, match, NEG)
    top = jnp.max(shown, 0, keepdims=True)
    total = jnp.sum(jnp.exp(shown - top), 0, keepdims=True)
    logsum = top + jnp.log(total)
    hit = ri == place
    chosen = jnp.sum(jnp.where(hit, match, 0.0), 0, keepdims=True)
    loss_ref[...] = jnp.sum(jnp.where(is_question, logsum - chosen, 0.0), 1, keepdims=True)

    first = spot[0] * per_device
    own = blocks_ref[0]
    own_units = own[:, :width]
    rown = lax.broadcasted_iota(jnp.int32, (per_device, count), 0)
    cown = lax.broadcasted_iota(jnp.int32, (per_device, count), 1)
    match_own = nt(own_units, units) * scale
    hit_p = jnp.logical_and(place == first + rown, is_question)
    share_p = jnp.exp(match_own - logsum) - jnp.where(hit_p, 1.0, 0.0)
    share_p = jnp.where(is_question, share_p, 0.0)
    clocal = cown % per_device
    col_passage = jnp.logical_and(clocal >= questions, clocal < questions + passages)
    shown_q = jnp.where(col_passage, match_own, NEG)
    weight_q = jnp.exp(shown_q - jnp.max(shown_q, 1, keepdims=True))
    code = own[:, width:].astype(F32)
    positive_q = (code[:, 0:1] * 256.0 + code[:, 1:2]).astype(jnp.int32)
    place_q = (positive_q // passages) * per_device + questions + positive_q % passages
    share_q = weight_q / jnp.sum(weight_q, 1, keepdims=True) - jnp.where(cown == place_q, 1.0, 0.0)
    share = jnp.where(rown < questions, share_q, share_p).astype(BF16)
    gunit = nn(share, units) * scale
    summed = summed_ref[...]
    r = lax.rsqrt(jnp.mean(summed * summed, -1, keepdims=True) + EPS)
    gsummed = r * gunit - (r * r * r) * summed * jnp.mean(gunit * summed, -1, keepdims=True)
    grow_ref[...] = gsummed / lens_ref[:, 0:1]


def match_loss(blocks, masks, spot, summed, lens, questions, passages):
    count, per_device, wide = blocks.shape
    vmem = pl.BlockSpec(memory_space=pltpu.VMEM)
    return pl.pallas_call(
        partial(match_kernel, masks, questions, passages),
        in_specs=[vmem, pl.BlockSpec(memory_space=pltpu.SMEM), vmem, vmem],
        out_specs=[vmem, vmem],
        out_shape=[
            jax.ShapeDtypeStruct((1, 1), F32),
            jax.ShapeDtypeStruct(summed.shape, F32),
        ],
        scratch_shapes=[pltpu.VMEM((count * per_device, wide), BF16)],
        compiler_params=pltpu.CompilerParams(vmem_limit_bytes=VMEM_BYTES),
        cost_estimate=cost(3),
        name="match_loss",
    )(blocks, spot, summed, lens)


ORDERS = ("xyz", "yxz")
PIECE = 512


def axis_layout(devices):
    bits = devices.bit_length() - 2
    x = bits // 3
    y = (bits - x) // 2
    return {"x": (1, x), "y": (1 + x, y), "z": (1 + x + y, bits - x - y)}


def chip_number(me, devices, order):
    layout = axis_layout(devices)
    number = jnp.zeros((), jnp.int32)
    for axis in order:
        start, count = layout[axis]
        number = (number << count) | ((me >> start) & ((1 << count) - 1))
    return number


def segments(streams, devices):
    found = []
    for stream in streams:
        rows_of, start = [], 0
        for height, terms in stream:
            columns = sum(n for *_, n in terms) // PIECE
            tall = height * columns // devices
            rows_of.append((start, tall, columns))
            start += -(-tall // 16) * 16
        found.append(rows_of)
    return found, start


def weight_grad_kernel(streams, places, spots, *refs):
    *operands, send_ref, keep_ref = refs
    for side, out in enumerate((send_ref, keep_ref)):
        for stream, parts in enumerate(streams):
            for (height, terms), (top, tall, columns) in zip(parts, places[stream]):
                column = 0
                half = height // 2
                step = min(half, 256)
                for x, g, first, n in terms:
                    for s in range(half // step):
                        lead = pl.multiple_of((spots[0] ^ (1 - side)) * half + s * step, step)
                        tile = tn(
                            operands[x][:, pl.ds(lead, step)], operands[g][:, first : first + n]
                        ).astype(BF16)
                        for b in range(step // tall):
                            for c in range(n // PIECE):
                                number = (s * (step // tall) + b) * columns + column + c
                                out[stream, number ^ spots[1 + stream], top : top + tall] = tile[
                                    b * tall : (b + 1) * tall, c * PIECE : (c + 1) * PIECE
                                ]
                    column += n // PIECE


def weight_grad(operands, streams, spots, devices, micros):
    places, tall = segments(streams, devices)
    vmem = pl.BlockSpec(memory_space=pltpu.VMEM)
    out = jax.ShapeDtypeStruct((len(streams), devices // 2, tall, PIECE), BF16)
    return pl.pallas_call(
        partial(weight_grad_kernel, streams, places),
        in_specs=[pl.BlockSpec(memory_space=pltpu.SMEM), *[vmem] * len(operands)],
        out_specs=[vmem, vmem],
        out_shape=[out, out],
        compiler_params=pltpu.CompilerParams(vmem_limit_bytes=VMEM_BYTES),
        cost_estimate=cost(micros),
        name="weight_gradient",
    )(spots, *operands)


PARTS = 4


def place_kernel(outputs, spots, *refs):
    inputs, outs = refs[:4], refs[4:]
    group = inputs[0].shape[1]
    for side in range(2):

        @pl.when(pl.program_id(0) == side)
        def _(side=side):
            for out, blocks in zip(outs, outputs):
                for k, (stream, (top, tall, columns), column) in enumerate(blocks):
                    inner = spots[1 + stream] & (group - 1)
                    for b in range(out.shape[0] // tall):
                        piece = inputs[2 * side + stream][
                            0, (b * columns + column) ^ inner, top : top + tall
                        ]
                        out[b * tall : (b + 1) * tall, k * PIECE : (k + 1) * PIECE] = piece.astype(F32)


def place(mine, other, spots, streams, outputs, devices):
    _, pieces, rows_of, _ = mine.shape
    group = pieces // PARTS
    places, _ = segments(streams, devices)

    def piece_spec(side, stream):
        def index(s, g, spots):
            g = jnp.where(s == side, g, (1 - side) * (PARTS - 1))
            return (stream, g ^ spots[3 + stream], 0, 0)

        return pl.BlockSpec((1, group, rows_of, PIECE), index)

    return pl.pallas_call(
        partial(
            place_kernel,
            [[(stream, places[stream][part], column) for stream, part, column in b] for _, b in outputs],
        ),
        grid_spec=pltpu.PrefetchScalarGridSpec(
            num_scalar_prefetch=1,
            grid=(2, PARTS),
            in_specs=[piece_spec(side, stream) for side in range(2) for stream in range(2)],
            out_specs=[
                pl.BlockSpec(
                    (height // (2 * PARTS), PIECE * len(b)),
                    lambda s, g, spots: ((spots[0] ^ s) * PARTS + g, 0),
                )
                for height, b in outputs
            ],
        ),
        out_shape=[jax.ShapeDtypeStruct((height, PIECE * len(b)), F32) for height, b in outputs],
        compiler_params=pltpu.CompilerParams(vmem_limit_bytes=VMEM_BYTES),
        cost_estimate=cost(5),
        name="place_gradient",
    )(spots, mine, mine, other, other)


def swap(array, mask, devices):
    return lax.ppermute(array, "dp", [(i, i ^ mask) for i in range(devices)])


def add(*terms):
    total = terms[0].astype(F32)
    for t in terms[1:]:
        total = total + t.astype(F32)
    return total.astype(BF16)


def sum_pieces(send, keep, devices):
    layout = axis_layout(devices)
    (got,) = yield [(send, 1)]
    held = [[keep[i], got[i]] for i in range(len(ORDERS))]
    for level in range(2):
        parts = []
        for terms, order in zip(held, ORDERS):
            ways = 1 << layout[order[level]][1]
            size = terms[0].shape[0] // ways
            parts.append([add(*[t[m * size : (m + 1) * size] for t in terms]) for m in range(ways)])
        got = yield [
            (p, m << layout[order[level]][0])
            for stream, order in zip(parts, ORDERS)
            for m, p in enumerate(stream)
            if m
        ]
        held = []
        for stream in parts:
            held.append([stream[0], *got[: len(stream) - 1]])
            got = got[len(stream) - 1 :]
    start, count = layout["z"]
    ways = 1 << count
    size = held[0][0].shape[0] // ways
    both = [
        jnp.stack([add(*[t[m * size : (m + 1) * size] for t in terms]) for terms in held])
        for m in range(ways)
    ]
    got = yield [(b, m << start) for m, b in enumerate(both) if m]
    total = add(both[0], *got)
    got = yield [(total, m << start) for m in range(1, ways)]
    every = jnp.concatenate([total, *got], 1)
    done = [every[i] for i in range(len(ORDERS))]
    for level in (1, 0):
        sends = []
        for mine, order in zip(done, ORDERS):
            start, count = layout[order[level]]
            sends.append([(mine, m << start) for m in range(1, 1 << count)])
        got = yield [s for stream in sends for s in stream]
        grown = []
        for mine, stream in zip(done, sends):
            grown.append(jnp.concatenate([mine, *got[: len(stream)]], 0))
            got = got[len(stream) :]
        done = grown
    mine = jnp.stack(done)
    (other,) = yield [(mine, 1)]
    return mine, other


def sum_small(array, devices):
    for bit in range(devices.bit_length() - 1):
        (got,) = yield [(array, 1 << bit)]
        array = array + got
    return array


class Line:
    def __init__(self, devices):
        self.devices = devices
        self.running = {}
        self.done = {}

    def add(self, name, steps):
        self.running[name] = (steps, next(steps))

    def step(self, names, kernel=None, operand=None):
        names = [n for n in names if n in self.running]
        sends = [self.running[n][1] for n in names]
        arrays = [[a for a, _ in s] for s in sends]
        arrays, operand = lax.optimization_barrier((arrays, operand))
        got = [[swap(a, m, self.devices) for a, (_, m) in zip(x, s)] for x, s in zip(arrays, sends)]
        result = kernel(operand) if kernel else None
        got, result = lax.optimization_barrier((got, result))
        for n, g in zip(names, got):
            steps, _ = self.running.pop(n)
            try:
                self.running[n] = (steps, steps.send(g))
            except StopIteration as end:
                self.done[n] = end.value
        return result


def gather_stages(devices):
    (x, nx), (y, ny), (z, nz) = (axis_layout(devices)[a] for a in "xyz")
    plane = [(x, nx + ny)] if nx + ny < 3 else [(y, ny), (x, nx)]
    return [(z, nz), *plane, (0, 1)]


def gather_units(own, devices):
    every, masks = own[None], [0]
    for start, count in gather_stages(devices):
        steps = [m << start for m in range(1 << count)]
        every = jnp.concatenate([every] + [swap(every, m, devices) for m in steps[1:]], 0)
        masks = [k ^ m for m in steps for k in masks]
    return every, masks


def on_device(devices, *args):
    (question_tokens, passage_tokens, question_lengths, passage_lengths, positives), weights = args[:5], args[5:]
    question_params, passage_params = weights[:9], weights[9:]
    me = lax.axis_index("dp").astype(jnp.int32)
    chips = [chip_number(me, devices, order) for order in ORDERS]
    group = devices // 8
    spots = jnp.stack([me & 1, *chips, *[c // group for c in chips]])
    questions, question_seq, width = question_tokens.shape
    passages, passage_seq, _ = passage_tokens.shape

    q_fwd, p_fwd = forward(
        [
            (question_tokens, question_lengths, question_params),
            (passage_tokens, passage_lengths, passage_params),
        ]
    )
    q_summed = q_fwd[1].reshape(questions, width)
    p_summed = p_fwd[1].reshape(passages, width)
    per_device = -(-(questions + passages) // 16) * 16
    spare = per_device - questions - passages
    summed = jnp.concatenate([q_summed, p_summed, jnp.zeros((spare, width), F32)], 0)
    units = (summed * lax.rsqrt(jnp.mean(summed * summed, -1, keepdims=True) + EPS)).astype(BF16)
    code = jnp.pad(
        jnp.stack([positives // 256, positives % 256], 1).astype(BF16),
        ((0, per_device - questions), (0, 126)),
    )
    every, masks = gather_units(jnp.concatenate([units, code], 1), devices)
    lens = jnp.concatenate([question_lengths, passage_lengths, jnp.ones((spare,), jnp.int32)])
    lens = jnp.broadcast_to(lens.astype(F32)[:, None], (per_device, 128))
    loss, grow = match_loss(every, masks, me[None], summed, lens, questions, passages)

    _, _, p_qkv, p_probs, p_context, *p_norm, p_middle, p_act, p_slope = p_fwd
    _, _, q_qkv, q_probs, q_context, *q_norm, q_middle, q_act, q_slope = q_fwd
    inner = p_act.shape[1]
    x_p, x_q = passage_tokens.reshape(-1, width), question_tokens.reshape(-1, width)

    def ffn_p(part):
        return ffn_back(passage_lengths, part, (*p_norm, p_slope), passage_params, passage_seq)

    def ffn_q(part):
        return ffn_back(question_lengths, part, (*q_norm, q_slope), question_params, question_seq)

    ffn_parts = [(width, [(4, 5, 0, inner)])], [(inner, [(6, 7, 0, width)])]
    attention_parts = (
        [(width, [(0, 1, 0, 2 * width)])],
        [(width, [(0, 1, 2 * width, width), (2, 3, 0, width)])],
    )
    all_parts = [f + a for f, a in zip(ffn_parts, attention_parts)]
    ffn_outputs = [(width, [(0, 0, c) for c in range(inner // PIECE)]), (inner, [(1, 0, 0)])]

    def attention_outputs(part):
        return [(width, [(0, part, 0), (0, part, 1), (1, part, 0)]), (width, [(1, part, 1)])]

    def grads(x, gmixed, context, gattn, middle, gpre, act, gffn, parts, micros):
        operands = [x, gmixed, context, gattn, middle, gpre, act, gffn]
        used = sorted({k for stream in parts for _, terms in stream for x, g, *_ in terms for k in (x, g)})
        parts = [
            [(h, [(used.index(x), used.index(g), *cols) for x, g, *cols in terms]) for h, terms in stream]
            for stream in parts
        ]
        return weight_grad([operands[k] for k in used], parts, spots, devices, micros)

    line = Line(devices)
    q_gffn, q_gpre, q_attn, q_small = ffn_q(grow[:questions])
    q_mixed, q_grad, q_small = attention_back(
        q_attn, q_context, q_qkv, q_probs, q_small, question_params
    )
    halves = grads(x_q, q_mixed, q_context, q_attn, q_middle, q_gpre, q_act, q_gffn, all_parts, 7)
    line.add("q", sum_pieces(*halves, devices))
    p_gffn, p_gpre, p_attn, p_small = line.step("q", ffn_p, grow[questions : questions + passages])
    halves = line.step(
        "q", lambda g: grads(None, None, None, None, p_middle, g, p_act, p_gffn, ffn_parts, 11), p_gpre
    )
    line.add("p", sum_pieces(*halves, devices))
    p_mixed, p_grad, p_small = line.step(
        "qp", lambda g: attention_back(g, p_context, p_qkv, p_probs, p_small, passage_params), p_attn
    )
    line.add("s", sum_small(jnp.stack([q_small, p_small]), devices))
    halves = line.step(
        "qps", lambda g: grads(x_p, g, p_context, p_attn, None, None, None, None, attention_parts, 5), p_mixed
    )
    line.add("a", sum_pieces(*halves, devices))
    for _ in range(4):
        line.step("qpas")
    q_outs = line.step(
        "pas",
        lambda mine: place(
            mine, line.done["q"][1], spots, all_parts, ffn_outputs + attention_outputs(1), devices
        ),
        line.done["q"][0],
    )
    line.step("pas")
    p_outs = line.step(
        "as",
        lambda mine: place(mine, line.done["p"][1], spots, ffn_parts, ffn_outputs, devices),
        line.done["p"][0],
    )
    while line.running:
        line.step("as")
    q_up, q_down, q_in, q_out = q_outs
    p_up, p_down = p_outs
    p_in, p_out = place(*line.done["a"], spots, attention_parts, attention_outputs(0), devices)
    small = line.done["s"]

    def outputs(small, gin, gout, gup, gdown):
        return (
            gin,
            small[0:2],
            gout,
            small[2:4],
            small[4:6],
            small[6:8],
            gup,
            small[8 : 8 + inner // width].reshape(inner),
            gdown,
        )

    return (
        loss[0, 0],
        q_fwd[0].reshape(question_tokens.shape),
        p_fwd[0].reshape(passage_tokens.shape),
        q_grad.reshape(question_tokens.shape),
        p_grad.reshape(passage_tokens.shape),
        *outputs(small[0], q_in, q_out, q_up, q_down),
        *outputs(small[1], p_in, p_out, p_up, p_down),
    )


def solution(mesh):
    batch = P("dp", None, None)
    return jax.shard_map(
        partial(on_device, mesh.shape["dp"]),
        mesh=mesh,
        in_specs=(batch, batch, P("dp"), P("dp"), P("dp"), *[P()] * 18),
        out_specs=(P(), batch, batch, batch, batch, *[P()] * 18),
        check_vma=False,
    )
```

```python
import math
from functools import partial

import jax
import jax.numpy as jnp
from jax import lax
from jax.experimental import pallas as pl
from jax.experimental.pallas import tpu as pltpu
from jax.sharding import PartitionSpec as P

HEAD = 64
ROWS = 256
SHARPNESS = 20.0
NEG = -1e30
EPS = 1e-06
F32 = jnp.float32
BF16 = jnp.bfloat16
VMEM_BYTES = 48 * 1024 * 1024
LARGE_VMEM_BYTES = 60 * 1024 * 1024

DENSITY = 1.0 / math.sqrt(2.0 * math.pi)


def nn(a, b):
    return lax.dot_general(a, b, (((1,), (0,)), ((), ())), preferred_element_type=F32)


def nt(a, b):
    return lax.dot_general(a, b, (((1,), (1,)), ((), ())), preferred_element_type=F32)


def tn(a, b):
    return lax.dot_general(a, b, (((0,), (0,)), ((), ())), preferred_element_type=F32)


def gelu_pair(v):
    cdf = 0.5 + 0.5 * lax.erf(v * math.sqrt(0.5))
    bell = jnp.exp(v * v * -0.5)
    return v * cdf, cdf + v * (bell * DENSITY)


def layer_norm(v):
    center = v - jnp.mean(v, -1, keepdims=True)
    scale = lax.rsqrt(jnp.mean(center * center, -1, keepdims=True) + EPS)
    return center * scale, scale


def norm_back(grad, unit, scale, gain):
    t = grad * gain
    return scale * (
        t - jnp.mean(t, -1, keepdims=True) - unit * jnp.mean(t * unit, -1, keepdims=True)
    )


def fold_rows(v):
    return jnp.sum(v, 0, keepdims=True)


def cost(micros):
    return pl.CostEstimate(flops=int(micros * 1.15e9), bytes_accessed=0, transcendentals=0)


def full(array):
    zeros = (0,) * array.ndim
    return pl.BlockSpec(array.shape, lambda *_: zeros, pipeline_mode=pl.Buffered(1))


FAR = pl.BlockSpec(memory_space=pltpu.HBM)


def room(*arrays):
    return [*[pltpu.VMEM(a.shape, a.dtype) for a in arrays], pltpu.SemaphoreType.DMA((len(arrays),))]


def fetch(*pairs, arrived):
    copies = [pltpu.make_async_copy(far, near, arrived.at[i]) for i, (far, near) in enumerate(pairs)]

    @pl.when(pl.program_id(0) == 0)
    def _():
        for copy in copies:
            copy.start()

    return copies


def ready(copy, step=0):
    @pl.when(pl.program_id(0) == step)
    def _():
        copy.wait()


def rows(width, first=0):
    return pl.BlockSpec((ROWS, width), lambda i, *_: (i + first, 0))


KEPT = pl.BlockSpec(memory_space=pl.ANY)


def forward_kernel(seqs, counts, *refs):
    lens, refs = refs[:2], refs[2:]
    near, far, outs, held = refs[:12], refs[12:20], refs[20:42], refs[42:50]
    copies = fetch(*zip(far, held), arrived=refs[50])
    step = pl.program_id(0)
    first = 0
    for e, (seq, count) in enumerate(zip(seqs, counts)):

        @pl.when(jnp.logical_and(step >= first, step < first + count))
        def _(e=e, seq=seq, first=first):
            forward_block(
                seq,
                step - first,
                [partial(ready, copy, first) for copy in copies[4 * e : 4 * e + 4]],
                lens[e],
                *near[6 * e : 6 * e + 6],
                *outs[11 * e : 11 * e + 11],
                *held[4 * e : 4 * e + 4],
            )

        first += count


def forward_block(
    seq,
    block,
    wait,
    lens,
    x_ref,
    in_bias,
    out_bias,
    gains,
    shifts,
    up_bias,
    out_ref,
    summed_ref,
    qkv_ref,
    probs_ref,
    context_ref,
    unit1_ref,
    unit2_ref,
    scale_ref,
    middle_ref,
    act_ref,
    slope_ref,
    in_proj,
    out_proj,
    up,
    down,
):
    groups = ROWS // seq
    width = x_ref.shape[1]
    row = lax.broadcasted_iota(jnp.int32, (ROWS, 128), 0)
    lane = lax.broadcasted_iota(jnp.int32, (ROWS, 128), 1)
    slot = lane % HEAD
    low_half = lane < HEAD
    group = row // seq
    limit = jnp.zeros((ROWS, 128), jnp.int32)
    for g in range(groups):
        limit = jnp.where(group == g, lens[block * groups + g], limit)
    live = (row - group * seq) < limit
    query_mark = jnp.where(slot == group, 1.0, 0.0).astype(BF16)
    key_mark = jnp.where(
        slot < groups, jnp.where(jnp.logical_and(slot == group, live), 0.0, NEG), 0.0
    ).astype(BF16)
    x = x_ref[...]
    wait[0]()
    mixed = nn(x, in_proj[...])
    query = ((mixed[:, :width] + in_bias[0:1]).astype(BF16) * (HEAD**-0.5)).astype(BF16)
    key = mixed[:, width : 2 * width].astype(BF16)
    value = (mixed[:, 2 * width :] + in_bias[1:2]).astype(BF16)
    qkv_ref[:, :width] = query
    qkv_ref[:, width : 2 * width] = key
    qkv_ref[:, 2 * width :] = value
    pairs = []
    for p in range(width // 128):
        cols = slice(128 * p, 128 * p + 128)
        total = None
        for h in range(2):
            mine = low_half if h == 0 else jnp.logical_not(low_half)
            query_h = jnp.where(mine, query[:, cols], query_mark)
            key_h = jnp.where(mine, key[:, cols], key_mark)
            value_h = jnp.where(mine, value[:, cols], jnp.zeros_like(key_mark))
            scores = nt(key_h, query_h)
            top = jnp.max(scores, 0, keepdims=True)
            weight = jnp.exp(scores - top)
            probs = (weight * (1.0 / jnp.sum(weight, 0, keepdims=True))).astype(BF16)
            probs_ref[0, 2 * p + h] = probs
            part = tn(probs, value_h)
            total = part if total is None else total + part
        pairs.append(total.astype(BF16))
    context = jnp.concatenate(pairs, 1)
    context_ref[...] = context
    wait[1]()
    first = x.astype(F32) + nn(context, out_proj[...]) + out_bias[0:1]
    unit1, scale1 = layer_norm(first)
    unit1_ref[...] = unit1.astype(BF16)
    middle_full = unit1 * gains[0:1] + shifts[0:1]
    middle = middle_full.astype(BF16)
    middle_ref[...] = middle
    second = middle_full + out_bias[1:2]
    wait[2]()
    wait[3]()
    chunk = 256
    for c in range(up.shape[1] // chunk):
        cols = slice(chunk * c, chunk * c + chunk)
        pre = nn(middle, up[:, cols]) + up_bias[:, cols]
        act, slope = gelu_pair(pre)
        act = act.astype(BF16)
        act_ref[:, cols] = act
        slope_ref[:, cols] = slope.astype(BF16)
        second += nn(act, down[cols, :])
    unit2, scale2 = layer_norm(second)
    unit2_ref[...] = unit2.astype(BF16)
    scale_ref[...] = jnp.where(lane == 0, scale1, scale2)
    out = unit2 * gains[1:2] + shifts[1:2]
    out_ref[...] = out.astype(BF16)
    kept = jnp.where(live[:, :1], out, 0.0)
    for g in range(groups):
        length = lens[block * groups + g].astype(F32)
        summed_ref[0, g : g + 1] = fold_rows(kept[g * seq : (g + 1) * seq]) / length


def forward(encoders):
    sds = jax.ShapeDtypeStruct
    lens, near, near_specs, far, out_specs, out_shape, seqs, counts = [], [], [], [], [], [], [], []
    first = 0
    for x, length, params in encoders:
        in_proj, in_bias, out_proj, out_bias, gains, shifts, up, up_bias, down = params
        examples, seq, width = x.shape
        tokens = examples * seq
        blocks, groups, heads = tokens // ROWS, ROWS // seq, width // HEAD
        inner = up.shape[1]

        def block(*shape, first=first, blocks=blocks):
            rest = (0,) * (len(shape) - 1)
            return pl.BlockSpec(shape, lambda i, *_: (jnp.clip(i - first, 0, blocks - 1), *rest))

        small = (in_bias, out_bias, gains, shifts, up_bias[None])
        lens.append(length)
        near += [x.reshape(tokens, width), *small]
        near_specs += [block(ROWS, width), *[full(w) for w in small]]
        far += [in_proj, out_proj, up, down]
        shapes = [
            ((tokens, width), BF16),
            ((blocks, groups, width), F32),
            ((tokens, 3 * width), BF16),
            ((blocks, heads, ROWS, ROWS), BF16),
            ((tokens, width), BF16),
            ((tokens, width), BF16),
            ((tokens, width), BF16),
            ((tokens, 128), F32),
            ((tokens, width), BF16),
            ((tokens, inner), BF16),
            ((tokens, inner), BF16),
        ]
        for shape, kind in shapes:
            out_specs.append(block(1 if shape[0] == blocks else ROWS, *shape[1:]))
            out_shape.append(sds(shape, kind))
        seqs.append(seq)
        counts.append(blocks)
        first += blocks
    outs = pl.pallas_call(
        partial(forward_kernel, seqs, counts),
        grid_spec=pltpu.PrefetchScalarGridSpec(
            num_scalar_prefetch=2,
            grid=(first,),
            in_specs=[*near_specs, *[FAR] * len(far)],
            out_specs=out_specs,
            scratch_shapes=room(*far),
        ),
        out_shape=out_shape,
        compiler_params=pltpu.CompilerParams(vmem_limit_bytes=LARGE_VMEM_BYTES),
        cost_estimate=cost(40),
        name="layer_forward",
    )(*lens, *near, *far)
    return outs[:11], outs[11:]


def ffn_back_kernel(seq, first, lens, *refs):
    near, (down_far, up_far, before), refs = refs[:6], refs[6:9], refs[9:]
    outs, (down, up, arrived) = refs[-7:-3], refs[-3:]
    copies = fetch((down_far, down), (up_far, up), arrived=arrived)

    @pl.when(pl.program_id(0) == 0)
    def _():
        outs[3][...] = before[...]

    ffn_back_block(seq, first + pl.program_id(0), lens, copies, *near, *outs, down, up)


def ffn_back_block(
    seq,
    block,
    lens,
    copies,
    grow_ref,
    unit1_ref,
    unit2_ref,
    scale_ref,
    slope_ref,
    gains,
    gffn_ref,
    gpre_ref,
    gattn_ref,
    small_ref,
    down,
    up,
):
    groups = ROWS // seq
    width = unit1_ref.shape[1]
    row = lax.broadcasted_iota(jnp.int32, (seq, width), 0)
    grad_out = jnp.concatenate(
        [
            jnp.where(row < lens[block * groups + g], grow_ref[0, g : g + 1], 0.0)
            for g in range(groups)
        ],
        0,
    )
    unit2 = unit2_ref[...].astype(F32)
    small_ref[7:8] += fold_rows(grad_out)
    small_ref[5:6] += fold_rows(grad_out * unit2)
    gsecond = norm_back(grad_out, unit2, scale_ref[:, 1:2], gains[1:2])
    gffn = gsecond.astype(BF16)
    gffn_ref[...] = gffn
    small_ref[3:4] += fold_rows(gffn.astype(F32))
    gmiddle = gsecond
    ready(copies[0])
    ready(copies[1])
    chunk = 256
    for c in range(up.shape[1] // chunk):
        cols = slice(chunk * c, chunk * c + chunk)
        gpre = (nt(gffn, down[cols, :]) * slope_ref[:, cols].astype(F32)).astype(BF16)
        gpre_ref[:, cols] = gpre
        line, left = 8 + chunk * c // width, chunk * c % width
        small_ref[line : line + 1, left : left + chunk] += fold_rows(gpre.astype(F32))
        gmiddle += nt(gpre, up[:, cols])
    unit1 = unit1_ref[...].astype(F32)
    small_ref[6:7] += fold_rows(gmiddle)
    small_ref[4:5] += fold_rows(gmiddle * unit1)
    gfirst = norm_back(gmiddle, unit1, scale_ref[:, 0:1], gains[0:1])
    gattn = gfirst.astype(BF16)
    gattn_ref[...] = gattn
    small_ref[2:3] += fold_rows(gattn.astype(F32))


def ffn_back(lens, grow, kept, params, seq, first, count, before):
    unit1, unit2, scale, slope = kept
    _, _, _, _, gains, _, up, _, down = params
    tokens, width = unit1.shape
    blocks, groups, inner = tokens // ROWS, ROWS // seq, up.shape[1]
    *arrays, small = before
    sds = jax.ShapeDtypeStruct
    return pl.pallas_call(
        partial(ffn_back_kernel, seq, first),
        grid_spec=pltpu.PrefetchScalarGridSpec(
            num_scalar_prefetch=1,
            grid=(count,),
            in_specs=[
                pl.BlockSpec((1, groups, width), lambda i, *_: (i + first, 0, 0)),
                rows(width, first),
                rows(width, first),
                rows(128, first),
                rows(inner, first),
                full(gains),
                FAR,
                FAR,
                full(small),
                *[KEPT] * len(arrays),
            ],
            out_specs=[
                rows(width, first),
                rows(inner, first),
                rows(width, first),
                pl.BlockSpec((16, width), lambda i, *_: (0, 0)),
            ],
            scratch_shapes=room(down, up),
        ),
        out_shape=[
            sds((tokens, width), BF16),
            sds((tokens, inner), BF16),
            sds((tokens, width), BF16),
            sds((16, width), F32),
        ],
        input_output_aliases={10 + i: i for i in range(len(arrays))},
        compiler_params=pltpu.CompilerParams(vmem_limit_bytes=VMEM_BYTES),
        cost_estimate=cost(count * ROWS / 80),
        name="ffn_backward",
    )(
        lens, grow.reshape(blocks, groups, width), unit1, unit2, scale, slope, gains, down, up, small, *arrays
    )


def attention_back_kernel(*refs):
    near, before_ref, (out_proj_far, in_proj_far), refs = refs[:4], refs[4], refs[5:7], refs[7:]
    outs, (out_proj, in_proj, arrived) = refs[-6:-3], refs[-3:]
    copies = fetch((out_proj_far, out_proj), (in_proj_far, in_proj), arrived=arrived)

    @pl.when(pl.program_id(0) == 0)
    def _():
        outs[2][...] = before_ref[...]

    attention_back_block(copies, *near, *outs, out_proj, in_proj)


def attention_back_block(
    copies,
    gattn_ref,
    context_ref,
    qkv_ref,
    probs_ref,
    gmixed_ref,
    gtokens_ref,
    small_ref,
    out_proj,
    in_proj,
):
    width = gattn_ref.shape[1]
    lane = lax.broadcasted_iota(jnp.int32, (ROWS, 128), 1)
    low_half = lane < HEAD
    blank = jnp.zeros((ROWS, 128), BF16)
    gattn = gattn_ref[...]
    ready(copies[0])
    gcontext = nt(gattn, out_proj[...]).astype(BF16)
    heads = width // HEAD
    member = (
        lax.broadcasted_iota(jnp.int32, (16, width), 1) // HEAD
        == lax.broadcasted_iota(jnp.int32, (16, width), 0)
    )
    member = jnp.where(member, 1.0, 0.0).astype(BF16)
    product = gcontext.astype(F32) * context_ref[...].astype(F32)
    coarse = product.astype(BF16)
    fine = (product - coarse.astype(F32)).astype(BF16)
    offsets = nt(member, coarse) + nt(member, fine)
    for p in range(width // 128):
        cols = slice(128 * p, 128 * p + 128)
        kcols = slice(width + 128 * p, width + 128 * p + 128)
        vcols = slice(2 * width + 128 * p, 2 * width + 128 * p + 128)
        query, key, value = qkv_ref[:, cols], qkv_ref[:, kcols], qkv_ref[:, vcols]
        gquery = gkey = gvalue = None
        for h in range(2):
            mine = low_half if h == 0 else jnp.logical_not(low_half)
            gcontext_h = jnp.where(mine, gcontext[:, cols], blank)
            probs = probs_ref[0, 2 * p + h]
            gprobs = nt(value, gcontext_h)
            head = 2 * p + h
            gscores = (probs.astype(F32) * (gprobs - offsets[head : head + 1])).astype(BF16)
            parts = (
                tn(gscores, jnp.where(mine, key, blank)),
                nn(gscores, jnp.where(mine, query, blank)),
                nn(probs, gcontext_h),
            )
            if h == 0:
                gquery, gkey, gvalue = parts
            else:
                gquery, gkey, gvalue = gquery + parts[0], gkey + parts[1], gvalue + parts[2]
        gquery = (gquery * (HEAD**-0.5)).astype(BF16)
        gmixed_ref[:, cols] = gquery
        gmixed_ref[:, kcols] = gkey.astype(BF16)
        gvalue = gvalue.astype(BF16)
        gmixed_ref[:, vcols] = gvalue
        small_ref[0:1, cols] += fold_rows(gquery.astype(F32))
        small_ref[1:2, cols] += fold_rows(gvalue.astype(F32))
    ready(copies[1])
    gtokens_ref[...] = (gattn.astype(F32) + nt(gmixed_ref[...], in_proj[...])).astype(BF16)


def attention_back(gattn, context, qkv, probs, small, params, first, count, arrays=()):
    in_proj, out_proj = params[0], params[2]
    tokens, width = context.shape
    sds = jax.ShapeDtypeStruct
    return pl.pallas_call(
        attention_back_kernel,
        grid=(count,),
        in_specs=[
            rows(width, first),
            rows(width, first),
            rows(3 * width, first),
            pl.BlockSpec((1, *probs.shape[1:]), lambda i: (i + first, 0, 0, 0)),
            full(small),
            FAR,
            FAR,
            *[KEPT] * len(arrays),
        ],
        out_specs=[
            rows(3 * width, first),
            rows(width, first),
            pl.BlockSpec(small.shape, lambda i: (0, 0)),
        ],
        out_shape=[
            sds((tokens, 3 * width), BF16),
            sds((tokens, width), BF16),
            sds(small.shape, F32),
        ],
        scratch_shapes=room(out_proj, in_proj),
        input_output_aliases={7 + i: i for i in range(len(arrays))},
        compiler_params=pltpu.CompilerParams(vmem_limit_bytes=VMEM_BYTES),
        cost_estimate=cost(count * ROWS / 70),
        name="attention_backward",
    )(gattn, context, qkv, probs, small, out_proj, in_proj, *arrays)


def match_kernel(masks, questions, passages, blocks_ref, spot, summed_ref, lens_ref, loss_ref, grow_ref, units_ref):
    per_device, width = summed_ref.shape
    for k, mask in enumerate(masks):
        lead = pl.multiple_of((spot[0] ^ mask) * per_device, per_device)
        units_ref[pl.ds(lead, per_device), :] = blocks_ref[k]
    every = units_ref[...]
    count = every.shape[0]
    units = every[:, :width]
    scale = SHARPNESS / width
    ri = lax.broadcasted_iota(jnp.int32, (count, count), 0)
    ci = lax.broadcasted_iota(jnp.int32, (count, count), 1)
    pick = jnp.where(
        lax.broadcasted_iota(jnp.int32, (8, 128), 0) == lax.broadcasted_iota(jnp.int32, (8, 128), 1), 1.0, 0.0
    ).astype(BF16)
    digits = nt(pick, every[:, width:])
    positive = (digits[0:1] * 256.0 + digits[1:2]).astype(jnp.int32)
    place = (positive // passages) * per_device + questions + positive % passages
    rlocal = ri % per_device
    is_passage = jnp.logical_and(rlocal >= questions, rlocal < questions + passages)
    is_question = (ci[0:1] % per_device) < questions
    match = nt(units, units) * scale
    shown = jnp.where(is_passage, match, NEG)
    top = jnp.max(shown, 0, keepdims=True)
    total = jnp.sum(jnp.exp(shown - top), 0, keepdims=True)
    logsum = top + jnp.log(total)
    hit = ri == place
    chosen = jnp.sum(jnp.where(hit, match, 0.0), 0, keepdims=True)
    loss_ref[...] = jnp.sum(jnp.where(is_question, logsum - chosen, 0.0), 1, keepdims=True)

    first = spot[0] * per_device
    own = blocks_ref[0]
    own_units = own[:, :width]
    rown = lax.broadcasted_iota(jnp.int32, (per_device, count), 0)
    cown = lax.broadcasted_iota(jnp.int32, (per_device, count), 1)
    match_own = nt(own_units, units) * scale
    hit_p = jnp.logical_and(place == first + rown, is_question)
    share_p = jnp.exp(match_own - logsum) - jnp.where(hit_p, 1.0, 0.0)
    share_p = jnp.where(is_question, share_p, 0.0)
    clocal = cown % per_device
    col_passage = jnp.logical_and(clocal >= questions, clocal < questions + passages)
    shown_q = jnp.where(col_passage, match_own, NEG)
    weight_q = jnp.exp(shown_q - jnp.max(shown_q, 1, keepdims=True))
    code = own[:, width:].astype(F32)
    positive_q = (code[:, 0:1] * 256.0 + code[:, 1:2]).astype(jnp.int32)
    place_q = (positive_q // passages) * per_device + questions + positive_q % passages
    share_q = weight_q / jnp.sum(weight_q, 1, keepdims=True) - jnp.where(cown == place_q, 1.0, 0.0)
    share = jnp.where(rown < questions, share_q, share_p).astype(BF16)
    gunit = nn(share, units) * scale
    summed = summed_ref[...]
    r = lax.rsqrt(jnp.mean(summed * summed, -1, keepdims=True) + EPS)
    gsummed = r * gunit - (r * r * r) * summed * jnp.mean(gunit * summed, -1, keepdims=True)
    grow_ref[...] = gsummed / lens_ref[:, 0:1]


def match_loss(blocks, masks, spot, summed, lens, questions, passages):
    count, per_device, wide = blocks.shape
    vmem = pl.BlockSpec(memory_space=pltpu.VMEM)
    return pl.pallas_call(
        partial(match_kernel, masks, questions, passages),
        in_specs=[vmem, pl.BlockSpec(memory_space=pltpu.SMEM), vmem, vmem],
        out_specs=[vmem, vmem],
        out_shape=[
            jax.ShapeDtypeStruct((1, 1), F32),
            jax.ShapeDtypeStruct(summed.shape, F32),
        ],
        scratch_shapes=[pltpu.VMEM((count * per_device, wide), BF16)],
        compiler_params=pltpu.CompilerParams(vmem_limit_bytes=VMEM_BYTES),
        cost_estimate=cost(3),
        name="match_loss",
    )(blocks, spot, summed, lens)


ORDERS = ("xyz", "yxz")
PIECE = 512


def axis_layout(devices):
    bits = devices.bit_length() - 2
    x = bits // 3
    y = (bits - x) // 2
    return {"x": (1, x), "y": (1 + x, y), "z": (1 + x + y, bits - x - y)}


def chip_number(me, devices, order):
    layout = axis_layout(devices)
    number = jnp.zeros((), jnp.int32)
    for axis in order:
        start, count = layout[axis]
        number = (number << count) | ((me >> start) & ((1 << count) - 1))
    return number


def segments(streams, devices):
    found = []
    for stream in streams:
        rows_of, start = [], 0
        for height, terms in stream:
            columns = sum(n for *_, n in terms) // PIECE
            tall = height * columns // devices
            rows_of.append((start, tall, columns))
            start += -(-tall // 16) * 16
        found.append(rows_of)
    return found, start


def weight_grad_kernel(streams, places, spots, *refs):
    *operands, send_ref, keep_ref = refs
    for side, out in enumerate((send_ref, keep_ref)):
        for stream, parts in enumerate(streams):
            for (height, terms), (top, tall, columns) in zip(parts, places[stream]):
                column = 0
                half = height // 2
                step = min(half, 256)
                for x, g, first, n in terms:
                    for s in range(half // step):
                        lead = pl.multiple_of((spots[0] ^ (1 - side)) * half + s * step, step)
                        tile = tn(
                            operands[x][:, pl.ds(lead, step)], operands[g][:, first : first + n]
                        ).astype(BF16)
                        for b in range(step // tall):
                            for c in range(n // PIECE):
                                number = (s * (step // tall) + b) * columns + column + c
                                out[stream, number ^ spots[1 + stream], top : top + tall] = tile[
                                    b * tall : (b + 1) * tall, c * PIECE : (c + 1) * PIECE
                                ]
                    column += n // PIECE


def weight_grad(operands, streams, spots, devices, micros):
    places, tall = segments(streams, devices)
    vmem = pl.BlockSpec(memory_space=pltpu.VMEM)
    out = jax.ShapeDtypeStruct((len(streams), devices // 2, tall, PIECE), BF16)
    return pl.pallas_call(
        partial(weight_grad_kernel, streams, places),
        in_specs=[pl.BlockSpec(memory_space=pltpu.SMEM), *[vmem] * len(operands)],
        out_specs=[vmem, vmem],
        out_shape=[out, out],
        compiler_params=pltpu.CompilerParams(vmem_limit_bytes=VMEM_BYTES),
        cost_estimate=cost(micros),
        name="weight_gradient",
    )(spots, *operands)


def encoder_back_kernel(seq, streams, places, lens, spots, *refs):
    (grow, unit1, unit2, scale, slope, gains, context, qkv, probs), refs = refs[:9], refs[9:]
    far, (gtokens, small, send, keep), held = refs[:8], refs[8:12], refs[12:20]
    gffn, gpre, gattn, gmixed, arrived = refs[20:]
    copies = fetch(*zip(far, held), arrived=arrived)
    down, up, out_proj, in_proj, x, contexts, middle, act = held
    block = pl.program_id(0)

    @pl.when(block == 0)
    def _():
        small[...] = jnp.zeros_like(small)

    span = pl.ds(pl.multiple_of(block * ROWS, ROWS), ROWS)
    here = [r.at[span] for r in (gffn, gpre, gattn, gmixed)]
    ffn_back_block(
        seq, block, lens, copies[:2], grow, unit1, unit2, scale, slope, gains, *here[:3], small, down, up
    )
    attention_back_block(
        copies[2:4], here[2], context, qkv, probs, here[3], gtokens, small, out_proj, in_proj
    )
    last = gffn.shape[0] // ROWS - 1
    for copy in copies[4:]:
        ready(copy, last)

    @pl.when(block == last)
    def _():
        operands = (x, gmixed, contexts, gattn, middle, gpre, act, gffn)
        weight_grad_kernel(streams, places, spots, *operands, send, keep)


def encoder_back(lens, spots, grow, x, kept, params, seq, streams, devices):
    qkv, probs, context, unit1, unit2, scale, middle, act, slope = kept
    in_proj, _, out_proj, _, gains, _, up, _, down = params
    tokens, width = context.shape
    blocks, groups, inner = tokens // ROWS, ROWS // seq, up.shape[1]
    places, tall = segments(streams, devices)
    sds = jax.ShapeDtypeStruct
    half = (len(streams), devices // 2, tall, PIECE)
    half_spec = pl.BlockSpec(half, lambda i, *_: (0, 0, 0, 0), pipeline_mode=pl.Buffered(1))
    far = (down, up, out_proj, in_proj, x, context, middle, act)
    return pl.pallas_call(
        partial(encoder_back_kernel, seq, streams, places),
        grid_spec=pltpu.PrefetchScalarGridSpec(
            num_scalar_prefetch=2,
            grid=(blocks,),
            in_specs=[
                pl.BlockSpec((1, groups, width), lambda i, *_: (i, 0, 0)),
                rows(width),
                rows(width),
                rows(128),
                rows(inner),
                full(gains),
                rows(width),
                rows(3 * width),
                pl.BlockSpec((1, *probs.shape[1:]), lambda i, *_: (i, 0, 0, 0)),
                *[FAR] * len(far),
            ],
            out_specs=[rows(width), pl.BlockSpec((16, width), lambda i, *_: (0, 0)), half_spec, half_spec],
            scratch_shapes=[
                *room(*far)[:-1],
                pltpu.VMEM((tokens, width), BF16),
                pltpu.VMEM((tokens, inner), BF16),
                pltpu.VMEM((tokens, width), BF16),
                pltpu.VMEM((tokens, 3 * width), BF16),
                room(*far)[-1],
            ],
        ),
        out_shape=[sds((tokens, width), BF16), sds((16, width), F32), sds(half, BF16), sds(half, BF16)],
        compiler_params=pltpu.CompilerParams(vmem_limit_bytes=LARGE_VMEM_BYTES),
        cost_estimate=cost(18),
        name="encoder_backward",
    )(
        lens, spots, grow.reshape(blocks, groups, width), unit1, unit2, scale, slope, gains, context, qkv, probs, *far
    )


PARTS = 4


def place_kernel(outputs, spots, *refs):
    inputs, outs = refs[:2], refs[-len(outputs) :]
    group = inputs[0].shape[1]
    for out, blocks in zip(outs, outputs):
        for k, (stream, (top, tall, columns), column) in enumerate(blocks):
            inner = spots[1 + stream] & (group - 1)
            for b in range(out.shape[0] // tall):
                piece = inputs[stream][0, (b * columns + column) ^ inner, top : top + tall]
                out[b * tall : (b + 1) * tall, k * PIECE : (k + 1) * PIECE] = piece.astype(F32)


def place(half, side, spots, streams, outputs, devices, arrays=()):
    _, pieces, rows_of, _ = half.shape
    group = pieces // PARTS
    places, _ = segments(streams, devices)

    def piece_spec(stream):
        return pl.BlockSpec(
            (1, group, rows_of, PIECE), lambda g, spots: (stream, g ^ spots[3 + stream], 0, 0)
        )

    return pl.pallas_call(
        partial(
            place_kernel,
            [[(stream, places[stream][part], column) for stream, part, column in b] for _, b in outputs],
        ),
        grid_spec=pltpu.PrefetchScalarGridSpec(
            num_scalar_prefetch=1,
            grid=(PARTS,),
            in_specs=[piece_spec(0), piece_spec(1), *[KEPT] * len(arrays)],
            out_specs=[
                pl.BlockSpec(
                    (height // (2 * PARTS), PIECE * len(b)),
                    lambda g, spots: ((spots[0] ^ side) * PARTS + g, 0),
                )
                for height, b in outputs
            ],
        ),
        out_shape=[jax.ShapeDtypeStruct((height, PIECE * len(b)), F32) for height, b in outputs],
        input_output_aliases={3 + i: i for i in range(len(arrays))},
        compiler_params=pltpu.CompilerParams(vmem_limit_bytes=VMEM_BYTES),
        cost_estimate=cost(3),
        name="place_gradient",
    )(spots, half, half, *arrays)


def swap(array, mask, devices):
    return lax.ppermute(array, "dp", [(i, i ^ mask) for i in range(devices)])


def add(*terms):
    total = terms[0].astype(F32)
    for t in terms[1:]:
        total = total + t.astype(F32)
    return total.astype(BF16)


def sum_pieces(send, keep, devices):
    layout = axis_layout(devices)
    (got,) = yield [(send, 1)]
    held = [[keep[i], got[i]] for i in range(len(ORDERS))]
    for level in range(2):
        parts = []
        for terms, order in zip(held, ORDERS):
            ways = 1 << layout[order[level]][1]
            size = terms[0].shape[0] // ways
            parts.append([add(*[t[m * size : (m + 1) * size] for t in terms]) for m in range(ways)])
        got = yield [
            (p, m << layout[order[level]][0])
            for stream, order in zip(parts, ORDERS)
            for m, p in enumerate(stream)
            if m
        ]
        held = []
        for stream in parts:
            held.append([stream[0], *got[: len(stream) - 1]])
            got = got[len(stream) - 1 :]
    start, count = layout["z"]
    ways = 1 << count
    size = held[0][0].shape[0] // ways
    both = [
        jnp.stack([add(*[t[m * size : (m + 1) * size] for t in terms]) for terms in held])
        for m in range(ways)
    ]
    got = yield [(b, m << start) for m, b in enumerate(both) if m]
    total = add(both[0], *got)
    got = yield [(total, m << start) for m in range(1, ways)]
    every = jnp.concatenate([total, *got], 1)
    done = [every[i] for i in range(len(ORDERS))]
    for level in (1, 0):
        sends = []
        for mine, order in zip(done, ORDERS):
            start, count = layout[order[level]]
            sends.append([(mine, m << start) for m in range(1, 1 << count)])
        got = yield [s for stream in sends for s in stream]
        grown = []
        for mine, stream in zip(done, sends):
            grown.append(jnp.concatenate([mine, *got[: len(stream)]], 0))
            got = got[len(stream) :]
        done = grown
    mine = jnp.stack(done)
    (other,) = yield [(mine, 1)]
    return mine, other


def sum_small(array, devices):
    for bit in range(devices.bit_length() - 1):
        (got,) = yield [(array, 1 << bit)]
        array = array + got
    return array


class Line:
    def __init__(self, devices):
        self.devices = devices
        self.running = {}
        self.done = {}

    def add(self, name, steps):
        self.running[name] = (steps, next(steps))

    def step(self, names, kernel=None, operand=None, again=""):
        names = [n for n in names if n in self.running]
        sends = [self.running[n][1] for n in names]
        arrays = [[a for a, _ in s] for s in sends]
        arrays, operand = lax.optimization_barrier((arrays, operand))
        got = [[swap(a, m, self.devices) for a, (_, m) in zip(x, s)] for x, s in zip(arrays, sends)]
        result = kernel(operand) if kernel else None
        for i, n in enumerate(names):
            if n in again:
                steps = self.running[n][0]
                sends = steps.send(got[i])
                self.running[n] = (steps, sends)
                arrays = lax.optimization_barrier([a for a, _ in sends])
                got[i] = [swap(a, m, self.devices) for a, (_, m) in zip(arrays, sends)]
        got, result = lax.optimization_barrier((got, result))
        for n, g in zip(names, got):
            steps, _ = self.running.pop(n)
            try:
                self.running[n] = (steps, steps.send(g))
            except StopIteration as end:
                self.done[n] = end.value
        return result


def gather_stages(devices):
    (x, nx), (y, ny), (z, nz) = (axis_layout(devices)[a] for a in "xyz")
    plane = [(x, nx + ny)] if nx + ny < 3 else [(y, ny), (x, nx)]
    return [(z, nz), *plane, (0, 1)]


def gather_units(own, devices):
    every, masks = own[None], [0]
    for start, count in gather_stages(devices):
        steps = [m << start for m in range(1 << count)]
        every = jnp.concatenate([every] + [swap(every, m, devices) for m in steps[1:]], 0)
        masks = [k ^ m for m in steps for k in masks]
    return every, masks


def on_device(devices, *args):
    (question_tokens, passage_tokens, question_lengths, passage_lengths, positives), weights = args[:5], args[5:]
    question_params, passage_params = weights[:9], weights[9:]
    me = lax.axis_index("dp").astype(jnp.int32)
    chips = [chip_number(me, devices, order) for order in ORDERS]
    group = devices // 8
    spots = jnp.stack([me & 1, *chips, *[c // group for c in chips]])
    questions, question_seq, width = question_tokens.shape
    passages, passage_seq, _ = passage_tokens.shape

    q_fwd, p_fwd = forward(
        [
            (question_tokens, question_lengths, question_params),
            (passage_tokens, passage_lengths, passage_params),
        ]
    )
    q_summed = q_fwd[1].reshape(questions, width)
    p_summed = p_fwd[1].reshape(passages, width)
    per_device = -(-(questions + passages) // 16) * 16
    spare = per_device - questions - passages
    summed = jnp.concatenate([q_summed, p_summed, jnp.zeros((spare, width), F32)], 0)
    units = (summed * lax.rsqrt(jnp.mean(summed * summed, -1, keepdims=True) + EPS)).astype(BF16)
    code = jnp.pad(
        jnp.stack([positives // 256, positives % 256], 1).astype(BF16),
        ((0, per_device - questions), (0, 126)),
    )
    every, masks = gather_units(jnp.concatenate([units, code], 1), devices)
    lens = jnp.concatenate([question_lengths, passage_lengths, jnp.ones((spare,), jnp.int32)])
    lens = jnp.broadcast_to(lens.astype(F32)[:, None], (per_device, 128))
    loss, grow = match_loss(every, masks, me[None], summed, lens, questions, passages)

    _, _, p_qkv, p_probs, p_context, *p_norm, p_middle, p_act, p_slope = p_fwd
    inner = p_act.shape[1]
    x_p, x_q = passage_tokens.reshape(-1, width), question_tokens.reshape(-1, width)

    p_blocks = x_p.shape[0] // ROWS
    p_ahead = -(-p_blocks * 3 // 5)

    def ffn_p(part, first, count, before):
        return ffn_back(
            passage_lengths, part, (*p_norm, p_slope), passage_params, passage_seq, first, count, before
        )

    def attention_p(gattn, small, first, count, arrays=()):
        return attention_back(gattn, p_context, p_qkv, p_probs, small, passage_params, first, count, arrays)

    ffn_parts = [(width, [(4, 5, 0, inner)])], [(inner, [(6, 7, 0, width)])]
    attention_parts = (
        [(width, [(0, 1, 0, 2 * width)])],
        [(width, [(0, 1, 2 * width, width), (2, 3, 0, width)])],
    )
    all_parts = [f + a for f, a in zip(ffn_parts, attention_parts)]
    ffn_outputs = [(width, [(0, 0, c) for c in range(inner // PIECE)]), (inner, [(1, 0, 0)])]

    def attention_outputs(part):
        return [(width, [(0, part, 0), (0, part, 1), (1, part, 0)]), (width, [(1, part, 1)])]

    def grads(x, gmixed, context, gattn, middle, gpre, act, gffn, parts, micros):
        operands = [x, gmixed, context, gattn, middle, gpre, act, gffn]
        used = sorted({k for stream in parts for _, terms in stream for x, g, *_ in terms for k in (x, g)})
        parts = [
            [(h, [(used.index(x), used.index(g), *cols) for x, g, *cols in terms]) for h, terms in stream]
            for stream in parts
        ]
        return weight_grad([operands[k] for k in used], parts, spots, devices, micros)

    line = Line(devices)
    q_grad, q_small, *halves = encoder_back(
        question_lengths, spots, grow[:questions], x_q, q_fwd[2:], question_params, question_seq, all_parts, devices
    )
    line.add("q", sum_pieces(*halves, devices))
    p_grow = grow[questions : questions + passages]
    none = jnp.zeros((16, width), F32)
    p_begun = line.step("q", lambda g: ffn_p(g, 0, p_ahead, [none]), p_grow)

    def second(begun):
        gffn, gpre, gattn, small = ffn_p(p_grow, p_ahead, p_blocks - p_ahead, begun)
        halves = grads(None, None, None, None, p_middle, gpre, p_act, gffn, ffn_parts, 11)
        return gattn, small, halves

    p_attn, p_small, halves = line.step("q", second, p_begun)
    line.add("p", sum_pieces(*halves, devices))
    p_mixed, p_grad, p_small = line.step("qp", lambda g: attention_p(g, p_small, 0, p_ahead), p_attn)

    def fourth(begun):
        gmixed, gtokens, small = attention_p(
            p_attn, begun[2], p_ahead, p_blocks - p_ahead, begun[:2]
        )
        halves = grads(x_p, gmixed, p_context, p_attn, None, None, None, None, attention_parts, 5)
        return gtokens, small, halves

    p_grad, p_small, halves = line.step("qp", fourth, (p_mixed, p_grad, p_small))
    line.add("a", sum_pieces(*halves, devices))
    line.add("s", sum_small(jnp.stack([q_small, p_small]), devices))
    line.step("qpas", again="a")
    line.step("qpas")
    line.step("qpas")

    def put(streams, outputs, part=None):
        def kernel(half):
            if part is None:
                return place(half, 0, spots, streams, outputs, devices)
            return place(half, 1, spots, streams, outputs, devices, part)

        return kernel

    def own(name):
        return line.running[name][1][0][0]

    q_outputs = ffn_outputs + attention_outputs(1)
    q_outs = line.step("qpas", put(all_parts, q_outputs), own("q"))
    q_outs = line.step("pas", put(all_parts, q_outputs, q_outs), line.done["q"][1], again="a")

    def last(halves):
        return (
            place(halves[0], 0, spots, ffn_parts, ffn_outputs, devices),
            place(halves[1], 0, spots, attention_parts, attention_outputs(0), devices),
        )

    p_outs, a_outs = line.step("pas", last, (own("p"), own("a")))
    while line.running:
        line.step("s")
    p_outs = place(line.done["p"][1], 1, spots, ffn_parts, ffn_outputs, devices, p_outs)
    p_in, p_out = place(
        line.done["a"][1], 1, spots, attention_parts, attention_outputs(0), devices, a_outs
    )
    q_up, q_down, q_in, q_out = q_outs
    p_up, p_down = p_outs
    small = line.done["s"]

    def outputs(small, gin, gout, gup, gdown):
        return (
            gin,
            small[0:2],
            gout,
            small[2:4],
            small[4:6],
            small[6:8],
            gup,
            small[8 : 8 + inner // width].reshape(inner),
            gdown,
        )

    return (
        loss[0, 0],
        q_fwd[0].reshape(question_tokens.shape),
        p_fwd[0].reshape(passage_tokens.shape),
        q_grad.reshape(question_tokens.shape),
        p_grad.reshape(passage_tokens.shape),
        *outputs(small[0], q_in, q_out, q_up, q_down),
        *outputs(small[1], p_in, p_out, p_up, p_down),
    )


def solution(mesh):
    batch = P("dp", None, None)
    return jax.shard_map(
        partial(on_device, mesh.shape["dp"]),
        mesh=mesh,
        in_specs=(batch, batch, P("dp"), P("dp"), P("dp"), *[P()] * 18),
        out_specs=(P(), batch, batch, batch, batch, *[P()] * 18),
        check_vma=False,
    )
```

```python
import math
from functools import partial

import jax
import jax.numpy as jnp
from jax import lax
from jax.experimental import pallas as pl
from jax.experimental.pallas import tpu as pltpu
from jax.sharding import PartitionSpec as P

HEAD = 64
ROWS = 256
SHARPNESS = 20.0
NEG = -1e30
EPS = 1e-06
F32 = jnp.float32
BF16 = jnp.bfloat16
VMEM_BYTES = 48 * 1024 * 1024
LARGE_VMEM_BYTES = 60 * 1024 * 1024

DENSITY = 1.0 / math.sqrt(2.0 * math.pi)


def nn(a, b):
    return lax.dot_general(a, b, (((1,), (0,)), ((), ())), preferred_element_type=F32)


def nt(a, b):
    return lax.dot_general(a, b, (((1,), (1,)), ((), ())), preferred_element_type=F32)


def tn(a, b):
    return lax.dot_general(a, b, (((0,), (0,)), ((), ())), preferred_element_type=F32)


def gelu_pair(v):
    cdf = 0.5 + 0.5 * lax.erf(v * math.sqrt(0.5))
    bell = jnp.exp(v * v * -0.5)
    return v * cdf, cdf + v * (bell * DENSITY)


def layer_norm(v):
    center = v - jnp.mean(v, -1, keepdims=True)
    scale = lax.rsqrt(jnp.mean(center * center, -1, keepdims=True) + EPS)
    return center * scale, scale


def norm_back(grad, unit, scale, gain):
    t = grad * gain
    return scale * (
        t - jnp.mean(t, -1, keepdims=True) - unit * jnp.mean(t * unit, -1, keepdims=True)
    )


def fold_rows(v):
    return jnp.sum(v, 0, keepdims=True)


def cost(micros):
    return pl.CostEstimate(flops=int(micros * 1.15e9), bytes_accessed=0, transcendentals=0)


def full(array):
    zeros = (0,) * array.ndim
    return pl.BlockSpec(array.shape, lambda *_: zeros, pipeline_mode=pl.Buffered(1))


FAR = pl.BlockSpec(memory_space=pltpu.HBM)


def room(*arrays):
    return [*[pltpu.VMEM(a.shape, a.dtype) for a in arrays], pltpu.SemaphoreType.DMA((len(arrays),))]


def fetch(*pairs, arrived, now=None):
    copies = [pltpu.make_async_copy(far, near, arrived.at[i]) for i, (far, near) in enumerate(pairs)]
    begin(copies[:now])
    return copies


def begin(copies, step=0):
    @pl.when(pl.program_id(0) == step)
    def _():
        for copy in copies:
            copy.start()


def ready(copy, step=0):
    @pl.when(pl.program_id(0) == step)
    def _():
        copy.wait()


def rows(width, first=0):
    return pl.BlockSpec((ROWS, width), lambda i, *_: (i + first, 0))


KEPT = pl.BlockSpec(memory_space=pl.ANY)


def forward_kernel(seqs, counts, *refs):
    lens, refs = refs[:2], refs[2:]
    near, far, outs, held = refs[:12], refs[12:20], refs[20:42], refs[42:50]
    copies = fetch(*zip(far, held), arrived=refs[50], now=1)
    begin(copies[4:], min(1, counts[0] - 1))
    step = pl.program_id(0)
    first = 0
    for e, (seq, count) in enumerate(zip(seqs, counts)):

        @pl.when(jnp.logical_and(step >= first, step < first + count))
        def _(e=e, seq=seq, first=first):
            forward_block(
                seq,
                step - first,
                [partial(ready, copy, first) for copy in copies[4 * e : 4 * e + 4]],
                [] if e else copies[1:4],
                lens[e],
                *near[6 * e : 6 * e + 6],
                *outs[11 * e : 11 * e + 11],
                *held[4 * e : 4 * e + 4],
            )

        first += count


def forward_block(
    seq,
    block,
    wait,
    next_copies,
    lens,
    x_ref,
    in_bias,
    out_bias,
    gains,
    shifts,
    up_bias,
    out_ref,
    summed_ref,
    qkv_ref,
    probs_ref,
    context_ref,
    unit1_ref,
    unit2_ref,
    scale_ref,
    middle_ref,
    act_ref,
    slope_ref,
    in_proj,
    out_proj,
    up,
    down,
):
    groups = ROWS // seq
    width = x_ref.shape[1]
    row = lax.broadcasted_iota(jnp.int32, (ROWS, 128), 0)
    lane = lax.broadcasted_iota(jnp.int32, (ROWS, 128), 1)
    slot = lane % HEAD
    low_half = lane < HEAD
    group = row // seq
    limit = jnp.zeros((ROWS, 128), jnp.int32)
    for g in range(groups):
        limit = jnp.where(group == g, lens[block * groups + g], limit)
    live = (row - group * seq) < limit
    query_mark = jnp.where(slot == group, 1.0, 0.0).astype(BF16)
    key_mark = jnp.where(
        slot < groups, jnp.where(jnp.logical_and(slot == group, live), 0.0, NEG), 0.0
    ).astype(BF16)
    x = x_ref[...]
    wait[0]()
    begin(next_copies)
    mixed = nn(x, in_proj[...])
    query = ((mixed[:, :width] + in_bias[0:1]).astype(BF16) * (HEAD**-0.5)).astype(BF16)
    key = mixed[:, width : 2 * width].astype(BF16)
    value = (mixed[:, 2 * width :] + in_bias[1:2]).astype(BF16)
    qkv_ref[:, :width] = query
    qkv_ref[:, width : 2 * width] = key
    qkv_ref[:, 2 * width :] = value
    pairs = []
    for p in range(width // 128):
        cols = slice(128 * p, 128 * p + 128)
        total = None
        for h in range(2):
            mine = low_half if h == 0 else jnp.logical_not(low_half)
            query_h = jnp.where(mine, query[:, cols], query_mark)
            key_h = jnp.where(mine, key[:, cols], key_mark)
            value_h = jnp.where(mine, value[:, cols], jnp.zeros_like(key_mark))
            scores = nt(key_h, query_h)
            top = jnp.max(scores, 0, keepdims=True)
            weight = jnp.exp(scores - top)
            probs = (weight * (1.0 / jnp.sum(weight, 0, keepdims=True))).astype(BF16)
            probs_ref[0, 2 * p + h] = probs
            part = tn(probs, value_h)
            total = part if total is None else total + part
        pairs.append(total.astype(BF16))
    context = jnp.concatenate(pairs, 1)
    context_ref[...] = context
    wait[1]()
    first = x.astype(F32) + nn(context, out_proj[...]) + out_bias[0:1]
    unit1, scale1 = layer_norm(first)
    unit1_ref[...] = unit1.astype(BF16)
    middle_full = unit1 * gains[0:1] + shifts[0:1]
    middle = middle_full.astype(BF16)
    middle_ref[...] = middle
    second = middle_full + out_bias[1:2]
    wait[2]()
    wait[3]()
    chunk = 256
    for c in range(up.shape[1] // chunk):
        cols = slice(chunk * c, chunk * c + chunk)
        pre = nn(middle, up[:, cols]) + up_bias[:, cols]
        act, slope = gelu_pair(pre)
        act = act.astype(BF16)
        act_ref[:, cols] = act
        slope_ref[:, cols] = slope.astype(BF16)
        second += nn(act, down[cols, :])
    unit2, scale2 = layer_norm(second)
    unit2_ref[...] = unit2.astype(BF16)
    scale_ref[...] = jnp.where(lane == 0, scale1, scale2)
    out = unit2 * gains[1:2] + shifts[1:2]
    out_ref[...] = out.astype(BF16)
    kept = jnp.where(live[:, :1], out, 0.0)
    for g in range(groups):
        length = lens[block * groups + g].astype(F32)
        summed_ref[0, g : g + 1] = fold_rows(kept[g * seq : (g + 1) * seq]) / length


def forward(encoders):
    sds = jax.ShapeDtypeStruct
    lens, near, near_specs, far, out_specs, out_shape, seqs, counts = [], [], [], [], [], [], [], []
    first = 0
    for x, length, params in encoders:
        in_proj, in_bias, out_proj, out_bias, gains, shifts, up, up_bias, down = params
        examples, seq, width = x.shape
        tokens = examples * seq
        blocks, groups, heads = tokens // ROWS, ROWS // seq, width // HEAD
        inner = up.shape[1]

        def block(*shape, first=first, blocks=blocks):
            rest = (0,) * (len(shape) - 1)
            return pl.BlockSpec(shape, lambda i, *_: (jnp.clip(i - first, 0, blocks - 1), *rest))

        small = (in_bias, out_bias, gains, shifts, up_bias[None])
        lens.append(length)
        near += [x.reshape(tokens, width), *small]
        near_specs += [block(ROWS, width), *[full(w) for w in small]]
        far += [in_proj, out_proj, up, down]
        shapes = [
            ((tokens, width), BF16),
            ((blocks, groups, width), F32),
            ((tokens, 3 * width), BF16),
            ((blocks, heads, ROWS, ROWS), BF16),
            ((tokens, width), BF16),
            ((tokens, width), BF16),
            ((tokens, width), BF16),
            ((tokens, 128), F32),
            ((tokens, width), BF16),
            ((tokens, inner), BF16),
            ((tokens, inner), BF16),
        ]
        for shape, kind in shapes:
            out_specs.append(block(1 if shape[0] == blocks else ROWS, *shape[1:]))
            out_shape.append(sds(shape, kind))
        seqs.append(seq)
        counts.append(blocks)
        first += blocks
    outs = pl.pallas_call(
        partial(forward_kernel, seqs, counts),
        grid_spec=pltpu.PrefetchScalarGridSpec(
            num_scalar_prefetch=2,
            grid=(first,),
            in_specs=[*near_specs, *[FAR] * len(far)],
            out_specs=out_specs,
            scratch_shapes=room(*far),
        ),
        out_shape=out_shape,
        compiler_params=pltpu.CompilerParams(vmem_limit_bytes=LARGE_VMEM_BYTES),
        cost_estimate=cost(40),
        name="layer_forward",
    )(*lens, *near, *far)
    return outs[:11], outs[11:]


def ffn_back_kernel(seq, first, lens, *refs):
    near, (down_far, up_far, before), refs = refs[:6], refs[6:9], refs[9:]
    outs, (down, up, arrived) = refs[-7:-3], refs[-3:]
    copies = fetch((down_far, down), (up_far, up), arrived=arrived)

    @pl.when(pl.program_id(0) == 0)
    def _():
        outs[3][...] = before[...]

    ffn_back_block(seq, first + pl.program_id(0), lens, copies, [], *near, *outs, down, up)


def ffn_back_block(
    seq,
    block,
    lens,
    copies,
    next_copies,
    grow_ref,
    unit1_ref,
    unit2_ref,
    scale_ref,
    slope_ref,
    gains,
    gffn_ref,
    gpre_ref,
    gattn_ref,
    small_ref,
    down,
    up,
):
    groups = ROWS // seq
    width = unit1_ref.shape[1]
    row = lax.broadcasted_iota(jnp.int32, (seq, width), 0)
    grad_out = jnp.concatenate(
        [
            jnp.where(row < lens[block * groups + g], grow_ref[0, g : g + 1], 0.0)
            for g in range(groups)
        ],
        0,
    )
    unit2 = unit2_ref[...].astype(F32)
    small_ref[7:8] += fold_rows(grad_out)
    small_ref[5:6] += fold_rows(grad_out * unit2)
    gsecond = norm_back(grad_out, unit2, scale_ref[:, 1:2], gains[1:2])
    gffn = gsecond.astype(BF16)
    gffn_ref[...] = gffn
    small_ref[3:4] += fold_rows(gffn.astype(F32))
    gmiddle = gsecond
    ready(copies[0])
    chunk = 256
    for c in range(up.shape[1] // chunk):
        cols = slice(chunk * c, chunk * c + chunk)
        gpre = (nt(gffn, down[cols, :]) * slope_ref[:, cols].astype(F32)).astype(BF16)
        gpre_ref[:, cols] = gpre
        line, left = 8 + chunk * c // width, chunk * c % width
        small_ref[line : line + 1, left : left + chunk] += fold_rows(gpre.astype(F32))
        if c == 0:
            ready(copies[1])
            begin(next_copies)
        gmiddle += nt(gpre, up[:, cols])
    unit1 = unit1_ref[...].astype(F32)
    small_ref[6:7] += fold_rows(gmiddle)
    small_ref[4:5] += fold_rows(gmiddle * unit1)
    gfirst = norm_back(gmiddle, unit1, scale_ref[:, 0:1], gains[0:1])
    gattn = gfirst.astype(BF16)
    gattn_ref[...] = gattn
    small_ref[2:3] += fold_rows(gattn.astype(F32))


def ffn_back(lens, grow, kept, params, seq, first, count, before):
    unit1, unit2, scale, slope = kept
    _, _, _, _, gains, _, up, _, down = params
    tokens, width = unit1.shape
    blocks, groups, inner = tokens // ROWS, ROWS // seq, up.shape[1]
    *arrays, small = before
    sds = jax.ShapeDtypeStruct
    return pl.pallas_call(
        partial(ffn_back_kernel, seq, first),
        grid_spec=pltpu.PrefetchScalarGridSpec(
            num_scalar_prefetch=1,
            grid=(count,),
            in_specs=[
                pl.BlockSpec((1, groups, width), lambda i, *_: (i + first, 0, 0)),
                rows(width, first),
                rows(width, first),
                rows(128, first),
                rows(inner, first),
                full(gains),
                FAR,
                FAR,
                full(small),
                *[KEPT] * len(arrays),
            ],
            out_specs=[
                rows(width, first),
                rows(inner, first),
                rows(width, first),
                pl.BlockSpec((16, width), lambda i, *_: (0, 0)),
            ],
            scratch_shapes=room(down, up),
        ),
        out_shape=[
            sds((tokens, width), BF16),
            sds((tokens, inner), BF16),
            sds((tokens, width), BF16),
            sds((16, width), F32),
        ],
        input_output_aliases={10 + i: i for i in range(len(arrays))},
        compiler_params=pltpu.CompilerParams(vmem_limit_bytes=VMEM_BYTES),
        cost_estimate=cost(count * ROWS / 80),
        name="ffn_backward",
    )(
        lens, grow.reshape(blocks, groups, width), unit1, unit2, scale, slope, gains, down, up, small, *arrays
    )


def attention_back_kernel(*refs):
    near, before_ref, (out_proj_far, in_proj_far), refs = refs[:4], refs[4], refs[5:7], refs[7:]
    outs, (out_proj, in_proj, arrived) = refs[-6:-3], refs[-3:]
    copies = fetch((out_proj_far, out_proj), (in_proj_far, in_proj), arrived=arrived)

    @pl.when(pl.program_id(0) == 0)
    def _():
        outs[2][...] = before_ref[...]

    attention_back_block(copies, *near, *outs, out_proj, in_proj)


def attention_back_block(
    copies,
    gattn_ref,
    context_ref,
    qkv_ref,
    probs_ref,
    gmixed_ref,
    gtokens_ref,
    small_ref,
    out_proj,
    in_proj,
):
    width = gattn_ref.shape[1]
    lane = lax.broadcasted_iota(jnp.int32, (ROWS, 128), 1)
    low_half = lane < HEAD
    blank = jnp.zeros((ROWS, 128), BF16)
    gattn = gattn_ref[...]
    ready(copies[0])
    gcontext = nt(gattn, out_proj[...]).astype(BF16)
    heads = width // HEAD
    member = (
        lax.broadcasted_iota(jnp.int32, (16, width), 1) // HEAD
        == lax.broadcasted_iota(jnp.int32, (16, width), 0)
    )
    member = jnp.where(member, 1.0, 0.0).astype(BF16)
    product = gcontext.astype(F32) * context_ref[...].astype(F32)
    coarse = product.astype(BF16)
    fine = (product - coarse.astype(F32)).astype(BF16)
    offsets = nt(member, coarse) + nt(member, fine)
    for p in range(width // 128):
        cols = slice(128 * p, 128 * p + 128)
        kcols = slice(width + 128 * p, width + 128 * p + 128)
        vcols = slice(2 * width + 128 * p, 2 * width + 128 * p + 128)
        query, key, value = qkv_ref[:, cols], qkv_ref[:, kcols], qkv_ref[:, vcols]
        gquery = gkey = gvalue = None
        for h in range(2):
            mine = low_half if h == 0 else jnp.logical_not(low_half)
            gcontext_h = jnp.where(mine, gcontext[:, cols], blank)
            probs = probs_ref[0, 2 * p + h]
            gprobs = nt(value, gcontext_h)
            head = 2 * p + h
            gscores = (probs.astype(F32) * (gprobs - offsets[head : head + 1])).astype(BF16)
            parts = (
                tn(gscores, jnp.where(mine, key, blank)),
                nn(gscores, jnp.where(mine, query, blank)),
                nn(probs, gcontext_h),
            )
            if h == 0:
                gquery, gkey, gvalue = parts
            else:
                gquery, gkey, gvalue = gquery + parts[0], gkey + parts[1], gvalue + parts[2]
        gquery = (gquery * (HEAD**-0.5)).astype(BF16)
        gmixed_ref[:, cols] = gquery
        gmixed_ref[:, kcols] = gkey.astype(BF16)
        gvalue = gvalue.astype(BF16)
        gmixed_ref[:, vcols] = gvalue
        small_ref[0:1, cols] += fold_rows(gquery.astype(F32))
        small_ref[1:2, cols] += fold_rows(gvalue.astype(F32))
    ready(copies[1])
    gtokens_ref[...] = (gattn.astype(F32) + nt(gmixed_ref[...], in_proj[...])).astype(BF16)


def attention_back(gattn, context, qkv, probs, small, params, first, count, arrays=()):
    in_proj, out_proj = params[0], params[2]
    tokens, width = context.shape
    sds = jax.ShapeDtypeStruct
    return pl.pallas_call(
        attention_back_kernel,
        grid=(count,),
        in_specs=[
            rows(width, first),
            rows(width, first),
            rows(3 * width, first),
            pl.BlockSpec((1, *probs.shape[1:]), lambda i: (i + first, 0, 0, 0)),
            full(small),
            FAR,
            FAR,
            *[KEPT] * len(arrays),
        ],
        out_specs=[
            rows(3 * width, first),
            rows(width, first),
            pl.BlockSpec(small.shape, lambda i: (0, 0)),
        ],
        out_shape=[
            sds((tokens, 3 * width), BF16),
            sds((tokens, width), BF16),
            sds(small.shape, F32),
        ],
        scratch_shapes=room(out_proj, in_proj),
        input_output_aliases={7 + i: i for i in range(len(arrays))},
        compiler_params=pltpu.CompilerParams(vmem_limit_bytes=VMEM_BYTES),
        cost_estimate=cost(count * ROWS / 70),
        name="attention_backward",
    )(gattn, context, qkv, probs, small, out_proj, in_proj, *arrays)


def match_kernel(masks, questions, passages, blocks_ref, spot, summed_ref, lens_ref, loss_ref, grow_ref, units_ref):
    per_device, width = summed_ref.shape
    for k, mask in enumerate(masks):
        lead = pl.multiple_of((spot[0] ^ mask) * per_device, per_device)
        units_ref[pl.ds(lead, per_device), :] = blocks_ref[k]
    every = units_ref[...]
    count = every.shape[0]
    units = every[:, :width]
    scale = SHARPNESS / width
    ri = lax.broadcasted_iota(jnp.int32, (count, count), 0)
    ci = lax.broadcasted_iota(jnp.int32, (count, count), 1)
    pick = jnp.where(
        lax.broadcasted_iota(jnp.int32, (8, 128), 0) == lax.broadcasted_iota(jnp.int32, (8, 128), 1), 1.0, 0.0
    ).astype(BF16)
    digits = nt(pick, every[:, width:])
    positive = (digits[0:1] * 256.0 + digits[1:2]).astype(jnp.int32)
    place = (positive // passages) * per_device + questions + positive % passages
    rlocal = ri % per_device
    is_passage = jnp.logical_and(rlocal >= questions, rlocal < questions + passages)
    is_question = (ci[0:1] % per_device) < questions
    match = nt(units, units) * scale
    shown = jnp.where(is_passage, match, NEG)
    top = jnp.max(shown, 0, keepdims=True)
    total = jnp.sum(jnp.exp(shown - top), 0, keepdims=True)
    logsum = top + jnp.log(total)
    hit = ri == place
    chosen = jnp.sum(jnp.where(hit, match, 0.0), 0, keepdims=True)
    loss_ref[...] = jnp.sum(jnp.where(is_question, logsum - chosen, 0.0), 1, keepdims=True)

    first = spot[0] * per_device
    own = blocks_ref[0]
    own_units = own[:, :width]
    rown = lax.broadcasted_iota(jnp.int32, (per_device, count), 0)
    cown = lax.broadcasted_iota(jnp.int32, (per_device, count), 1)
    match_own = nt(own_units, units) * scale
    hit_p = jnp.logical_and(place == first + rown, is_question)
    share_p = jnp.exp(match_own - logsum) - jnp.where(hit_p, 1.0, 0.0)
    share_p = jnp.where(is_question, share_p, 0.0)
    clocal = cown % per_device
    col_passage = jnp.logical_and(clocal >= questions, clocal < questions + passages)
    shown_q = jnp.where(col_passage, match_own, NEG)
    weight_q = jnp.exp(shown_q - jnp.max(shown_q, 1, keepdims=True))
    code = own[:, width:].astype(F32)
    positive_q = (code[:, 0:1] * 256.0 + code[:, 1:2]).astype(jnp.int32)
    place_q = (positive_q // passages) * per_device + questions + positive_q % passages
    share_q = weight_q / jnp.sum(weight_q, 1, keepdims=True) - jnp.where(cown == place_q, 1.0, 0.0)
    share = jnp.where(rown < questions, share_q, share_p).astype(BF16)
    gunit = nn(share, units) * scale
    summed = summed_ref[...]
    r = lax.rsqrt(jnp.mean(summed * summed, -1, keepdims=True) + EPS)
    gsummed = r * gunit - (r * r * r) * summed * jnp.mean(gunit * summed, -1, keepdims=True)
    grow_ref[...] = gsummed / lens_ref[:, 0:1]


def match_loss(blocks, masks, spot, summed, lens, questions, passages):
    count, per_device, wide = blocks.shape
    vmem = pl.BlockSpec(memory_space=pltpu.VMEM)
    return pl.pallas_call(
        partial(match_kernel, masks, questions, passages),
        in_specs=[vmem, pl.BlockSpec(memory_space=pltpu.SMEM), vmem, vmem],
        out_specs=[vmem, vmem],
        out_shape=[
            jax.ShapeDtypeStruct((1, 1), F32),
            jax.ShapeDtypeStruct(summed.shape, F32),
        ],
        scratch_shapes=[pltpu.VMEM((count * per_device, wide), BF16)],
        compiler_params=pltpu.CompilerParams(vmem_limit_bytes=VMEM_BYTES),
        cost_estimate=cost(3),
        name="match_loss",
    )(blocks, spot, summed, lens)


ORDERS = ("xyz", "yxz")
PIECE = 512


def axis_layout(devices):
    bits = devices.bit_length() - 2
    x = bits // 3
    y = (bits - x) // 2
    return {"x": (1, x), "y": (1 + x, y), "z": (1 + x + y, bits - x - y)}


def chip_number(me, devices, order):
    layout = axis_layout(devices)
    number = jnp.zeros((), jnp.int32)
    for axis in order:
        start, count = layout[axis]
        number = (number << count) | ((me >> start) & ((1 << count) - 1))
    return number


def segments(streams, devices):
    found = []
    for stream in streams:
        rows_of, start = [], 0
        for height, terms in stream:
            columns = sum(n for *_, n in terms) // PIECE
            tall = height * columns // devices
            rows_of.append((start, tall, columns))
            start += -(-tall // 16) * 16
        found.append(rows_of)
    return found, start


def weight_grad_kernel(streams, places, spots, *refs):
    *operands, send_ref, keep_ref = refs
    for side, out in enumerate((send_ref, keep_ref)):
        for stream, parts in enumerate(streams):
            for (height, terms), (top, tall, columns) in zip(parts, places[stream]):
                column = 0
                half = height // 2
                step = min(half, 256)
                for x, g, first, n in terms:
                    for s in range(half // step):
                        lead = pl.multiple_of((spots[0] ^ (1 - side)) * half + s * step, step)
                        tile = tn(
                            operands[x][:, pl.ds(lead, step)], operands[g][:, first : first + n]
                        ).astype(BF16)
                        for b in range(step // tall):
                            for c in range(n // PIECE):
                                number = (s * (step // tall) + b) * columns + column + c
                                out[stream, number ^ spots[1 + stream], top : top + tall] = tile[
                                    b * tall : (b + 1) * tall, c * PIECE : (c + 1) * PIECE
                                ]
                    column += n // PIECE


def weight_grad(operands, streams, spots, devices, micros):
    places, tall = segments(streams, devices)
    vmem = pl.BlockSpec(memory_space=pltpu.VMEM)
    out = jax.ShapeDtypeStruct((len(streams), devices // 2, tall, PIECE), BF16)
    return pl.pallas_call(
        partial(weight_grad_kernel, streams, places),
        in_specs=[pl.BlockSpec(memory_space=pltpu.SMEM), *[vmem] * len(operands)],
        out_specs=[vmem, vmem],
        out_shape=[out, out],
        compiler_params=pltpu.CompilerParams(vmem_limit_bytes=VMEM_BYTES),
        cost_estimate=cost(micros),
        name="weight_gradient",
    )(spots, *operands)


def encoder_back_kernel(seq, streams, places, lens, spots, *refs):
    (grow, unit1, unit2, scale, slope, gains, context, qkv, probs), refs = refs[:9], refs[9:]
    far, (gtokens, small, send, keep), held = refs[:8], refs[8:12], refs[12:20]
    gffn, gpre, gattn, gmixed, arrived = refs[20:]
    copies = fetch(*zip(far, held), arrived=arrived, now=2)
    down, up, out_proj, in_proj, x, contexts, middle, act = held
    block = pl.program_id(0)

    @pl.when(block == 0)
    def _():
        small[...] = jnp.zeros_like(small)

    span = pl.ds(pl.multiple_of(block * ROWS, ROWS), ROWS)
    here = [r.at[span] for r in (gffn, gpre, gattn, gmixed)]
    ffn_back_block(
        seq, block, lens, copies[:2], copies[2:4], grow, unit1, unit2, scale, slope, gains, *here[:3], small, down, up
    )
    begin(copies[4:])
    attention_back_block(
        copies[2:4], here[2], context, qkv, probs, here[3], gtokens, small, out_proj, in_proj
    )
    last = gffn.shape[0] // ROWS - 1
    for copy in copies[4:]:
        ready(copy, last)

    @pl.when(block == last)
    def _():
        operands = (x, gmixed, contexts, gattn, middle, gpre, act, gffn)
        weight_grad_kernel(streams, places, spots, *operands, send, keep)


def encoder_back(lens, spots, grow, x, kept, params, seq, streams, devices):
    qkv, probs, context, unit1, unit2, scale, middle, act, slope = kept
    in_proj, _, out_proj, _, gains, _, up, _, down = params
    tokens, width = context.shape
    blocks, groups, inner = tokens // ROWS, ROWS // seq, up.shape[1]
    places, tall = segments(streams, devices)
    sds = jax.ShapeDtypeStruct
    half = (len(streams), devices // 2, tall, PIECE)
    half_spec = pl.BlockSpec(half, lambda i, *_: (0, 0, 0, 0), pipeline_mode=pl.Buffered(1))
    far = (down, up, out_proj, in_proj, x, context, middle, act)
    return pl.pallas_call(
        partial(encoder_back_kernel, seq, streams, places),
        grid_spec=pltpu.PrefetchScalarGridSpec(
            num_scalar_prefetch=2,
            grid=(blocks,),
            in_specs=[
                pl.BlockSpec((1, groups, width), lambda i, *_: (i, 0, 0)),
                rows(width),
                rows(width),
                rows(128),
                rows(inner),
                full(gains),
                rows(width),
                rows(3 * width),
                pl.BlockSpec((1, *probs.shape[1:]), lambda i, *_: (i, 0, 0, 0)),
                *[FAR] * len(far),
            ],
            out_specs=[rows(width), pl.BlockSpec((16, width), lambda i, *_: (0, 0)), half_spec, half_spec],
            scratch_shapes=[
                *room(*far)[:-1],
                pltpu.VMEM((tokens, width), BF16),
                pltpu.VMEM((tokens, inner), BF16),
                pltpu.VMEM((tokens, width), BF16),
                pltpu.VMEM((tokens, 3 * width), BF16),
                room(*far)[-1],
            ],
        ),
        out_shape=[sds((tokens, width), BF16), sds((16, width), F32), sds(half, BF16), sds(half, BF16)],
        compiler_params=pltpu.CompilerParams(vmem_limit_bytes=LARGE_VMEM_BYTES),
        cost_estimate=cost(18),
        name="encoder_backward",
    )(
        lens, spots, grow.reshape(blocks, groups, width), unit1, unit2, scale, slope, gains, context, qkv, probs, *far
    )


PARTS = 4


def place_kernel(outputs, spots, *refs):
    inputs, outs = refs, refs[-len(outputs) :]
    group = inputs[0].shape[1]
    for out, blocks in zip(outs, outputs):
        for k, (source, stream, (top, tall, columns), column) in enumerate(blocks):
            inner = spots[1 + stream] & (group - 1)
            for b in range(out.shape[0] // tall):
                piece = inputs[source][0, (b * columns + column) ^ inner, top : top + tall]
                out[b * tall : (b + 1) * tall, k * PIECE : (k + 1) * PIECE] = piece.astype(F32)


def place(halves, side, spots, layouts, devices, arrays=()):
    group = halves[0].shape[1] // PARTS
    blocks_of, heights = [], []
    for k, (streams, outputs) in enumerate(layouts):
        places, _ = segments(streams, devices)
        for height, blocks in outputs:
            blocks_of.append([(2 * k + st, st, places[st][part], column) for st, part, column in blocks])
            heights.append(height)

    def piece_spec(half, stream):
        return pl.BlockSpec(
            (1, group, half.shape[2], PIECE), lambda g, spots: (stream, g ^ spots[3 + stream], 0, 0)
        )

    count = 2 * len(halves)
    return pl.pallas_call(
        partial(place_kernel, blocks_of),
        grid_spec=pltpu.PrefetchScalarGridSpec(
            num_scalar_prefetch=1,
            grid=(PARTS,),
            in_specs=[
                *[piece_spec(half, stream) for half in halves for stream in range(2)],
                *[KEPT] * len(arrays),
            ],
            out_specs=[
                pl.BlockSpec(
                    (height // (2 * PARTS), PIECE * len(b)),
                    lambda g, spots: ((spots[0] ^ side) * PARTS + g, 0),
                )
                for height, b in zip(heights, blocks_of)
            ],
        ),
        out_shape=[
            jax.ShapeDtypeStruct((height, PIECE * len(b)), F32) for height, b in zip(heights, blocks_of)
        ],
        input_output_aliases={1 + count + i: i for i in range(len(arrays))},
        compiler_params=pltpu.CompilerParams(vmem_limit_bytes=VMEM_BYTES),
        cost_estimate=cost(3),
        name="place_gradient",
    )(spots, *[half for half in halves for _ in range(2)], *arrays)


def swap(array, mask, devices):
    return lax.ppermute(array, "dp", [(i, i ^ mask) for i in range(devices)])


def add(*terms):
    total = terms[0].astype(F32)
    for t in terms[1:]:
        total = total + t.astype(F32)
    return total.astype(BF16)


def sum_pieces(send, keep, devices, pairs=True):
    layout = axis_layout(devices)
    (got,) = yield [(send, 1)]
    held = [[keep[i], got[i]] for i in range(len(ORDERS))]
    for level in range(2):
        parts = []
        for terms, order in zip(held, ORDERS):
            ways = 1 << layout[order[level]][1]
            size = terms[0].shape[0] // ways
            parts.append([add(*[t[m * size : (m + 1) * size] for t in terms]) for m in range(ways)])
        got = yield [
            (p, m << layout[order[level]][0])
            for stream, order in zip(parts, ORDERS)
            for m, p in enumerate(stream)
            if m
        ]
        held = []
        for stream in parts:
            held.append([stream[0], *got[: len(stream) - 1]])
            got = got[len(stream) - 1 :]
    start, count = layout["z"]
    size = held[0][0].shape[0] >> count
    pieces = {
        m: jnp.stack(
            [sum(t[m * size : (m + 1) * size].astype(F32) for t in terms) for terms in held]
        )
        for m in range(1 << count)
    }
    if pairs:
        for bit in range(count):
            away = [m for m in sorted(pieces) if m >> bit & 1]
            (got,) = yield [
                (jnp.concatenate([pieces[m] for m in away], 1).astype(BF16), 1 << (start + bit))
            ]
            pieces = {
                m ^ (1 << bit): pieces[m ^ (1 << bit)] + got[:, k * size : (k + 1) * size].astype(F32)
                for k, m in enumerate(away)
            }
    else:
        got = yield [(pieces[m].astype(BF16), m << start) for m in range(1, 1 << count)]
        pieces = {0: pieces[0] + sum(g.astype(F32) for g in got)}
    pieces = {0: pieces[0].astype(BF16)}
    for bit in reversed(range(count)):
        known = sorted(pieces)
        (got,) = yield [(jnp.concatenate([pieces[m] for m in known], 1), 1 << (start + bit))]
        for k, m in enumerate(known):
            pieces[m | (1 << bit)] = got[:, k * size : (k + 1) * size]
    every = jnp.concatenate([pieces[m] for m in sorted(pieces)], 1)
    done = [every[i] for i in range(len(ORDERS))]
    for level in (1, 0):
        sends = []
        for mine, order in zip(done, ORDERS):
            start, count = layout[order[level]]
            sends.append([(mine, m << start) for m in range(1, 1 << count)])
        got = yield [s for stream in sends for s in stream]
        grown = []
        for mine, stream in zip(done, sends):
            grown.append(jnp.concatenate([mine, *got[: len(stream)]], 0))
            got = got[len(stream) :]
        done = grown
    mine = jnp.stack(done)
    (other,) = yield [(mine, 1)]
    return mine, other


def sum_small(array, devices):
    for bit in range(devices.bit_length() - 1):
        (got,) = yield [(array, 1 << bit)]
        array = array + got
    return array


class Line:
    def __init__(self, devices):
        self.devices = devices
        self.running = {}
        self.done = {}

    def add(self, name, steps):
        self.running[name] = (steps, next(steps))

    def step(self, names, kernel=None, operand=None, again=""):
        names = [n for n in names if n in self.running]
        sends = [self.running[n][1] for n in names]
        arrays = [[a for a, _ in s] for s in sends]
        arrays, operand = lax.optimization_barrier((arrays, operand))
        got = [[swap(a, m, self.devices) for a, (_, m) in zip(x, s)] for x, s in zip(arrays, sends)]
        result = kernel(operand) if kernel else None
        for i, n in enumerate(names):
            if n in again:
                steps = self.running[n][0]
                sends = steps.send(got[i])
                self.running[n] = (steps, sends)
                arrays = lax.optimization_barrier([a for a, _ in sends])
                got[i] = [swap(a, m, self.devices) for a, (_, m) in zip(arrays, sends)]
        got, result = lax.optimization_barrier((got, result))
        for n, g in zip(names, got):
            steps, _ = self.running.pop(n)
            try:
                self.running[n] = (steps, steps.send(g))
            except StopIteration as end:
                self.done[n] = end.value
        return result


def gather_stages(devices):
    (x, nx), (y, ny), (z, nz) = (axis_layout(devices)[a] for a in "xyz")
    plane = [(x, nx + ny)] if nx + ny < 3 else [(y, ny), (x, nx)]
    return [(z, nz), *plane, (0, 1)]


def gather_units(own, devices):
    every, masks = own[None], [0]
    for start, count in gather_stages(devices):
        steps = [m << start for m in range(1 << count)]
        every = jnp.concatenate([every] + [swap(every, m, devices) for m in steps[1:]], 0)
        masks = [k ^ m for m in steps for k in masks]
    return every, masks


def on_device(devices, *args):
    (question_tokens, passage_tokens, question_lengths, passage_lengths, positives), weights = args[:5], args[5:]
    question_params, passage_params = weights[:9], weights[9:]
    me = lax.axis_index("dp").astype(jnp.int32)
    chips = [chip_number(me, devices, order) for order in ORDERS]
    group = devices // 8
    spots = jnp.stack([me & 1, *chips, *[c // group for c in chips]])
    questions, question_seq, width = question_tokens.shape
    passages, passage_seq, _ = passage_tokens.shape

    q_fwd, p_fwd = forward(
        [
            (question_tokens, question_lengths, question_params),
            (passage_tokens, passage_lengths, passage_params),
        ]
    )
    q_summed = q_fwd[1].reshape(questions, width)
    p_summed = p_fwd[1].reshape(passages, width)
    per_device = -(-(questions + passages) // 16) * 16
    spare = per_device - questions - passages
    summed = jnp.concatenate([q_summed, p_summed, jnp.zeros((spare, width), F32)], 0)
    units = (summed * lax.rsqrt(jnp.mean(summed * summed, -1, keepdims=True) + EPS)).astype(BF16)
    code = jnp.pad(
        jnp.stack([positives // 256, positives % 256], 1).astype(BF16),
        ((0, per_device - questions), (0, 126)),
    )
    every, masks = gather_units(jnp.concatenate([units, code], 1), devices)
    lens = jnp.concatenate([question_lengths, passage_lengths, jnp.ones((spare,), jnp.int32)])
    lens = jnp.broadcast_to(lens.astype(F32)[:, None], (per_device, 128))
    loss, grow = match_loss(every, masks, me[None], summed, lens, questions, passages)

    _, _, p_qkv, p_probs, p_context, *p_norm, p_middle, p_act, p_slope = p_fwd
    inner = p_act.shape[1]
    x_p, x_q = passage_tokens.reshape(-1, width), question_tokens.reshape(-1, width)

    p_blocks = x_p.shape[0] // ROWS
    p_ahead = -(-p_blocks * 3 // 5)

    def ffn_p(part, first, count, before):
        return ffn_back(
            passage_lengths, part, (*p_norm, p_slope), passage_params, passage_seq, first, count, before
        )

    def attention_p(gattn, small, first, count, arrays=()):
        return attention_back(gattn, p_context, p_qkv, p_probs, small, passage_params, first, count, arrays)

    ffn_parts = [(width, [(4, 5, 0, inner)])], [(inner, [(6, 7, 0, width)])]
    attention_parts = (
        [(width, [(0, 1, 0, 2 * width)])],
        [(width, [(0, 1, 2 * width, width), (2, 3, 0, width)])],
    )
    all_parts = [f + a for f, a in zip(ffn_parts, attention_parts)]
    ffn_outputs = [(width, [(0, 0, c) for c in range(inner // PIECE)]), (inner, [(1, 0, 0)])]

    def attention_outputs(part):
        return [(width, [(0, part, 0), (0, part, 1), (1, part, 0)]), (width, [(1, part, 1)])]

    def grads(x, gmixed, context, gattn, middle, gpre, act, gffn, parts, micros):
        operands = [x, gmixed, context, gattn, middle, gpre, act, gffn]
        used = sorted({k for stream in parts for _, terms in stream for x, g, *_ in terms for k in (x, g)})
        parts = [
            [(h, [(used.index(x), used.index(g), *cols) for x, g, *cols in terms]) for h, terms in stream]
            for stream in parts
        ]
        return weight_grad([operands[k] for k in used], parts, spots, devices, micros)

    line = Line(devices)
    q_grad, q_small, *halves = encoder_back(
        question_lengths, spots, grow[:questions], x_q, q_fwd[2:], question_params, question_seq, all_parts, devices
    )
    line.add("q", sum_pieces(*halves, devices, pairs=False))
    p_grow = grow[questions : questions + passages]
    none = jnp.zeros((16, width), F32)
    p_begun = line.step("q", lambda g: ffn_p(g, 0, p_ahead, [none]), p_grow)

    def second(begun):
        gffn, gpre, gattn, small = ffn_p(p_grow, p_ahead, p_blocks - p_ahead, begun)
        halves = grads(None, None, None, None, p_middle, gpre, p_act, gffn, ffn_parts, 11)
        return gattn, small, halves

    p_attn, p_small, halves = line.step("q", second, p_begun)
    line.add("p", sum_pieces(*halves, devices))
    p_mixed, p_grad, p_small = line.step("qp", lambda g: attention_p(g, p_small, 0, p_ahead), p_attn)

    def fourth(begun):
        gmixed, gtokens, small = attention_p(
            p_attn, begun[2], p_ahead, p_blocks - p_ahead, begun[:2]
        )
        halves = grads(x_p, gmixed, p_context, p_attn, None, None, None, None, attention_parts, 5)
        return gtokens, small, halves

    p_grad, p_small, halves = line.step("qp", fourth, (p_mixed, p_grad, p_small))
    line.add("a", sum_pieces(*halves, devices))
    line.add("s", sum_small(jnp.stack([q_small, p_small]), devices))
    line.step("qpas", again="qa")
    line.step("qpas", again="pa")
    line.step("qpas", again="pa")

    q_layout = [(all_parts, ffn_outputs + attention_outputs(1))]
    p_layout = [(ffn_parts, ffn_outputs), (attention_parts, attention_outputs(0))]

    def own(name):
        return line.running[name][1][0][0]

    q_outs = line.step(
        "qpas", lambda half: place([half], 0, spots, q_layout, devices), own("q"), again="a"
    )
    q_outs = line.step(
        "pas",
        lambda half: place([half], 1, spots, q_layout, devices, q_outs),
        line.done["q"][1],
        again="",
    )
    p_outs = line.step(
        "pas", lambda halves: place(halves, 0, spots, p_layout, devices), [own("p"), own("a")]
    )
    while line.running:
        line.step("s")
    p_outs = place([line.done["p"][1], line.done["a"][1]], 1, spots, p_layout, devices, p_outs)
    q_up, q_down, q_in, q_out = q_outs
    p_up, p_down, p_in, p_out = p_outs
    small = line.done["s"]

    def outputs(small, gin, gout, gup, gdown):
        return (
            gin,
            small[0:2],
            gout,
            small[2:4],
            small[4:6],
            small[6:8],
            gup,
            small[8 : 8 + inner // width].reshape(inner),
            gdown,
        )

    return (
        loss[0, 0],
        q_fwd[0].reshape(question_tokens.shape),
        p_fwd[0].reshape(passage_tokens.shape),
        q_grad.reshape(question_tokens.shape),
        p_grad.reshape(passage_tokens.shape),
        *outputs(small[0], q_in, q_out, q_up, q_down),
        *outputs(small[1], p_in, p_out, p_up, p_down),
    )


def solution(mesh):
    batch = P("dp", None, None)
    return jax.shard_map(
        partial(on_device, mesh.shape["dp"]),
        mesh=mesh,
        in_specs=(batch, batch, P("dp"), P("dp"), P("dp"), *[P()] * 18),
        out_specs=(P(), batch, batch, batch, batch, *[P()] * 18),
        check_vma=False,
    )
```

```python
import math
from functools import partial

import jax
import jax.numpy as jnp
from jax import lax
from jax.experimental import pallas as pl
from jax.experimental.pallas import tpu as pltpu
from jax.sharding import PartitionSpec as P

HEAD = 64
ROWS = 256
SHARPNESS = 20.0
NEG = -1e30
EPS = 1e-06
F32 = jnp.float32
BF16 = jnp.bfloat16
VMEM_BYTES = 44 * 1024 * 1024
LARGE_VMEM_BYTES = 60 * 1024 * 1024

DENSITY = 1.0 / math.sqrt(2.0 * math.pi)


def nn(a, b):
    return lax.dot_general(a, b, (((1,), (0,)), ((), ())), preferred_element_type=F32)


def nt(a, b):
    return lax.dot_general(a, b, (((1,), (1,)), ((), ())), preferred_element_type=F32)


def tn(a, b):
    return lax.dot_general(a, b, (((0,), (0,)), ((), ())), preferred_element_type=F32)


def gelu_pair(v):
    cdf = 0.5 + 0.5 * lax.erf(v * math.sqrt(0.5))
    bell = jnp.exp(v * v * -0.5)
    return v * cdf, cdf + v * (bell * DENSITY)


def layer_norm(v):
    center = v - jnp.mean(v, -1, keepdims=True)
    scale = lax.rsqrt(jnp.mean(center * center, -1, keepdims=True) + EPS)
    return center * scale, scale


def norm_back(grad, unit, scale, gain):
    t = grad * gain
    return scale * (
        t - jnp.mean(t, -1, keepdims=True) - unit * jnp.mean(t * unit, -1, keepdims=True)
    )


def fold_rows(v):
    return jnp.sum(v, 0, keepdims=True)


def cost(micros):
    return pl.CostEstimate(flops=int(micros * 1.15e9), bytes_accessed=0, transcendentals=0)


def full(array):
    zeros = (0,) * array.ndim
    return pl.BlockSpec(array.shape, lambda *_: zeros, pipeline_mode=pl.Buffered(1))


FAR = pl.BlockSpec(memory_space=pltpu.HBM)


def room(*arrays):
    return [*[pltpu.VMEM(a.shape, a.dtype) for a in arrays], pltpu.SemaphoreType.DMA((len(arrays),))]


def fetch(*pairs, arrived, now=None):
    copies = [pltpu.make_async_copy(far, near, arrived.at[i]) for i, (far, near) in enumerate(pairs)]
    begin(copies[:now])
    return copies


def begin(copies, step=0):
    @pl.when(pl.program_id(0) == step)
    def _():
        for copy in copies:
            copy.start()


def ready(copy, step=0):
    @pl.when(pl.program_id(0) == step)
    def _():
        copy.wait()


def rows(width, first=0):
    return pl.BlockSpec((ROWS, width), lambda i, *_: (i + first, 0))


KEPT = pl.BlockSpec(memory_space=pl.ANY)


def forward_kernel(seqs, counts, *refs):
    lens, refs = refs[:2], refs[2:]
    near, far, outs, held = refs[:12], refs[12:20], refs[20:42], refs[42:50]
    copies = fetch(*zip(far, held), arrived=refs[50], now=1)
    begin(copies[4:], min(1, counts[0] - 1))
    step = pl.program_id(0)
    first = 0
    for e, (seq, count) in enumerate(zip(seqs, counts)):

        @pl.when(jnp.logical_and(step >= first, step < first + count))
        def _(e=e, seq=seq, first=first):
            forward_block(
                seq,
                step - first,
                [partial(ready, copy, first) for copy in copies[4 * e : 4 * e + 4]],
                [] if e else copies[1:4],
                lens[e],
                *near[6 * e : 6 * e + 6],
                *outs[11 * e : 11 * e + 11],
                *held[4 * e : 4 * e + 4],
            )

        first += count


def forward_block(
    seq,
    block,
    wait,
    next_copies,
    lens,
    x_ref,
    in_bias,
    out_bias,
    gains,
    shifts,
    up_bias,
    out_ref,
    summed_ref,
    qkv_ref,
    probs_ref,
    context_ref,
    unit1_ref,
    unit2_ref,
    scale_ref,
    middle_ref,
    act_ref,
    slope_ref,
    in_proj,
    out_proj,
    up,
    down,
):
    groups = ROWS // seq
    width = x_ref.shape[1]
    row = lax.broadcasted_iota(jnp.int32, (ROWS, 128), 0)
    lane = lax.broadcasted_iota(jnp.int32, (ROWS, 128), 1)
    slot = lane % HEAD
    low_half = lane < HEAD
    group = row // seq
    limit = jnp.zeros((ROWS, 128), jnp.int32)
    for g in range(groups):
        limit = jnp.where(group == g, lens[block * groups + g], limit)
    live = (row - group * seq) < limit
    query_mark = jnp.where(slot == group, 1.0, 0.0).astype(BF16)
    key_mark = jnp.where(
        slot < groups, jnp.where(jnp.logical_and(slot == group, live), 0.0, NEG), 0.0
    ).astype(BF16)
    x = x_ref[...]
    wait[0]()
    begin(next_copies)
    mixed = nn(x, in_proj[...])
    query = ((mixed[:, :width] + in_bias[0:1]).astype(BF16) * (HEAD**-0.5)).astype(BF16)
    key = mixed[:, width : 2 * width].astype(BF16)
    value = (mixed[:, 2 * width :] + in_bias[1:2]).astype(BF16)
    qkv_ref[:, :width] = query
    qkv_ref[:, width : 2 * width] = key
    qkv_ref[:, 2 * width :] = value
    pairs = []
    for p in range(width // 128):
        cols = slice(128 * p, 128 * p + 128)
        total = None
        for h in range(2):
            mine = low_half if h == 0 else jnp.logical_not(low_half)
            query_h = jnp.where(mine, query[:, cols], query_mark)
            key_h = jnp.where(mine, key[:, cols], key_mark)
            value_h = jnp.where(mine, value[:, cols], jnp.zeros_like(key_mark))
            scores = nt(key_h, query_h)
            top = jnp.max(scores, 0, keepdims=True)
            weight = jnp.exp(scores - top)
            probs = (weight * (1.0 / jnp.sum(weight, 0, keepdims=True))).astype(BF16)
            probs_ref[0, 2 * p + h] = probs
            part = tn(probs, value_h)
            total = part if total is None else total + part
        pairs.append(total.astype(BF16))
    context = jnp.concatenate(pairs, 1)
    context_ref[...] = context
    wait[1]()
    first = x.astype(F32) + nn(context, out_proj[...]) + out_bias[0:1]
    unit1, scale1 = layer_norm(first)
    unit1_ref[...] = unit1.astype(BF16)
    middle_full = unit1 * gains[0:1] + shifts[0:1]
    middle = middle_full.astype(BF16)
    middle_ref[...] = middle
    second = middle_full + out_bias[1:2]
    wait[2]()
    wait[3]()
    chunk = 256
    for c in range(up.shape[1] // chunk):
        cols = slice(chunk * c, chunk * c + chunk)
        pre = nn(middle, up[:, cols]) + up_bias[:, cols]
        act, slope = gelu_pair(pre)
        act = act.astype(BF16)
        act_ref[:, cols] = act
        slope_ref[:, cols] = slope.astype(BF16)
        second += nn(act, down[cols, :])
    unit2, scale2 = layer_norm(second)
    unit2_ref[...] = unit2.astype(BF16)
    scale_ref[...] = jnp.where(lane == 0, scale1, scale2)
    out = unit2 * gains[1:2] + shifts[1:2]
    out_ref[...] = out.astype(BF16)
    kept = jnp.where(live[:, :1], out, 0.0)
    for g in range(groups):
        length = lens[block * groups + g].astype(F32)
        summed_ref[0, g : g + 1] = fold_rows(kept[g * seq : (g + 1) * seq]) / length


def forward(encoders):
    sds = jax.ShapeDtypeStruct
    lens, near, near_specs, far, out_specs, out_shape, seqs, counts = [], [], [], [], [], [], [], []
    first = 0
    for x, length, params in encoders:
        in_proj, in_bias, out_proj, out_bias, gains, shifts, up, up_bias, down = params
        examples, seq, width = x.shape
        tokens = examples * seq
        blocks, groups, heads = tokens // ROWS, ROWS // seq, width // HEAD
        inner = up.shape[1]

        def block(*shape, first=first, blocks=blocks):
            rest = (0,) * (len(shape) - 1)
            return pl.BlockSpec(shape, lambda i, *_: (jnp.clip(i - first, 0, blocks - 1), *rest))

        small = (in_bias, out_bias, gains, shifts, up_bias[None])
        lens.append(length)
        near += [x.reshape(tokens, width), *small]
        near_specs += [block(ROWS, width), *[full(w) for w in small]]
        far += [in_proj, out_proj, up, down]
        shapes = [
            ((tokens, width), BF16),
            ((blocks, groups, width), F32),
            ((tokens, 3 * width), BF16),
            ((blocks, heads, ROWS, ROWS), BF16),
            ((tokens, width), BF16),
            ((tokens, width), BF16),
            ((tokens, width), BF16),
            ((tokens, 128), F32),
            ((tokens, width), BF16),
            ((tokens, inner), BF16),
            ((tokens, inner), BF16),
        ]
        for shape, kind in shapes:
            out_specs.append(block(1 if shape[0] == blocks else ROWS, *shape[1:]))
            out_shape.append(sds(shape, kind))
        seqs.append(seq)
        counts.append(blocks)
        first += blocks
    outs = pl.pallas_call(
        partial(forward_kernel, seqs, counts),
        grid_spec=pltpu.PrefetchScalarGridSpec(
            num_scalar_prefetch=2,
            grid=(first,),
            in_specs=[*near_specs, *[FAR] * len(far)],
            out_specs=out_specs,
            scratch_shapes=room(*far),
        ),
        out_shape=out_shape,
        compiler_params=pltpu.CompilerParams(vmem_limit_bytes=LARGE_VMEM_BYTES),
        cost_estimate=cost(40),
        name="layer_forward",
    )(*lens, *near, *far)
    return outs[:11], outs[11:]


def ffn_back_kernel(seq, first, lens, *refs):
    near, (down_far, up_far, before), refs = refs[:6], refs[6:9], refs[9:]
    outs, (down, up, arrived) = refs[-7:-3], refs[-3:]
    copies = fetch((down_far, down), (up_far, up), arrived=arrived)

    @pl.when(pl.program_id(0) == 0)
    def _():
        outs[3][...] = before[...]

    ffn_back_block(seq, first + pl.program_id(0), lens, copies, [], *near, *outs, down, up)


def ffn_back_block(
    seq,
    block,
    lens,
    copies,
    next_copies,
    grow_ref,
    unit1_ref,
    unit2_ref,
    scale_ref,
    slope_ref,
    gains,
    gffn_ref,
    gpre_ref,
    gattn_ref,
    small_ref,
    down,
    up,
):
    groups = ROWS // seq
    width = unit1_ref.shape[1]
    row = lax.broadcasted_iota(jnp.int32, (seq, width), 0)
    grad_out = jnp.concatenate(
        [
            jnp.where(row < lens[block * groups + g], grow_ref[0, g : g + 1], 0.0)
            for g in range(groups)
        ],
        0,
    )
    unit2 = unit2_ref[...].astype(F32)
    small_ref[7:8] += fold_rows(grad_out)
    small_ref[5:6] += fold_rows(grad_out * unit2)
    gsecond = norm_back(grad_out, unit2, scale_ref[:, 1:2], gains[1:2])
    gffn = gsecond.astype(BF16)
    gffn_ref[...] = gffn
    small_ref[3:4] += fold_rows(gffn.astype(F32))
    gmiddle = gsecond
    ready(copies[0])
    chunk = 256
    for c in range(up.shape[1] // chunk):
        cols = slice(chunk * c, chunk * c + chunk)
        gpre = (nt(gffn, down[cols, :]) * slope_ref[:, cols].astype(F32)).astype(BF16)
        gpre_ref[:, cols] = gpre
        line, left = 8 + chunk * c // width, chunk * c % width
        small_ref[line : line + 1, left : left + chunk] += fold_rows(gpre.astype(F32))
        if c == 0:
            ready(copies[1])
            begin(next_copies)
        gmiddle += nt(gpre, up[:, cols])
    unit1 = unit1_ref[...].astype(F32)
    small_ref[6:7] += fold_rows(gmiddle)
    small_ref[4:5] += fold_rows(gmiddle * unit1)
    gfirst = norm_back(gmiddle, unit1, scale_ref[:, 0:1], gains[0:1])
    gattn = gfirst.astype(BF16)
    gattn_ref[...] = gattn
    small_ref[2:3] += fold_rows(gattn.astype(F32))


def ffn_back(lens, grow, kept, params, seq, first, count, before):
    unit1, unit2, scale, slope = kept
    _, _, _, _, gains, _, up, _, down = params
    tokens, width = unit1.shape
    blocks, groups, inner = tokens // ROWS, ROWS // seq, up.shape[1]
    *arrays, small = before
    sds = jax.ShapeDtypeStruct
    return pl.pallas_call(
        partial(ffn_back_kernel, seq, first),
        grid_spec=pltpu.PrefetchScalarGridSpec(
            num_scalar_prefetch=1,
            grid=(count,),
            in_specs=[
                pl.BlockSpec((1, groups, width), lambda i, *_: (i + first, 0, 0)),
                rows(width, first),
                rows(width, first),
                rows(128, first),
                rows(inner, first),
                full(gains),
                FAR,
                FAR,
                full(small),
                *[KEPT] * len(arrays),
            ],
            out_specs=[
                rows(width, first),
                rows(inner, first),
                rows(width, first),
                pl.BlockSpec((16, width), lambda i, *_: (0, 0)),
            ],
            scratch_shapes=room(down, up),
        ),
        out_shape=[
            sds((tokens, width), BF16),
            sds((tokens, inner), BF16),
            sds((tokens, width), BF16),
            sds((16, width), F32),
        ],
        input_output_aliases={10 + i: i for i in range(len(arrays))},
        compiler_params=pltpu.CompilerParams(vmem_limit_bytes=VMEM_BYTES),
        cost_estimate=cost(count * ROWS / 80),
        name="ffn_backward",
    )(
        lens, grow.reshape(blocks, groups, width), unit1, unit2, scale, slope, gains, down, up, small, *arrays
    )


def attention_back_kernel(*refs):
    near, before_ref, out_proj_far, refs = refs[:4], refs[4], refs[5], refs[6:]
    outs, (out_proj, arrived) = refs[-4:-2], refs[-2:]
    copies = fetch((out_proj_far, out_proj), arrived=arrived)

    @pl.when(pl.program_id(0) == 0)
    def _():
        outs[1][...] = before_ref[...]

    attention_back_block(copies, *near, *outs, out_proj)


def attention_back_block(
    copies,
    gattn_ref,
    context_ref,
    qkv_ref,
    probs_ref,
    gmixed_ref,
    small_ref,
    out_proj,
):
    width = gattn_ref.shape[1]
    lane = lax.broadcasted_iota(jnp.int32, (ROWS, 128), 1)
    low_half = lane < HEAD
    blank = jnp.zeros((ROWS, 128), BF16)
    gattn = gattn_ref[...]
    ready(copies[0])
    gcontext = nt(gattn, out_proj[...]).astype(BF16)
    heads = width // HEAD
    member = (
        lax.broadcasted_iota(jnp.int32, (16, width), 1) // HEAD
        == lax.broadcasted_iota(jnp.int32, (16, width), 0)
    )
    member = jnp.where(member, 1.0, 0.0).astype(BF16)
    product = gcontext.astype(F32) * context_ref[...].astype(F32)
    coarse = product.astype(BF16)
    fine = (product - coarse.astype(F32)).astype(BF16)
    offsets = nt(member, coarse) + nt(member, fine)
    for p in range(width // 128):
        cols = slice(128 * p, 128 * p + 128)
        kcols = slice(width + 128 * p, width + 128 * p + 128)
        vcols = slice(2 * width + 128 * p, 2 * width + 128 * p + 128)
        query, key, value = qkv_ref[:, cols], qkv_ref[:, kcols], qkv_ref[:, vcols]
        gquery = gkey = gvalue = None
        for h in range(2):
            mine = low_half if h == 0 else jnp.logical_not(low_half)
            gcontext_h = jnp.where(mine, gcontext[:, cols], blank)
            probs = probs_ref[0, 2 * p + h]
            gprobs = nt(value, gcontext_h)
            head = 2 * p + h
            gscores = (probs.astype(F32) * (gprobs - offsets[head : head + 1])).astype(BF16)
            parts = (
                tn(gscores, jnp.where(mine, key, blank)),
                nn(gscores, jnp.where(mine, query, blank)),
                nn(probs, gcontext_h),
            )
            if h == 0:
                gquery, gkey, gvalue = parts
            else:
                gquery, gkey, gvalue = gquery + parts[0], gkey + parts[1], gvalue + parts[2]
        gquery = (gquery * (HEAD**-0.5)).astype(BF16)
        gmixed_ref[:, cols] = gquery
        gmixed_ref[:, kcols] = gkey.astype(BF16)
        gvalue = gvalue.astype(BF16)
        gmixed_ref[:, vcols] = gvalue
        small_ref[0:1, cols] += fold_rows(gquery.astype(F32))
        small_ref[1:2, cols] += fold_rows(gvalue.astype(F32))


def attention_back(gattn, context, qkv, probs, small, params, first, count, arrays=()):
    out_proj = params[2]
    tokens, width = context.shape
    sds = jax.ShapeDtypeStruct
    return pl.pallas_call(
        attention_back_kernel,
        grid=(count,),
        in_specs=[
            rows(width, first),
            rows(width, first),
            rows(3 * width, first),
            pl.BlockSpec((1, *probs.shape[1:]), lambda i: (i + first, 0, 0, 0)),
            full(small),
            FAR,
            *[KEPT] * len(arrays),
        ],
        out_specs=[
            rows(3 * width, first),
            pl.BlockSpec(small.shape, lambda i: (0, 0)),
        ],
        out_shape=[
            sds((tokens, 3 * width), BF16),
            sds(small.shape, F32),
        ],
        scratch_shapes=room(out_proj),
        input_output_aliases={6 + i: i for i in range(len(arrays))},
        compiler_params=pltpu.CompilerParams(vmem_limit_bytes=VMEM_BYTES),
        cost_estimate=cost(count * ROWS / 70),
        name="attention_backward",
    )(gattn, context, qkv, probs, small, out_proj, *arrays)


def token_grad(gattn, gmixed, in_proj):
    return (gattn.astype(F32) + nt(gmixed, in_proj)).astype(BF16)


def match_kernel(masks, questions, passages, blocks_ref, spot, summed_ref, lens_ref, loss_ref, grow_ref, units_ref):
    per_device, width = summed_ref.shape
    for k, mask in enumerate(masks):
        lead = pl.multiple_of((spot[0] ^ mask) * per_device, per_device)
        units_ref[pl.ds(lead, per_device), :] = blocks_ref[k]
    every = units_ref[...]
    count = every.shape[0]
    units = every[:, :width]
    scale = SHARPNESS / width
    ri = lax.broadcasted_iota(jnp.int32, (count, count), 0)
    ci = lax.broadcasted_iota(jnp.int32, (count, count), 1)
    pick = jnp.where(
        lax.broadcasted_iota(jnp.int32, (8, 128), 0) == lax.broadcasted_iota(jnp.int32, (8, 128), 1), 1.0, 0.0
    ).astype(BF16)
    digits = nt(pick, every[:, width:])
    positive = (digits[0:1] * 256.0 + digits[1:2]).astype(jnp.int32)
    place = (positive // passages) * per_device + questions + positive % passages
    rlocal = ri % per_device
    is_passage = jnp.logical_and(rlocal >= questions, rlocal < questions + passages)
    is_question = (ci[0:1] % per_device) < questions
    match = nt(units, units) * scale
    shown = jnp.where(is_passage, match, NEG)
    top = jnp.max(shown, 0, keepdims=True)
    total = jnp.sum(jnp.exp(shown - top), 0, keepdims=True)
    logsum = top + jnp.log(total)
    hit = ri == place
    chosen = jnp.sum(jnp.where(hit, match, 0.0), 0, keepdims=True)
    loss_ref[...] = jnp.sum(jnp.where(is_question, logsum - chosen, 0.0), 1, keepdims=True)

    first = spot[0] * per_device
    own = blocks_ref[0]
    own_units = own[:, :width]
    rown = lax.broadcasted_iota(jnp.int32, (per_device, count), 0)
    cown = lax.broadcasted_iota(jnp.int32, (per_device, count), 1)
    match_own = nt(own_units, units) * scale
    hit_p = jnp.logical_and(place == first + rown, is_question)
    share_p = jnp.exp(match_own - logsum) - jnp.where(hit_p, 1.0, 0.0)
    share_p = jnp.where(is_question, share_p, 0.0)
    clocal = cown % per_device
    col_passage = jnp.logical_and(clocal >= questions, clocal < questions + passages)
    shown_q = jnp.where(col_passage, match_own, NEG)
    weight_q = jnp.exp(shown_q - jnp.max(shown_q, 1, keepdims=True))
    code = own[:, width:].astype(F32)
    positive_q = (code[:, 0:1] * 256.0 + code[:, 1:2]).astype(jnp.int32)
    place_q = (positive_q // passages) * per_device + questions + positive_q % passages
    share_q = weight_q / jnp.sum(weight_q, 1, keepdims=True) - jnp.where(cown == place_q, 1.0, 0.0)
    share = jnp.where(rown < questions, share_q, share_p).astype(BF16)
    gunit = nn(share, units) * scale
    summed = summed_ref[...]
    r = lax.rsqrt(jnp.mean(summed * summed, -1, keepdims=True) + EPS)
    gsummed = r * gunit - (r * r * r) * summed * jnp.mean(gunit * summed, -1, keepdims=True)
    grow_ref[...] = gsummed / lens_ref[:, 0:1]


def match_loss(blocks, masks, spot, summed, lens, questions, passages):
    count, per_device, wide = blocks.shape
    vmem = pl.BlockSpec(memory_space=pltpu.VMEM)
    return pl.pallas_call(
        partial(match_kernel, masks, questions, passages),
        in_specs=[vmem, pl.BlockSpec(memory_space=pltpu.SMEM), vmem, vmem],
        out_specs=[vmem, vmem],
        out_shape=[
            jax.ShapeDtypeStruct((1, 1), F32),
            jax.ShapeDtypeStruct(summed.shape, F32),
        ],
        scratch_shapes=[pltpu.VMEM((count * per_device, wide), BF16)],
        compiler_params=pltpu.CompilerParams(vmem_limit_bytes=VMEM_BYTES),
        cost_estimate=cost(3),
        name="match_loss",
    )(blocks, spot, summed, lens)


ORDERS = ("xyz", "yxz")
PIECE = 512


def axis_layout(devices):
    bits = devices.bit_length() - 2
    x = bits // 3
    y = (bits - x) // 2
    return {"x": (1, x), "y": (1 + x, y), "z": (1 + x + y, bits - x - y)}


def chip_number(me, devices, order):
    layout = axis_layout(devices)
    number = jnp.zeros((), jnp.int32)
    for axis in order:
        start, count = layout[axis]
        number = (number << count) | ((me >> start) & ((1 << count) - 1))
    return number


def segments(streams, devices):
    found = []
    for stream in streams:
        rows_of, start = [], 0
        for height, terms in stream:
            columns = sum(n for *_, n in terms) // PIECE
            tall = height * columns // devices
            rows_of.append((start, tall, columns))
            start += -(-tall // 16) * 16
        found.append(rows_of)
    return found, start


def weight_grad_kernel(streams, places, spots, *refs):
    *operands, send_ref, keep_ref = refs
    for side, out in enumerate((send_ref, keep_ref)):
        for stream, parts in enumerate(streams):
            for (height, terms), (top, tall, columns) in zip(parts, places[stream]):
                column = 0
                half = height // 2
                step = min(half, 256)
                for x, g, first, n in terms:
                    for s in range(half // step):
                        lead = pl.multiple_of((spots[0] ^ (1 - side)) * half + s * step, step)
                        tile = tn(
                            operands[x][:, pl.ds(lead, step)], operands[g][:, first : first + n]
                        ).astype(BF16)
                        for b in range(step // tall):
                            for c in range(n // PIECE):
                                number = (s * (step // tall) + b) * columns + column + c
                                out[stream, number ^ spots[1 + stream], top : top + tall] = tile[
                                    b * tall : (b + 1) * tall, c * PIECE : (c + 1) * PIECE
                                ]
                    column += n // PIECE


def weight_grad(operands, streams, spots, devices, micros):
    places, tall = segments(streams, devices)
    vmem = pl.BlockSpec(memory_space=pltpu.VMEM)
    out = jax.ShapeDtypeStruct((len(streams), devices // 2, tall, PIECE), BF16)
    return pl.pallas_call(
        partial(weight_grad_kernel, streams, places),
        in_specs=[pl.BlockSpec(memory_space=pltpu.SMEM), *[vmem] * len(operands)],
        out_specs=[vmem, vmem],
        out_shape=[out, out],
        compiler_params=pltpu.CompilerParams(vmem_limit_bytes=VMEM_BYTES),
        cost_estimate=cost(micros),
        name="weight_gradient",
    )(spots, *operands)


def encoder_back_kernel(seq, streams, places, lens, spots, *refs):
    (grow, unit1, unit2, scale, slope, gains, context, qkv, probs), refs = refs[:9], refs[9:]
    far, (gattn, gmixed, small, send, keep), held = refs[:7], refs[7:12], refs[12:19]
    gffn, gpre, arrived = refs[19:]
    copies = fetch(*zip(far, held), arrived=arrived, now=2)
    down, up, out_proj, x, contexts, middle, act = held
    block = pl.program_id(0)

    @pl.when(block == 0)
    def _():
        small[...] = jnp.zeros_like(small)

    span = pl.ds(pl.multiple_of(block * ROWS, ROWS), ROWS)
    here = [r.at[span] for r in (gffn, gpre, gattn, gmixed)]
    ffn_back_block(
        seq, block, lens, copies[:2], copies[2:3], grow, unit1, unit2, scale, slope, gains, *here[:3], small, down, up
    )
    begin(copies[3:])
    attention_back_block(copies[2:3], here[2], context, qkv, probs, here[3], small, out_proj)
    last = gffn.shape[0] // ROWS - 1
    for copy in copies[3:]:
        ready(copy, last)

    @pl.when(block == last)
    def _():
        operands = (x, gmixed, contexts, gattn, middle, gpre, act, gffn)
        weight_grad_kernel(streams, places, spots, *operands, send, keep)


def encoder_back(lens, spots, grow, x, kept, params, seq, streams, devices):
    qkv, probs, context, unit1, unit2, scale, middle, act, slope = kept
    _, _, out_proj, _, gains, _, up, _, down = params
    tokens, width = context.shape
    blocks, groups, inner = tokens // ROWS, ROWS // seq, up.shape[1]
    places, tall = segments(streams, devices)
    sds = jax.ShapeDtypeStruct
    half = (len(streams), devices // 2, tall, PIECE)
    far = (down, up, out_proj, x, context, middle, act)

    def whole(*shape):
        return pl.BlockSpec(shape, lambda i, *_: (0,) * len(shape), pipeline_mode=pl.Buffered(1))

    return pl.pallas_call(
        partial(encoder_back_kernel, seq, streams, places),
        grid_spec=pltpu.PrefetchScalarGridSpec(
            num_scalar_prefetch=2,
            grid=(blocks,),
            in_specs=[
                pl.BlockSpec((1, groups, width), lambda i, *_: (i, 0, 0)),
                rows(width),
                rows(width),
                rows(128),
                rows(inner),
                full(gains),
                rows(width),
                rows(3 * width),
                pl.BlockSpec((1, *probs.shape[1:]), lambda i, *_: (i, 0, 0, 0)),
                *[FAR] * len(far),
            ],
            out_specs=[
                whole(tokens, width),
                whole(tokens, 3 * width),
                pl.BlockSpec((16, width), lambda i, *_: (0, 0)),
                whole(*half),
                whole(*half),
            ],
            scratch_shapes=[
                *room(*far)[:-1],
                pltpu.VMEM((tokens, width), BF16),
                pltpu.VMEM((tokens, inner), BF16),
                room(*far)[-1],
            ],
        ),
        out_shape=[
            sds((tokens, width), BF16),
            sds((tokens, 3 * width), BF16),
            sds((16, width), F32),
            sds(half, BF16),
            sds(half, BF16),
        ],
        compiler_params=pltpu.CompilerParams(vmem_limit_bytes=LARGE_VMEM_BYTES),
        cost_estimate=cost(18),
        name="encoder_backward",
    )(
        lens, spots, grow.reshape(blocks, groups, width), unit1, unit2, scale, slope, gains, context, qkv, probs, *far
    )


PARTS = 4


def place_kernel(outputs, spots, *refs):
    inputs, outs = refs, refs[-len(outputs) :]
    group = inputs[0].shape[1]
    for out, blocks in zip(outs, outputs):
        for k, (source, stream, (top, tall, columns), column) in enumerate(blocks):
            inner = spots[1 + stream] & (group - 1)
            for b in range(out.shape[0] // tall):
                piece = inputs[source][0, (b * columns + column) ^ inner, top : top + tall]
                out[b * tall : (b + 1) * tall, k * PIECE : (k + 1) * PIECE] = piece.astype(F32)


def place(halves, side, spots, layouts, devices, arrays=()):
    group = halves[0].shape[1] // PARTS
    blocks_of, heights = [], []
    for k, (streams, outputs) in enumerate(layouts):
        places, _ = segments(streams, devices)
        for height, blocks in outputs:
            blocks_of.append([(2 * k + st, st, places[st][part], column) for st, part, column in blocks])
            heights.append(height)

    def piece_spec(half, stream):
        return pl.BlockSpec(
            (1, group, half.shape[2], PIECE), lambda g, spots: (stream, g ^ spots[3 + stream], 0, 0)
        )

    count = 2 * len(halves)
    return pl.pallas_call(
        partial(place_kernel, blocks_of),
        grid_spec=pltpu.PrefetchScalarGridSpec(
            num_scalar_prefetch=1,
            grid=(PARTS,),
            in_specs=[
                *[piece_spec(half, stream) for half in halves for stream in range(2)],
                *[KEPT] * len(arrays),
            ],
            out_specs=[
                pl.BlockSpec(
                    (height // (2 * PARTS), PIECE * len(b)),
                    lambda g, spots: ((spots[0] ^ side) * PARTS + g, 0),
                )
                for height, b in zip(heights, blocks_of)
            ],
        ),
        out_shape=[
            jax.ShapeDtypeStruct((height, PIECE * len(b)), F32) for height, b in zip(heights, blocks_of)
        ],
        input_output_aliases={1 + count + i: i for i in range(len(arrays))},
        compiler_params=pltpu.CompilerParams(vmem_limit_bytes=VMEM_BYTES),
        cost_estimate=cost(3),
        name="place_gradient",
    )(spots, *[half for half in halves for _ in range(2)], *arrays)


def swap(array, mask, devices):
    return lax.ppermute(array, "dp", [(i, i ^ mask) for i in range(devices)])


def add(*terms):
    total = terms[0].astype(F32)
    for t in terms[1:]:
        total = total + t.astype(F32)
    return total.astype(BF16)


def sum_pieces(send, keep, devices, pairs=True):
    layout = axis_layout(devices)
    (got,) = yield [(send, 1)]
    held = [[keep[i], got[i]] for i in range(len(ORDERS))]
    for level in range(2):
        parts = []
        for terms, order in zip(held, ORDERS):
            ways = 1 << layout[order[level]][1]
            size = terms[0].shape[0] // ways
            parts.append([add(*[t[m * size : (m + 1) * size] for t in terms]) for m in range(ways)])
        got = yield [
            (p, m << layout[order[level]][0])
            for stream, order in zip(parts, ORDERS)
            for m, p in enumerate(stream)
            if m
        ]
        held = []
        for stream in parts:
            held.append([stream[0], *got[: len(stream) - 1]])
            got = got[len(stream) - 1 :]
    start, count = layout["z"]
    size = held[0][0].shape[0] >> count
    pieces = {
        m: jnp.stack(
            [sum(t[m * size : (m + 1) * size].astype(F32) for t in terms) for terms in held]
        )
        for m in range(1 << count)
    }
    if pairs:
        for bit in range(count):
            away = [m for m in sorted(pieces) if m >> bit & 1]
            (got,) = yield [
                (jnp.concatenate([pieces[m] for m in away], 1).astype(BF16), 1 << (start + bit))
            ]
            pieces = {
                m ^ (1 << bit): pieces[m ^ (1 << bit)] + got[:, k * size : (k + 1) * size].astype(F32)
                for k, m in enumerate(away)
            }
    else:
        got = yield [(pieces[m].astype(BF16), m << start) for m in range(1, 1 << count)]
        pieces = {0: pieces[0] + sum(g.astype(F32) for g in got)}
    pieces = {0: pieces[0].astype(BF16)}
    if not pairs:
        got = yield [(pieces[0], m << start) for m in range(1, 1 << count)]
        pieces.update(enumerate(got, 1))
    for bit in reversed(range(count if pairs else 0)):
        known = sorted(pieces)
        (got,) = yield [(jnp.concatenate([pieces[m] for m in known], 1), 1 << (start + bit))]
        for k, m in enumerate(known):
            pieces[m | (1 << bit)] = got[:, k * size : (k + 1) * size]
    every = jnp.concatenate([pieces[m] for m in sorted(pieces)], 1)
    done = [every[i] for i in range(len(ORDERS))]
    for level in (1, 0):
        sends = []
        for mine, order in zip(done, ORDERS):
            start, count = layout[order[level]]
            sends.append([(mine, m << start) for m in range(1, 1 << count)])
        got = yield [s for stream in sends for s in stream]
        grown = []
        for mine, stream in zip(done, sends):
            grown.append(jnp.concatenate([mine, *got[: len(stream)]], 0))
            got = got[len(stream) :]
        done = grown
    mine = jnp.stack(done)
    (other,) = yield [(mine, 1)]
    return mine, other


def sum_small(array, devices):
    for bit in range(devices.bit_length() - 1):
        (got,) = yield [(array, 1 << bit)]
        array = array + got
    return array


class Line:
    def __init__(self, devices):
        self.devices = devices
        self.running = {}
        self.done = {}

    def add(self, name, steps):
        self.running[name] = (steps, next(steps))

    def step(self, names, kernel=None, operand=None, again=""):
        names = [n for n in names if n in self.running]
        sends = [self.running[n][1] for n in names]
        arrays = [[a for a, _ in s] for s in sends]
        arrays, operand = lax.optimization_barrier((arrays, operand))
        got = [[swap(a, m, self.devices) for a, (_, m) in zip(x, s)] for x, s in zip(arrays, sends)]
        result = kernel(operand) if kernel else None
        for i, n in enumerate(names):
            if n in again:
                steps = self.running[n][0]
                sends = steps.send(got[i])
                self.running[n] = (steps, sends)
                arrays = lax.optimization_barrier([a for a, _ in sends])
                got[i] = [swap(a, m, self.devices) for a, (_, m) in zip(arrays, sends)]
        got, result = lax.optimization_barrier((got, result))
        for n, g in zip(names, got):
            steps, _ = self.running.pop(n)
            try:
                self.running[n] = (steps, steps.send(g))
            except StopIteration as end:
                self.done[n] = end.value
        return result


def gather_stages(devices):
    (x, nx), (y, ny), (z, nz) = (axis_layout(devices)[a] for a in "xyz")
    plane = [(x, nx + ny)] if nx + ny < 3 else [(y, ny), (x, nx)]
    return [(z, nz), *plane, (0, 1)]


def gather_units(own, devices):
    every, masks = own[None], [0]
    for start, count in gather_stages(devices):
        steps = [m << start for m in range(1 << count)]
        every = jnp.concatenate([every] + [swap(every, m, devices) for m in steps[1:]], 0)
        masks = [k ^ m for m in steps for k in masks]
    return every, masks


def on_device(devices, *args):
    (question_tokens, passage_tokens, question_lengths, passage_lengths, positives), weights = args[:5], args[5:]
    question_params, passage_params = weights[:9], weights[9:]
    me = lax.axis_index("dp").astype(jnp.int32)
    chips = [chip_number(me, devices, order) for order in ORDERS]
    group = devices // 8
    spots = jnp.stack([me & 1, *chips, *[c // group for c in chips]])
    questions, question_seq, width = question_tokens.shape
    passages, passage_seq, _ = passage_tokens.shape

    q_fwd, p_fwd = forward(
        [
            (question_tokens, question_lengths, question_params),
            (passage_tokens, passage_lengths, passage_params),
        ]
    )
    q_summed = q_fwd[1].reshape(questions, width)
    p_summed = p_fwd[1].reshape(passages, width)
    per_device = -(-(questions + passages) // 16) * 16
    spare = per_device - questions - passages
    summed = jnp.concatenate([q_summed, p_summed, jnp.zeros((spare, width), F32)], 0)
    units = (summed * lax.rsqrt(jnp.mean(summed * summed, -1, keepdims=True) + EPS)).astype(BF16)
    code = jnp.pad(
        jnp.stack([positives // 256, positives % 256], 1).astype(BF16),
        ((0, per_device - questions), (0, 126)),
    )
    every, masks = gather_units(jnp.concatenate([units, code], 1), devices)
    lens = jnp.concatenate([question_lengths, passage_lengths, jnp.ones((spare,), jnp.int32)])
    lens = jnp.broadcast_to(lens.astype(F32)[:, None], (per_device, 128))
    loss, grow = match_loss(every, masks, me[None], summed, lens, questions, passages)

    _, _, p_qkv, p_probs, p_context, *p_norm, p_middle, p_act, p_slope = p_fwd
    inner = p_act.shape[1]
    x_p, x_q = passage_tokens.reshape(-1, width), question_tokens.reshape(-1, width)

    p_blocks = x_p.shape[0] // ROWS
    p_ahead = -(-p_blocks * 3 // 5)

    def ffn_p(part, first, count, before):
        return ffn_back(
            passage_lengths, part, (*p_norm, p_slope), passage_params, passage_seq, first, count, before
        )

    def attention_p(gattn, small, first, count, arrays=()):
        return attention_back(gattn, p_context, p_qkv, p_probs, small, passage_params, first, count, arrays)

    ffn_parts = [(width, [(4, 5, 0, inner)])], [(inner, [(6, 7, 0, width)])]
    attention_parts = (
        [(width, [(0, 1, 0, 2 * width)])],
        [(width, [(0, 1, 2 * width, width), (2, 3, 0, width)])],
    )
    all_parts = [f + a for f, a in zip(ffn_parts, attention_parts)]
    ffn_outputs = [(width, [(0, 0, c) for c in range(inner // PIECE)]), (inner, [(1, 0, 0)])]

    def attention_outputs(part):
        return [(width, [(0, part, 0), (0, part, 1), (1, part, 0)]), (width, [(1, part, 1)])]

    def grads(x, gmixed, context, gattn, middle, gpre, act, gffn, parts, micros):
        operands = [x, gmixed, context, gattn, middle, gpre, act, gffn]
        used = sorted({k for stream in parts for _, terms in stream for x, g, *_ in terms for k in (x, g)})
        parts = [
            [(h, [(used.index(x), used.index(g), *cols) for x, g, *cols in terms]) for h, terms in stream]
            for stream in parts
        ]
        return weight_grad([operands[k] for k in used], parts, spots, devices, micros)

    line = Line(devices)
    q_attn, q_mixed, q_small, *halves = encoder_back(
        question_lengths, spots, grow[:questions], x_q, q_fwd[2:], question_params, question_seq, all_parts, devices
    )
    line.add("q", sum_pieces(*halves, devices, pairs=False))
    p_grow = grow[questions : questions + passages]
    none = jnp.zeros((16, width), F32)
    p_begun = line.step("q", lambda g: ffn_p(g, 0, p_ahead, [none]), p_grow)

    def second(begun):
        gffn, gpre, gattn, small = ffn_p(p_grow, p_ahead, p_blocks - p_ahead, begun)
        halves = grads(None, None, None, None, p_middle, gpre, p_act, gffn, ffn_parts, 11)
        return gattn, small, halves

    p_attn, p_small, halves = line.step("q", second, p_begun)
    line.add("p", sum_pieces(*halves, devices))
    p_mixed, p_small = line.step("qp", lambda g: attention_p(g, p_small, 0, p_ahead), p_attn)

    def fourth(begun):
        gmixed, small = attention_p(p_attn, begun[1], p_ahead, p_blocks - p_ahead, begun[:1])
        halves = grads(x_p, gmixed, p_context, p_attn, None, None, None, None, attention_parts, 5)
        return gmixed, small, halves

    p_mixed, p_small, halves = line.step("qp", fourth, (p_mixed, p_small))
    line.add("a", sum_pieces(*halves, devices))
    line.add("s", sum_small(jnp.stack([q_small, p_small]), devices))
    line.step("qpas", again="a")
    p_grad = line.step("qpas", lambda g: token_grad(p_attn, g, passage_params[0]), p_mixed, again="pa")
    q_grad = line.step("qpas", lambda g: token_grad(q_attn, g, question_params[0]), q_mixed, again="pa")

    q_layout = [(all_parts, ffn_outputs + attention_outputs(1))]
    p_layout = [(ffn_parts, ffn_outputs), (attention_parts, attention_outputs(0))]

    def own(name):
        return line.running[name][1][0][0]

    q_outs = line.step(
        "qpas", lambda half: place([half], 0, spots, q_layout, devices), own("q"), again="a"
    )
    q_outs = line.step(
        "pas",
        lambda half: place([half], 1, spots, q_layout, devices, q_outs),
        line.done["q"][1],
        again="",
    )
    p_outs = line.step(
        "pas", lambda halves: place(halves, 0, spots, p_layout, devices), [own("p"), own("a")]
    )
    while line.running:
        line.step("s")
    p_outs = place([line.done["p"][1], line.done["a"][1]], 1, spots, p_layout, devices, p_outs)
    q_up, q_down, q_in, q_out = q_outs
    p_up, p_down, p_in, p_out = p_outs
    small = line.done["s"]

    def outputs(small, gin, gout, gup, gdown):
        return (
            gin,
            small[0:2],
            gout,
            small[2:4],
            small[4:6],
            small[6:8],
            gup,
            small[8 : 8 + inner // width].reshape(inner),
            gdown,
        )

    return (
        loss[0, 0],
        q_fwd[0].reshape(question_tokens.shape),
        p_fwd[0].reshape(passage_tokens.shape),
        q_grad.reshape(question_tokens.shape),
        p_grad.reshape(passage_tokens.shape),
        *outputs(small[0], q_in, q_out, q_up, q_down),
        *outputs(small[1], p_in, p_out, p_up, p_down),
    )


def solution(mesh):
    batch = P("dp", None, None)
    return jax.shard_map(
        partial(on_device, mesh.shape["dp"]),
        mesh=mesh,
        in_specs=(batch, batch, P("dp"), P("dp"), P("dp"), *[P()] * 18),
        out_specs=(P(), batch, batch, batch, batch, *[P()] * 18),
        check_vma=False,
    )
```
